32 devices in a mesh: dp: 16 (over z, y, x), tensor: 2 (over core).
Axes of the slice: x: 2, y: 2, z: 4, core: 2. Of those that a mesh axis runs over, the one named last changes fastest.
Arguments:
- tokens: bfloat16 [32, 1024, 768], P('dp'), may hold values from -6 to 6
- condition: bfloat16 [32, 128], P('dp'), may hold values from -6 to 6
- lengths: int32 [32], P('dp'), may hold values from 128 to 1024, as said below
- modulation_weight: bfloat16 [128, 4608], replicated, may hold values from -0.5 to 0.5
- modulation_bias: float32 [4608], replicated, may hold values from -3 to 3
- first_gain: float32 [768], replicated, may hold values from 0.5 to 1.5
- query_key_value_weight: bfloat16 [768, 3, 768], P(None, None, 'tensor'), may hold values from -0.21875 to 0.21875
- attention_out_weight: bfloat16 [768, 768], P('tensor'), may hold values from -1.25 to 1.25
- second_gain: float32 [768], replicated, may hold values from 0.5 to 1.5
- up_projection_weight: bfloat16 [768, 3072], P(None, 'tensor'), may hold values from -0.21875 to 0.21875
- upward_bias: float32 [3072], P('tensor'), may hold values from -2 to 2
- down_projection_weight: bfloat16 [3072, 768], P('tensor'), may hold values from -0.109375 to 0.109375
- downward_bias: float32 [768], replicated, may hold values from -2 to 2
- cotangent: bfloat16 [32, 1024, 768], P('dp', 'tensor'), may hold values from -6 to 6
Outputs:
- output: bfloat16 [32, 1024, 768], P('dp', 'tensor')
- grad_tokens: float32 [32, 1024, 768], P('dp', 'tensor')
- grad_condition: float32 [32, 128], P('dp')
- grad_modulation_weight: float32 [128, 4608], replicated
- grad_modulation_bias: float32 [4608], replicated
- grad_first_gain: float32 [768], replicated
- grad_input_weight: float32 [768, 3, 768], P(None, None, 'tensor')
- grad_output_weight: float32 [768, 768], P('tensor')
- grad_second_gain: float32 [768], replicated
- grad_upward_weight: float32 [768, 3072], P(None, 'tensor')
- grad_upward_bias: float32 [3072], P('tensor')
- grad_downward_weight: float32 [3072, 768], P('tensor')
- grad_downward_bias: float32 [768], replicated
The draws below stay inside these ranges and needn't reach their ends.
Inputs may be any that keep to these rules, and one draw needn't show every extreme that they name: `lengths`: each sequence has 128, 512 or 1024 live slots, the first ones; every draw holds sequences of the shortest and of the full length.
All inputs are finite; a program needn't handle non-finite values.
Results may differ from the reference program's by a relative error of at most 0.012.
The reference program's roundings to bfloat16 on the way count: a program that leaves them out, or rounds other values in their place, can miss the bound.
Values may be sent and summed in bfloat16 or wider, within the bound.
No kernel may reach another device: no remote copies, remote signals or barrier semaphores. Data moves between devices by JAX's collectives and lax.ppermute only.
A program may use at most 192 MiB of HBM per device.

```python
import jax
import jax.numpy as jnp
from jax import lax

D = 768
HEADS = 12
HEAD = 64
FF = 3072
COND = 128
SEQ_LEN = 1024
SEQS = 32


def draw_lengths(key, part):
    key = jax.random.fold_in(key, 7)
    chosen_key, shuffle_key = jax.random.split(key)
    chosen = jax.random.randint(chosen_key, (SEQS,), 0, 3)
    length_table = jnp.array([SEQ_LEN // 8, SEQ_LEN // 2, SEQ_LEN], dtype=jnp.int32)
    matches = chosen[:, None] == jnp.arange(3, dtype=jnp.int32)[None, :]
    chosen_lengths = jnp.sum(jnp.where(matches, length_table[None, :], 0), axis=1).astype(jnp.int32)
    shuffled = jax.random.permutation(shuffle_key, SEQS)
    chosen_lengths = chosen_lengths.at[shuffled[0]].set(SEQ_LEN).at[shuffled[1]].set(SEQ_LEN // 8)
    return chosen_lengths


def steps_of(stream_key, shape, cuts, low, top_value):
    factor_of = 1.0
    for axis_at, parts in cuts:
        heights = jax.random.uniform(jax.random.fold_in(jax.random.fold_in(stream_key, 6), axis_at), (parts,), jnp.float32, low / len(cuts), top_value / len(cuts))
        factor_of = factor_of * jnp.repeat(jnp.exp(heights), shape[axis_at] // parts).reshape((-1,) + (1,) * (len(shape) - 1 - axis_at))
    return factor_of


def normal_values(rng, extent, scale, most, cuts=(), held_as=jnp.bfloat16):
    values = scale * jax.random.normal(rng, extent, jnp.float32)
    if cuts:
        values = values * steps_of(rng, extent, cuts, -0.22, 0.18)
    return jnp.clip(values, -most, most).astype(held_as)


def setup_inputs(seed: int = 0) -> dict:
    streams_of = jax.random.split(jax.random.key(seed), 15)
    return {
        "tokens": normal_values(streams_of[0], (SEQS, SEQ_LEN, D), 1.0, 6.0, ((0, 16),)),
        "condition": normal_values(streams_of[1], (SEQS, COND), 1.0, 6.0, ((0, 16),)),
        "lengths": draw_lengths(jax.random.fold_in(streams_of[14], 71), 0),
        "modulation_weight": normal_values(streams_of[3], (COND, 6 * D), COND ** -0.5, 0.5),
        "modulation_bias": normal_values(streams_of[4], (6 * D,), 0.5, 3.0, (), jnp.float32),
        "first_gain": jnp.clip(1.0 + 0.1 * jax.random.normal(streams_of[5], (D,), jnp.float32), 0.5, 1.5),
        "query_key_value_weight": normal_values(streams_of[6], (D, 3, D), D ** -0.5, 0.21875, ((2, 2),)),
        "attention_out_weight": normal_values(streams_of[7], (D, D), (D // 32) ** -0.5, 1.25, ((0, 2),)),
        "second_gain": jnp.clip(1.0 + 0.1 * jax.random.normal(streams_of[8], (D,), jnp.float32), 0.5, 1.5),
        "up_projection_weight": normal_values(streams_of[9], (D, FF), D ** -0.5, 0.21875, ((1, 2),)),
        "upward_bias": normal_values(streams_of[10], (FF,), 0.3, 2.0, ((0, 2),), jnp.float32),
        "down_projection_weight": normal_values(streams_of[11], (FF, D), FF ** -0.5, 0.109375, ((0, 2),)),
        "downward_bias": normal_values(streams_of[12], (D,), 0.3, 2.0, (), jnp.float32),
        "cotangent": normal_values(streams_of[13], (SEQS, SEQ_LEN, D), 1.0, 6.0, ((0, 16), (1, 2))),
    }


highest = lax.Precision.HIGHEST

@jax.custom_vjp
def low(v):
    return lax.optimization_barrier(v.astype(jnp.bfloat16)).astype(jnp.float32)

@jax.custom_vjp
def low_back(v):
    return v

def low_keep(v):
    return (low(v), None)

def low_pass(kept, grad):
    return (grad,)

def back_keep(v):
    return (v, None)

def back_low(kept, grad):
    return (low(grad),)
low.defvjp(low_keep, low_pass)
low_back.defvjp(back_keep, back_low)

def modulate_rows(rows, gain, shift, scale):
    centre = lax.optimization_barrier(jnp.mean(rows, axis=-1, keepdims=True))
    centred = rows - centre
    spread = lax.optimization_barrier(jnp.mean(centred * centred, axis=-1, keepdims=True))
    normed = centred * lax.rsqrt(spread + 1e-05)
    return normed * gain * (1.0 + scale) + shift

def rotary_tables(full_span, head_size):
    half_size = head_size // 2
    frequency = 10000.0 ** (-(jnp.arange(half_size, dtype=jnp.float32) * 2.0 / head_size))
    angles = jnp.arange(full_span, dtype=jnp.float32)[:, None] * frequency[None, :]
    angles = jnp.concatenate([angles, angles], axis=1)
    return (jnp.cos(angles)[:, None, :], jnp.sin(angles)[:, None, :])

def rotate(values, cosine, sine):
    half_size = values.shape[-1] // 2
    turned = jnp.concatenate([-values[..., half_size:], values[..., :half_size]], axis=-1)
    return values * cosine + turned * sine

def layer(params, rows, cond_row, length):
    modulation_weight, modulation_bias, first_gain, query_key_value_weight, attention_out_weight, second_gain, up_projection_weight, upward_bias, down_projection_weight, downward_bias = params
    silu_cond = low(jax.nn.silu(cond_row))
    mods = low_back(jnp.dot(silu_cond, modulation_weight, precision=highest) + modulation_bias).reshape(6, D)
    leading_rows = low(modulate_rows(rows, first_gain, mods[0], mods[1]))
    joined = low_back(jnp.einsum('ld,dce->lce', leading_rows, query_key_value_weight, precision=highest))
    cosine, sine = rotary_tables(SEQ_LEN, HEAD)
    queries = low(rotate(joined[:, 0].reshape(SEQ_LEN, HEADS, HEAD), cosine, sine))
    keys = low(rotate(joined[:, 1].reshape(SEQ_LEN, HEADS, HEAD), cosine, sine))
    values = low(joined[:, 2].reshape(SEQ_LEN, HEADS, HEAD))
    scores = low_back(jnp.einsum('qhd,khd->hqk', queries, keys, precision=highest) * HEAD ** (-0.5))
    live = jnp.arange(SEQ_LEN) < length
    scores = jnp.where(live[None, None, :], scores, -1e+30)
    probs = low(jax.nn.softmax(scores, axis=-1))
    attention_result = jnp.einsum('hqk,khd->qhd', probs, values, precision=highest).reshape(SEQ_LEN, D)
    attention_result = low(low_back(attention_result))
    branch_one = low_back(jnp.dot(attention_result, attention_out_weight, precision=highest))
    middle = rows + mods[2] * branch_one
    trailing_rows = low(modulate_rows(middle, second_gain, mods[3], mods[4]))
    upper = low_back(jnp.dot(trailing_rows, up_projection_weight, precision=highest) + upward_bias)
    activation_values = low(jax.nn.gelu(upper, approximate=True))
    branch_two = low_back(jnp.dot(activation_values, down_projection_weight, precision=highest) + downward_bias)
    return middle + mods[5] * branch_two

def reference(tokens, condition, lengths, modulation_weight, modulation_bias, first_gain, query_key_value_weight, attention_out_weight, second_gain, up_projection_weight, upward_bias, down_projection_weight, downward_bias, cotangent):
    params = tuple((entry.astype(jnp.float32) for entry in (modulation_weight, modulation_bias, first_gain, query_key_value_weight, attention_out_weight, second_gain, up_projection_weight, upward_bias, down_projection_weight, downward_bias)))

    def one_sequence(totals, element):
        rows, cond_row, length, upstream = element

        def forward(weights, inputs, conditioning):
            return layer(weights, inputs, conditioning, length)
        result, pull = jax.vjp(forward, params, rows.astype(jnp.float32), cond_row.astype(jnp.float32))
        grad_params, grad_rows, grad_cond = pull(upstream.astype(jnp.float32))
        totals = jax.tree.map(jnp.add, totals, grad_params)
        return (totals, (result.astype(jnp.bfloat16), grad_rows, grad_cond))
    zeros = jax.tree.map(jnp.zeros_like, params)
    totals, stacked = lax.scan(one_sequence, zeros, (tokens, condition, lengths, cotangent))
    return (stacked[0], stacked[1], stacked[2], totals[0], totals[1], totals[2], totals[3], totals[4], totals[5], totals[6], totals[7], totals[8], totals[9])
```

```python
import math
from functools import partial

import jax
import jax.numpy as jnp
import numpy as np
from jax import lax
from jax.experimental import pallas as pl
from jax.experimental.pallas import tpu as pltpu
from jax.sharding import PartitionSpec as P

HEAD = 64
HALF = HEAD // 2
EPS = 1e-05
LOG2_SCALE = math.log2(math.e) * HEAD ** (-0.5)
SAFE_BOUND = 70.0
GELU_A = math.sqrt(2.0 / math.pi)
GELU_B = 0.044715
BF = jnp.bfloat16
F32 = jnp.float32

NN = (((1,), (0,)), ((), ()))
NT = (((1,), (1,)), ((), ()))
TN = (((0,), (0,)), ((), ()))
TT = (((0,), (1,)), ((), ()))
dot = partial(lax.dot_general, preferred_element_type=F32)


def call(body, grid, in_specs, out_specs, out_shape, flops, scratch=(), prefetch=0, vmem=56):
    moved = sum(math.prod(s.shape) * s.dtype.itemsize for s in out_shape)
    return pl.pallas_call(
        body,
        grid_spec=pltpu.PrefetchScalarGridSpec(
            num_scalar_prefetch=prefetch,
            grid=grid,
            in_specs=in_specs,
            out_specs=out_specs,
            scratch_shapes=list(scratch),
        ),
        out_shape=out_shape,
        compiler_params=pltpu.CompilerParams(vmem_limit_bytes=vmem * 2**20),
        cost_estimate=pl.CostEstimate(
            flops=int(flops), bytes_accessed=int(2 * moved), transcendentals=0
        ),
    )


def shaped(shape, dtype):
    return jax.ShapeDtypeStruct(shape, dtype)


def rotary_tables(span):
    frequency = (
        np.float32(10000.0) ** (-(np.arange(HALF, dtype=np.float32) * np.float32(2.0 / HEAD)))
    ).astype(np.float32)
    angles = (np.arange(span, dtype=np.float32)[None, :] * frequency[:, None]).astype(np.float32)
    angles = angles.astype(np.float64)
    return np.cos(angles).astype(np.float32), np.sin(angles).astype(np.float32)


def normed_rows(rows):
    centre = jnp.mean(rows, axis=-1, keepdims=True)
    centred = rows - centre
    spread = jnp.mean(centred * centred, axis=-1, keepdims=True)
    inverse = lax.rsqrt(spread + EPS)
    return centred * inverse, inverse


def project(source, weight, vectors, cosine, sine, first):
    span, features = source.shape
    _, _, width = weight.shape

    def body(source_ref, weight_ref, vector_ref, cos_ref, sin_ref, *rest):
        if first:
            rows_ref, out_ref = rest

            @pl.when(pl.program_id(0) == 0)
            def _():
                for start in range(0, span, 128):
                    hat, _ = normed_rows(source_ref[start : start + 128, :].astype(F32))
                    rows_ref[start : start + 128, :] = (
                        hat * vector_ref[0:1, :] + vector_ref[1:2, :]
                    ).astype(BF)
        else:
            (out_ref,) = rest
            rows_ref = source_ref
        joined = dot(weight_ref[0], rows_ref[...], TT)

        @pl.when(pl.program_id(0) < 2)
        def _():
            cos, sin = cos_ref[...], sin_ref[...]
            for at in range(0, width, HEAD):
                low, high = joined[at : at + HALF], joined[at + HALF : at + HEAD]
                out_ref[0, at : at + HALF, :] = (low * cos - high * sin).astype(BF)
                out_ref[0, at + HALF : at + HEAD, :] = (high * cos + low * sin).astype(BF)

        @pl.when(pl.program_id(0) == 2)
        def _():
            out_ref[0] = joined.astype(BF)

    whole = lambda c: (0, 0)
    out_specs = [pl.BlockSpec((1, width, span), lambda c: (c, 0, 0))]
    out_shape = [shaped((3, width, span), BF)]
    if first:
        out_specs = [pl.BlockSpec((span, features), whole)] + out_specs
        out_shape = [shaped((span, features), BF)] + out_shape
    return call(
        body,
        (3,),
        [
            pl.BlockSpec((span, features), whole),
            pl.BlockSpec((1, features, width), lambda c: (c, 0, 0)),
            pl.BlockSpec(vectors.shape, whole),
            pl.BlockSpec(cosine.shape, whole),
            pl.BlockSpec(sine.shape, whole),
        ],
        out_specs,
        out_shape,
        6 * span * features * width,
    )(source, weight, vectors, cosine, sine)


def live_lengths(span):
    return (span, span // 2, span // 8)


def attend(length, joined):
    _, width, span = joined.shape
    per_step = 2
    query_block = min(512, span)

    def one_length(live, query_ref, key_ref, value_ref, out_ref, total_ref):
        key_block = min(512, live)
        for head in range(per_step):
            at = slice(head * HEAD, (head + 1) * HEAD)
            keys = key_ref[0, at, :live].T
            query_size = jnp.sum(jnp.square(query_ref[0, at, :].astype(F32)), axis=0)
            key_size = jnp.sum(jnp.square(key_ref[0, at, :live].astype(F32)), axis=0)
            largest = jnp.max(query_size) * jnp.max(key_size)
            safe = largest < (SAFE_BOUND / HEAD ** (-0.5)) ** 2

            @pl.when(safe)
            def _():
                for first in range(0, span, query_block):
                    columns = slice(first, first + query_block)
                    queries = query_ref[0, at, columns]
                    result = jnp.zeros((HEAD, query_block), F32)
                    total = jnp.zeros((1, query_block), F32)
                    for start in range(0, live, key_block):
                        rows = slice(start, start + key_block)
                        probs = jnp.exp2(dot(keys[rows], queries, NN) * LOG2_SCALE)
                        total = total + jnp.sum(probs, axis=0, keepdims=True)
                        result = result + dot(value_ref[0, at, rows], probs.astype(BF), NN)
                    out_ref[at, columns] = (result * (1.0 / total)).astype(BF)
                    total_ref[0, head : head + 1, columns] = jnp.log2(total)

            @pl.when(jnp.logical_not(safe))
            def _():
                for first in range(0, span, query_block):
                    columns = slice(first, first + query_block)
                    scores = dot(keys, query_ref[0, at, columns], NN) * LOG2_SCALE
                    highest = jnp.max(scores, axis=0, keepdims=True)
                    probs = jnp.exp2(scores - highest)
                    total = jnp.sum(probs, axis=0, keepdims=True)
                    result = dot(value_ref[0, at, :live], probs.astype(BF), NN)
                    out_ref[at, columns] = (result * (1.0 / total)).astype(BF)
                    total_ref[0, head : head + 1, columns] = highest + jnp.log2(total)

    def body(length_ref, query_ref, key_ref, value_ref, out_ref, total_ref):
        for live in live_lengths(span):

            @pl.when(length_ref[0] == live)
            def _():
                one_length(live, query_ref, key_ref, value_ref, out_ref, total_ref)

    rows = per_step * HEAD

    def part(c):
        return pl.BlockSpec((1, rows, span), lambda i, n: (c, i, 0))

    return call(
        body,
        (width // rows,),
        [part(0), part(1), part(2)],
        [
            pl.BlockSpec((rows, span), lambda i, n: (i, 0)),
            pl.BlockSpec((1, per_step, span), lambda i, n: (i, 0, 0)),
        ],
        [shaped((width, span), BF), shaped((width // rows, per_step, span), F32)],
        16 * span * span * width,
        prefetch=1,
    )(length, joined, joined, joined)


def attend_back(length, joined, attended, dattended, totals, cosine, sine):
    _, width, span = joined.shape
    per_step = 2
    key_block_most = 256

    def turned(grads, cos, sin, out_ref, part, head, columns):
        low, high = grads[:HALF], grads[HALF:]
        top = head * HEAD
        out_ref[part, top : top + HALF, columns] = (low * cos + high * sin).astype(BF)
        out_ref[part, top + HALF : top + HEAD, columns] = (high * cos - low * sin).astype(BF)

    def one_length(live, query_ref, key_ref, value_ref, out_ref, dout_ref, total_ref, cos_ref, sin_ref, grad_ref):
        key_block = min(key_block_most, live)
        for head in range(per_step):
            at = slice(head * HEAD, (head + 1) * HEAD)
            keys = key_ref[0, at, :live].T
            values = value_ref[0, at, :live].T
            queries = query_ref[0, at, :]
            dout = dout_ref[at, :]
            weighted = jnp.sum(
                dout.astype(F32) * out_ref[at, :].astype(F32), axis=0, keepdims=True
            )
            totals = total_ref[0, head : head + 1, :]
            dquery = jnp.zeros((HEAD, span), F32)
            for start in range(0, live, key_block):
                rows = slice(start, start + key_block)
                probs = jnp.exp2(dot(keys[rows], queries, NN) * LOG2_SCALE - totals)
                dprobs = dot(values[rows], dout, NN)
                dscores = (probs * (dprobs - weighted)).astype(BF)
                dvalue = dot(dout, probs.astype(BF), NT)
                dkey = dot(queries, dscores, NT) * HEAD ** (-0.5)
                dquery = dquery + dot(key_ref[0, at, rows], dscores, NN)
                turned(dkey, cos_ref[:, rows], sin_ref[:, rows], grad_ref, 1, head, rows)
                grad_ref[2, at, rows] = dvalue.astype(BF)
            turned(dquery * HEAD ** (-0.5), cos_ref[...], sin_ref[...], grad_ref, 0, head, slice(0, span))
        if live < span:
            empty = jnp.zeros((per_step * HEAD, span - live), BF)
            grad_ref[1, :, live:] = empty
            grad_ref[2, :, live:] = empty

    def body(length_ref, *refs):
        for live in live_lengths(span):

            @pl.when(length_ref[0] == live)
            def _():
                one_length(live, *refs)

    rows = per_step * HEAD

    def part(c):
        return pl.BlockSpec((1, rows, span), lambda i, n: (c, i, 0))

    flat = pl.BlockSpec((rows, span), lambda i, n: (i, 0))
    table = pl.BlockSpec((HALF, span), lambda i, n: (0, 0))
    return call(
        body,
        (width // rows,),
        [part(0), part(1), part(2), flat, flat, pl.BlockSpec((1, per_step, span), lambda i, n: (i, 0, 0)), table, table],
        [pl.BlockSpec((3, rows, span), lambda i, n: (0, i, 0))],
        [shaped((3, width, span), BF)],
        40 * span * span * width,
        prefetch=1,
    )(length, joined, joined, joined, attended, dattended, totals, cosine, sine)[0]


def middle_forward(attended, tokens, outs, ups, biases, vectors):
    width, span = attended[0].shape
    features = tokens.shape[1]
    hidden = ups[0].shape[1]
    rows = 256

    def body(att_a, att_b, tok_ref, out_a, out_b, up_a, up_b, bias_a, bias_b, vec_ref, branch_ref, h_ref, act_a, act_b, slope_a, slope_b):
        branch = dot(att_a[...], out_a[...], TN) + dot(att_b[...], out_b[...], TN)
        branch_ref[...] = branch
        middle = tok_ref[...].astype(F32) + vec_ref[0:1, :] * branch
        hat, _ = normed_rows(middle)
        h = (hat * vec_ref[1:2, :] + vec_ref[2:3, :]).astype(BF)
        h_ref[...] = h
        for up, bias, act, slope in ((up_a, bias_a, act_a, slope_a), (up_b, bias_b, act_b, slope_b)):
            for at in range(0, hidden, 256):
                columns = slice(at, at + 256)
                upper = dot(h, up[:, columns], NN) + bias[0:1, columns]
                square = upper * upper
                tanh = jnp.tanh(upper * (GELU_A + (GELU_A * GELU_B) * square))
                half = 0.5 * upper
                act[:, columns] = (half + half * tanh).astype(BF)
                slope[:, columns] = (
                    (0.5 + 0.5 * tanh)
                    + half * (1.0 - tanh * tanh) * (GELU_A + (3.0 * GELU_A * GELU_B) * square)
                ).astype(BF)

    whole = lambda i: (0, 0)
    att = pl.BlockSpec((width, rows), lambda i: (0, i))
    tok = pl.BlockSpec((rows, features), lambda i: (i, 0))
    wide = pl.BlockSpec((rows, hidden), lambda i: (i, 0))
    fixed = lambda a: pl.BlockSpec(a.shape, whole)
    return call(
        body,
        (span // rows,),
        [att, att, tok] + [fixed(a) for a in (*outs, *ups, *biases, vectors)],
        [tok, tok, wide, wide, wide, wide],
        [shaped((span, features), F32), shaped((span, features), BF)] + [shaped((span, hidden), BF)] * 4,
        4 * span * features * (width + hidden),
    )(*attended, tokens, *outs, *ups, *biases, vectors)


def hidden_back(act, slope, down, dbranch, h, out_type):
    span, hidden = act.shape
    features = h.shape[1]
    block = 256
    per = features // block

    def body(act_ref, slope_ref, down_ref, db_ref, h_ref, du_ref, gd_ref, gu_ref, gb_ref):
        gd_ref[...] = dot(act_ref[...], db_ref[...], TN).astype(out_type)
        du = (dot(db_ref[...], down_ref[...], NT) * slope_ref[...].astype(F32)).astype(BF)
        du_ref[...] = du
        gb_ref[...] = jnp.sum(du.astype(F32), axis=0, keepdims=True)
        gu_ref[0] = dot(h_ref[...], du, TN).astype(out_type)

    whole = lambda i: (0, 0)
    column = pl.BlockSpec((span, block), lambda i: (0, i))
    fixed = pl.BlockSpec((span, features), whole)
    return call(
        body,
        (hidden // block,),
        [column, column, pl.BlockSpec((block, features), lambda i: (i, 0)), fixed, fixed],
        [
            column,
            pl.BlockSpec((block, features), lambda i: (i, 0)),
            pl.BlockSpec((1, features, block), lambda i: (i // per, 0, i % per)),
            pl.BlockSpec((1, block), lambda i: (0, i)),
        ],
        [
            shaped((span, hidden), BF),
            shaped((hidden, features), out_type),
            shaped((hidden // features, features, features), out_type),
            shaped((1, hidden), F32),
        ],
        6 * span * features * hidden,
    )(act, slope, down, dbranch, h)


def middle_back(dupper, ups, outs, branch, tokens, upstream, vectors):
    span, hidden = dupper[0].shape
    features = tokens.shape[1]
    width = outs[0].shape[0]
    rows = 256

    def body(du_a, du_b, up_a, up_b, out_a, out_b, branch_ref, tok_ref, g_ref, vec_ref, dmid_ref, db_ref, da_a, da_b, sum_ref):
        dh = dot(du_a[...], up_a[...], NT) + dot(du_b[...], up_b[...], NT)
        branch = branch_ref[...]
        hat, inverse = normed_rows(tok_ref[...].astype(F32) + vec_ref[0:1, :] * branch)
        dhat = dh * hat
        e = dh * vec_ref[1:2, :]
        e_mean = jnp.mean(e, axis=-1, keepdims=True)
        eh_mean = jnp.mean(e * hat, axis=-1, keepdims=True)
        dmid = g_ref[...].astype(F32) + (e - e_mean - hat * eh_mean) * inverse
        dmid_ref[...] = dmid
        db = (vec_ref[0:1, :] * dmid).astype(BF)
        db_ref[...] = db
        da_a[...] = dot(out_a[...], db, NT).astype(BF)
        da_b[...] = dot(out_b[...], db, NT).astype(BF)
        sums = jnp.concatenate(
            [
                jnp.sum(dh, axis=0, keepdims=True),
                jnp.sum(dhat, axis=0, keepdims=True),
                jnp.sum(dmid * branch, axis=0, keepdims=True),
                jnp.zeros((5, features), F32),
            ],
            axis=0,
        )

        @pl.when(pl.program_id(0) == 0)
        def _():
            sum_ref[...] = sums

        @pl.when(pl.program_id(0) > 0)
        def _():
            sum_ref[...] += sums

    whole = lambda i: (0, 0)
    tok = pl.BlockSpec((rows, features), lambda i: (i, 0))
    wide = pl.BlockSpec((rows, hidden), lambda i: (i, 0))
    att = pl.BlockSpec((width, rows), lambda i: (0, i))
    fixed = lambda a: pl.BlockSpec(a.shape, whole)
    return call(
        body,
        (span // rows,),
        [wide, wide] + [fixed(a) for a in (*ups, *outs)] + [tok, tok, tok, fixed(vectors)],
        [tok, tok, att, att, pl.BlockSpec((8, features), whole)],
        [
            shaped((span, features), F32),
            shaped((span, features), BF),
            shaped((width, span), BF),
            shaped((width, span), BF),
            shaped((8, features), F32),
        ],
        4 * span * features * (width + hidden),
    )(*dupper, *ups, *outs, branch, tokens, upstream, vectors)


def finish_forward(acts, downs, branch, tokens, upstream, vectors):
    span, hidden = acts[0].shape
    features = tokens.shape[1]
    rows = 256

    def body(act_a, act_b, down_a, down_b, branch_ref, tok_ref, g_ref, vec_ref, out_ref, sum_ref):
        second = dot(act_a[...], down_a[...], NN) + dot(act_b[...], down_b[...], NN) + vec_ref[2:3, :]
        middle = tok_ref[...].astype(F32) + vec_ref[0:1, :] * branch_ref[...]
        out_ref[...] = (middle + vec_ref[1:2, :] * second).astype(BF)
        sums = jnp.sum(g_ref[...].astype(F32) * second, axis=0, keepdims=True)

        @pl.when(pl.program_id(0) == 0)
        def _():
            sum_ref[...] = sums

        @pl.when(pl.program_id(0) > 0)
        def _():
            sum_ref[...] += sums

    whole = lambda i: (0, 0)
    tok = pl.BlockSpec((rows, features), lambda i: (i, 0))
    wide = pl.BlockSpec((rows, hidden), lambda i: (i, 0))
    fixed = lambda a: pl.BlockSpec(a.shape, whole)
    return call(
        body,
        (span // rows,),
        [wide, wide] + [fixed(a) for a in downs] + [tok, tok, tok, fixed(vectors)],
        [tok, pl.BlockSpec((1, features), whole)],
        [shaped((span, features), BF), shaped((1, features), F32)],
        4 * span * features * hidden,
    )(*acts, *downs, branch, tokens, upstream, vectors)


def project_weight_back(h, djoined, out_type):
    span, features = h.shape
    _, width, _ = djoined.shape

    def body(h_ref, dj_ref, out_ref):
        out_ref[0] = dot(h_ref[...], dj_ref[0], TT).astype(out_type)

    return call(
        body,
        (3,),
        [
            pl.BlockSpec((span, features), lambda c: (0, 0)),
            pl.BlockSpec((1, width, span), lambda c: (c, 0, 0)),
        ],
        [pl.BlockSpec((1, features, width), lambda c: (c, 0, 0))],
        [shaped((3, features, width), out_type)],
        6 * span * features * width,
    )(h, djoined)[0]


def project_back(djoined, weights, tokens, dmiddle, vectors):
    _, width, span = djoined[0].shape
    features = tokens.shape[1]
    rows = 256

    def body(dj_a, dj_b, w_a, w_b, tok_ref, dmid_ref, vec_ref, out_ref, sum_ref):
        dh = jnp.zeros((rows, features), F32)
        for c in range(3):
            dh = dh + dot(dj_a[c], w_a[c], TT) + dot(dj_b[c], w_b[c], TT)
        hat, inverse = normed_rows(tok_ref[...].astype(F32))
        e = dh * vec_ref[0:1, :]
        e_mean = jnp.mean(e, axis=-1, keepdims=True)
        eh_mean = jnp.mean(e * hat, axis=-1, keepdims=True)
        out_ref[...] = dmid_ref[...] + (e - e_mean - hat * eh_mean) * inverse
        sums = jnp.concatenate(
            [
                jnp.sum(dh, axis=0, keepdims=True),
                jnp.sum(dh * hat, axis=0, keepdims=True),
                jnp.zeros((6, features), F32),
            ],
            axis=0,
        )

        @pl.when(pl.program_id(0) == 0)
        def _():
            sum_ref[...] = sums

        @pl.when(pl.program_id(0) > 0)
        def _():
            sum_ref[...] += sums

    whole = lambda i: (0, 0)
    tok = pl.BlockSpec((rows, features), lambda i: (i, 0))
    joined = pl.BlockSpec((3, width, rows), lambda i: (0, 0, i))
    weight = pl.BlockSpec((3, features, width), lambda i: (0, 0, 0))
    return call(
        body,
        (span // rows,),
        [joined, joined, weight, weight, tok, tok, pl.BlockSpec(vectors.shape, whole)],
        [tok, pl.BlockSpec((8, features), whole)],
        [shaped((span, features), F32), shaped((8, features), F32)],
        12 * span * features * width,
    )(*djoined, *weights, tokens, dmiddle, vectors)


def halving_steps(size):
    if size == 16:
        return [
            (1, lambda d: d & 1),
            (2, lambda d: (d >> 1) & 1),
            (4, lambda d: ((d >> 2) ^ (d >> 3)) & 1),
            (12, lambda d: (d >> 3) & 1),
        ]
    steps, mask = [], 1
    while mask < size:
        steps.append((mask, partial(lambda shift, d: (d >> shift) & 1, len(steps))))
        mask *= 2
    return steps


def sum_over_dp(total, dp_size, tensor_size, dp_index, tensor_index, orders):
    if dp_size & (dp_size - 1) or total.shape[0] % dp_size:
        return lax.psum(total, "dp")
    steps = halving_steps(dp_size)
    count = len(steps)
    rounds = []
    for at in range(count):
        chosen = [steps[orders[t % len(orders)][at] if count == 4 else (at + t) % count] for t in range(tensor_size)]
        pairs = [
            (d * tensor_size + t, (d ^ chosen[t][0]) * tensor_size + t)
            for d in range(dp_size)
            for t in range(tensor_size)
        ]
        bit = chosen[0][1](dp_index)
        for t in range(1, tensor_size):
            bit = jnp.where(tensor_index == t, chosen[t][1](dp_index), bit)
        rounds.append((pairs, bit))
    for pairs, bit in rounds:
        half = total.shape[0] // 2
        leaving = lax.dynamic_slice_in_dim(total, (1 - bit) * half, half, 0).astype(BF)
        arrived = lax.ppermute(leaving, ("dp", "tensor"), pairs)
        total = lax.dynamic_slice_in_dim(total, bit * half, half, 0) + arrived.astype(F32)
    total = total.astype(BF)
    for pairs, bit in rounds[::-1]:
        half = total.shape[0]
        arrived = lax.ppermute(total, ("dp", "tensor"), pairs)
        both = jnp.zeros((2 * half,) + total.shape[1:], BF)
        both = lax.dynamic_update_slice_in_dim(both, total, bit * half, 0)
        total = lax.dynamic_update_slice_in_dim(both, arrived, (1 - bit) * half, 0)
    return total.astype(F32)


def per_device(
    dp_size,
    tensor_size,
    tokens,
    condition,
    lengths,
    modulation_weight,
    modulation_bias,
    first_gain,
    query_key_value_weight,
    attention_out_weight,
    second_gain,
    up_projection_weight,
    upward_bias,
    down_projection_weight,
    downward_bias,
    cotangent,
):
    sequences, span, features = tokens.shape
    hidden = up_projection_weight.shape[1]
    width = attention_out_weight.shape[0]
    dp_index = lax.axis_index("dp")
    mine = lax.axis_index("tensor")
    swap = [(0, 1), (1, 0)]

    def from_sibling(value):
        return lax.ppermute(value, "tensor", swap)

    def ordered(own, other, axis):
        return jnp.where(
            mine == 0,
            jnp.concatenate([own, other], axis=axis),
            jnp.concatenate([other, own], axis=axis),
        )

    qkv_own = query_key_value_weight.transpose(1, 0, 2)
    qkv_weights = (qkv_own, from_sibling(qkv_own))
    out_weights = (attention_out_weight, from_sibling(attention_out_weight))
    up_weights = (up_projection_weight, from_sibling(up_projection_weight))
    up_biases = (upward_bias[None], from_sibling(upward_bias)[None])
    down_weights = (down_projection_weight, from_sibling(down_projection_weight))
    gone = lax.dynamic_index_in_dim(cotangent, 1 - mine, 0, keepdims=False)
    kept = lax.dynamic_index_in_dim(cotangent, mine, 0, keepdims=False)
    upstream = ordered(kept, from_sibling(gone), 0)
    rows = lax.dynamic_index_in_dim(tokens, mine, 0, keepdims=False)
    length = lax.dynamic_slice_in_dim(lengths, mine, 1, 0)

    cond_float = condition.astype(F32)
    silu_values, silu_pull = jax.vjp(jax.nn.silu, cond_float)
    silu_cond = silu_values.astype(BF)
    mods = dot(silu_cond, modulation_weight, NN) + modulation_bias
    mods = lax.dynamic_index_in_dim(mods, mine, 0, keepdims=False).reshape(6, features)
    shift_one, scale_one, gate_one, shift_two, scale_two, gate_two = mods
    empty = jnp.zeros((features,), F32)
    gain_one = first_gain * (1.0 + scale_one)
    gain_two = second_gain * (1.0 + scale_two)
    vectors_one = jnp.stack([gain_one, shift_one] + [empty] * 6)
    vectors_two = jnp.stack([gate_one, gain_two, shift_two] + [empty] * 5)
    vectors_three = jnp.stack([gate_one, gate_two, downward_bias] + [empty] * 5)
    cosine, sine = (jnp.asarray(table) for table in rotary_tables(span))

    leading, joined_own = project(rows, qkv_weights[0], vectors_one, cosine, sine, True)
    (joined_other,) = project(leading, qkv_weights[1], vectors_one, cosine, sine, False)
    attended_own, totals_own = attend(length, joined_own)
    attended_other, totals_other = attend(length, joined_other)
    attended = (attended_own, attended_other)
    branch_one, trailing, act_own, act_other, slope_own, slope_other = middle_forward(
        attended, rows, out_weights, up_weights, up_biases, vectors_two
    )
    dbranch = (gate_two * upstream.astype(F32)).astype(BF)
    grad_downward_bias = jnp.sum(dbranch, axis=0, dtype=F32)
    dupper_other, gd_other, gu_other, gb_other = hidden_back(
        act_other, slope_other, down_weights[1], dbranch, trailing, BF
    )
    gd_other = from_sibling(gd_other)
    gu_other = from_sibling(gu_other)
    dupper_own, gd_own, gu_own, gb_own = hidden_back(
        act_own, slope_own, down_weights[0], dbranch, trailing, F32
    )
    grad_upward_bias = ordered(gb_own, gb_other, 1)

    def reduced(total, orders):
        return sum_over_dp(total, dp_size, tensor_size, dp_index, mine, orders)

    grad_downward_weight = reduced(gd_own + gd_other.astype(F32), ((0, 1, 2, 3), (1, 0, 3, 2)))
    grad_upward_weight = reduced(
        (gu_own + gu_other.astype(F32)).reshape(hidden, features), ((2, 3, 0, 1), (3, 2, 1, 0))
    )
    grad_upward_weight = (
        grad_upward_weight.reshape(hidden // features, features, features)
        .transpose(1, 0, 2)
        .reshape(features, hidden)
    )
    dmiddle, dbranch_one, dattended_own, dattended_other, sums_two = middle_back(
        (dupper_own, dupper_other), up_weights, out_weights, branch_one, rows, upstream, vectors_two
    )
    go_other = from_sibling(dot(attended_other, dbranch_one, NN).astype(BF))
    go_own = dot(attended_own, dbranch_one, NN) + go_other.astype(F32)
    grad_output_weight = reduced(go_own, ((0, 1, 2, 3), (1, 0, 3, 2)))

    djoined_other = attend_back(
        length, joined_other, attended_other, dattended_other, totals_other, cosine, sine
    )
    gq_other = from_sibling(project_weight_back(leading, djoined_other, BF))
    djoined_own = attend_back(
        length, joined_own, attended_own, dattended_own, totals_own, cosine, sine
    )
    gq_own = project_weight_back(leading, djoined_own, F32)
    grad_input_weight = reduced(
        (gq_own + gq_other.astype(F32)).reshape(3 * features, width), ((0, 1, 2, 3), (1, 0, 3, 2))
    )
    grad_input_weight = grad_input_weight.reshape(3, features, width).transpose(1, 0, 2)

    output, dgate_two = finish_forward(
        (act_own, act_other), down_weights, branch_one, rows, upstream, vectors_three
    )
    grad_rows, sums_one = project_back(
        (djoined_own, djoined_other), qkv_weights, rows, dmiddle, vectors_one
    )

    def by_halves(value):
        halves = value.reshape(2, span // 2, features)
        kept = lax.dynamic_index_in_dim(halves, mine, 0, keepdims=True)
        gone = lax.dynamic_index_in_dim(halves, 1 - mine, 0, keepdims=True)
        return ordered(kept, from_sibling(gone), 0)

    output = by_halves(output)
    grad_tokens = by_halves(grad_rows)

    small = jnp.concatenate(
        [
            sums_one[0:1],
            sums_one[1:2] * first_gain,
            sums_two[2:3],
            sums_two[0:1],
            sums_two[1:2] * second_gain,
            dgate_two,
            sums_one[1:2] * (1.0 + scale_one),
            sums_two[1:2] * (1.0 + scale_two),
            grad_downward_bias[None],
            grad_upward_bias.reshape(-1, features),
        ],
        axis=0,
    )
    gathered = lax.all_gather(small, ("dp", "tensor"), axis=0)
    everyone = lax.all_gather(silu_cond, "dp", axis=0, tiled=True)
    dmods_low = gathered[:, :6].reshape(-1, 6 * features).astype(BF)
    grad_modulation_bias = jnp.sum(dmods_low, axis=0, dtype=F32)
    grad_modulation_weight = dot(everyone, dmods_low, TN)
    pair = lax.dynamic_slice_in_dim(dmods_low, dp_index * sequences, sequences, 0)
    grad_condition = silu_pull(dot(pair, modulation_weight, NT))[0]
    sums = jnp.sum(gathered[:, 6:], axis=0)
    grad_upward_bias = lax.dynamic_slice_in_dim(sums[3:].reshape(-1), mine * hidden, hidden, 0)
    return (
        output,
        grad_tokens,
        grad_condition,
        grad_modulation_weight,
        grad_modulation_bias,
        sums[0],
        grad_input_weight,
        grad_output_weight,
        sums[1],
        grad_upward_weight,
        grad_upward_bias,
        grad_downward_weight,
        sums[2],
    )


def solution(mesh):
    placed = (
        P("dp", None, None),
        P("dp", None),
        P("dp"),
        P(),
        P(),
        P(),
        P(None, None, "tensor"),
        P("tensor", None),
        P(),
        P(None, "tensor"),
        P("tensor"),
        P("tensor", None),
        P(),
        P("dp", "tensor", None),
    )
    return jax.shard_map(
        partial(per_device, mesh.shape["dp"], mesh.shape["tensor"]),
        mesh=mesh,
        in_specs=placed,
        out_specs=(
            P("dp", "tensor", None),
            P("dp", "tensor", None),
            P("dp", None),
            P(),
            P(),
            P(),
            P(None, None, "tensor"),
            P("tensor", None),
            P(),
            P(None, "tensor"),
            P("tensor"),
            P("tensor", None),
            P(),
        ),
        check_vma=False,
    )
```

```python
import math
from functools import partial

import jax
import jax.numpy as jnp
import numpy as np
from jax import lax
from jax.experimental import pallas as pl
from jax.experimental.pallas import tpu as pltpu
from jax.sharding import PartitionSpec as P

HEAD = 64
HALF = HEAD // 2
EPS = 1e-05
LOG2_SCALE = math.log2(math.e) * HEAD ** (-0.5)
SAFE_BOUND = 70.0
GELU_A = math.sqrt(2.0 / math.pi)
GELU_B = 0.044715
BF = jnp.bfloat16
F32 = jnp.float32

NN = (((1,), (0,)), ((), ()))
NT = (((1,), (1,)), ((), ()))
TN = (((0,), (0,)), ((), ()))
TT = (((0,), (1,)), ((), ()))
dot = partial(lax.dot_general, preferred_element_type=F32)


def call(body, grid, in_specs, out_specs, out_shape, flops, scratch=(), prefetch=0, spare=8, after=()):
    known = prefetch + len(in_specs)

    def with_after(*refs):
        return body(*refs[:known], *refs[known + len(after) :])

    def run(*operands):
        held = 0
        for spec, array in zip(
            list(in_specs) + list(out_specs), list(operands[prefetch:]) + list(out_shape)
        ):
            size = math.prod(spec.block_shape) * array.dtype.itemsize
            held += size if spec.pipeline_mode is not None else 2 * size
        moved = sum(a.size * a.dtype.itemsize for a in operands)
        moved += sum(math.prod(a.shape) * a.dtype.itemsize for a in out_shape)
        return pl.pallas_call(
            with_after if after else body,
            grid_spec=pltpu.PrefetchScalarGridSpec(
                num_scalar_prefetch=prefetch,
                grid=grid,
                in_specs=list(in_specs) + [pl.BlockSpec(memory_space=pl.ANY)] * len(after),
                out_specs=out_specs,
                scratch_shapes=list(scratch),
            ),
            out_shape=out_shape,
            compiler_params=pltpu.CompilerParams(
                vmem_limit_bytes=min(held + spare * 2**20, 60 * 2**20)
            ),
            cost_estimate=pl.CostEstimate(
                flops=int(flops), bytes_accessed=int(moved), transcendentals=0
            ),
        )(*operands, *after)

    return run


def shaped(shape, dtype):
    return jax.ShapeDtypeStruct(shape, dtype)


def rotary_tables(span):
    frequency = (
        np.float32(10000.0) ** (-(np.arange(HALF, dtype=np.float32) * np.float32(2.0 / HEAD)))
    ).astype(np.float32)
    angles = (np.arange(span, dtype=np.float32)[None, :] * frequency[:, None]).astype(np.float32)
    angles = angles.astype(np.float64)
    return np.cos(angles).astype(np.float32), np.sin(angles).astype(np.float32)


def normed_rows(rows):
    centre = jnp.mean(rows, axis=-1, keepdims=True)
    centred = rows - centre
    spread = jnp.mean(centred * centred, axis=-1, keepdims=True)
    inverse = lax.rsqrt(spread + EPS)
    return centred * inverse, inverse


def project(source, weights, vectors, cosine, sine):
    span, features = source.shape
    width = weights[0].shape[2]

    def body(source_ref, own_ref, other_ref, vector_ref, cos_ref, sin_ref, rows_ref, out_ref):
        step = pl.program_id(0)

        @pl.when(step == 0)
        def _():
            for start in range(0, span, 128):
                hat, _ = normed_rows(source_ref[start : start + 128, :].astype(F32))
                rows_ref[start : start + 128, :] = (
                    hat * vector_ref[0:1, :] + vector_ref[1:2, :]
                ).astype(BF)

        def emit(weight_ref):
            joined = dot(weight_ref[0], rows_ref[...], TT)

            @pl.when(step % 3 < 2)
            def _():
                cos, sin = cos_ref[...], sin_ref[...]
                for at in range(0, width, HEAD):
                    low, high = joined[at : at + HALF], joined[at + HALF : at + HEAD]
                    out_ref[0, at : at + HALF, :] = (low * cos - high * sin).astype(BF)
                    out_ref[0, at + HALF : at + HEAD, :] = (high * cos + low * sin).astype(BF)

            @pl.when(step % 3 == 2)
            def _():
                out_ref[0] = joined.astype(BF)

        @pl.when(step < 3)
        def _():
            emit(own_ref)

        @pl.when(step >= 3)
        def _():
            emit(other_ref)

    whole = lambda i: (0, 0)
    return call(
        body,
        (6,),
        [
            pl.BlockSpec((span, features), whole),
            pl.BlockSpec((1, features, width), lambda i: (jnp.minimum(i, 2), 0, 0)),
            pl.BlockSpec((1, features, width), lambda i: (jnp.maximum(i - 3, 0), 0, 0)),
            pl.BlockSpec(vectors.shape, whole),
            pl.BlockSpec(cosine.shape, whole),
            pl.BlockSpec(sine.shape, whole),
        ],
        [
            pl.BlockSpec((span, features), whole),
            pl.BlockSpec((1, width, span), lambda i: (i % 3, i // 3, 0)),
        ],
        [shaped((span, features), BF), shaped((3, 2 * width, span), BF)],
        12 * span * features * width,
    )(source, *weights, vectors, cosine, sine)


def live_lengths(span):
    return (span, span // 2, span // 8)


def attend(length, joined):
    _, width, span = joined.shape
    per_step = 2
    query_block = min(512, span)

    def one_length(live, query_ref, key_ref, value_ref, out_ref, total_ref):
        key_block = min(512, live)
        for head in range(per_step):
            at = slice(head * HEAD, (head + 1) * HEAD)
            keys = key_ref[0, at, :live].T
            query_size = jnp.sum(jnp.square(query_ref[0, at, :].astype(F32)), axis=0)
            key_size = jnp.sum(jnp.square(key_ref[0, at, :live].astype(F32)), axis=0)
            largest = jnp.max(query_size) * jnp.max(key_size)
            safe = largest < (SAFE_BOUND / HEAD ** (-0.5)) ** 2

            @pl.when(safe)
            def _():
                for first in range(0, span, query_block):
                    columns = slice(first, first + query_block)
                    queries = query_ref[0, at, columns]
                    result = jnp.zeros((HEAD, query_block), F32)
                    total = jnp.zeros((1, query_block), F32)
                    for start in range(0, live, key_block):
                        rows = slice(start, start + key_block)
                        probs = jnp.exp2(dot(keys[rows], queries, NN) * LOG2_SCALE)
                        total = total + jnp.sum(probs, axis=0, keepdims=True)
                        result = result + dot(value_ref[0, at, rows], probs.astype(BF), NN)
                    out_ref[at, columns] = (result * (1.0 / total)).astype(BF)
                    total_ref[0, head : head + 1, columns] = jnp.log2(total)

            @pl.when(jnp.logical_not(safe))
            def _():
                for first in range(0, span, query_block):
                    columns = slice(first, first + query_block)
                    scores = dot(keys, query_ref[0, at, columns], NN) * LOG2_SCALE
                    highest = jnp.max(scores, axis=0, keepdims=True)
                    probs = jnp.exp2(scores - highest)
                    total = jnp.sum(probs, axis=0, keepdims=True)
                    result = dot(value_ref[0, at, :live], probs.astype(BF), NN)
                    out_ref[at, columns] = (result * (1.0 / total)).astype(BF)
                    total_ref[0, head : head + 1, columns] = highest + jnp.log2(total)

    def body(length_ref, query_ref, key_ref, value_ref, out_ref, total_ref):
        for live in live_lengths(span):

            @pl.when(length_ref[0] == live)
            def _():
                one_length(live, query_ref, key_ref, value_ref, out_ref, total_ref)

    rows = per_step * HEAD

    def part(c):
        return pl.BlockSpec((1, rows, span), lambda i, n: (c, i, 0))

    return call(
        body,
        (width // rows,),
        [part(0), part(1), part(2)],
        [
            pl.BlockSpec((rows, span), lambda i, n: (i, 0)),
            pl.BlockSpec((1, per_step, span), lambda i, n: (i, 0, 0)),
        ],
        [shaped((width, span), BF), shaped((width // rows, per_step, span), F32)],
        16 * span * span * width,
        prefetch=1,
    )(length, joined, joined, joined)


def attend_back(length, joined, attended, dattended, totals, cosine, sine, piece, after=()):
    _, width, span = joined.shape
    per_step = 2
    key_block_most = 256

    def turned(grads, cos, sin, out_ref, part, head, columns):
        low, high = grads[:HALF], grads[HALF:]
        top = head * HEAD
        out_ref[part, top : top + HALF, columns] = (low * cos + high * sin).astype(BF)
        out_ref[part, top + HALF : top + HEAD, columns] = (high * cos - low * sin).astype(BF)

    def one_length(live, query_ref, key_ref, value_ref, out_ref, dout_ref, total_ref, cos_ref, sin_ref, grad_ref):
        key_block = min(key_block_most, live)
        for head in range(per_step):
            at = slice(head * HEAD, (head + 1) * HEAD)
            keys = key_ref[0, at, :live].T
            values = value_ref[0, at, :live].T
            queries = query_ref[0, at, :]
            dout = dout_ref[at, :]
            weighted = jnp.sum(
                dout.astype(F32) * out_ref[at, :].astype(F32), axis=0, keepdims=True
            )
            totals = total_ref[0, head : head + 1, :]
            dquery = jnp.zeros((HEAD, span), F32)
            for start in range(0, live, key_block):
                rows = slice(start, start + key_block)
                probs = jnp.exp2(dot(keys[rows], queries, NN) * LOG2_SCALE - totals)
                dprobs = dot(values[rows], dout, NN)
                dscores = (probs * (dprobs - weighted)).astype(BF)
                dvalue = dot(dout, probs.astype(BF), NT)
                dkey = dot(queries, dscores, NT) * HEAD ** (-0.5)
                dquery = dquery + dot(key_ref[0, at, rows], dscores, NN)
                turned(dkey, cos_ref[:, rows], sin_ref[:, rows], grad_ref, 1, head, rows)
                grad_ref[2, at, rows] = dvalue.astype(BF)
            turned(dquery * HEAD ** (-0.5), cos_ref[...], sin_ref[...], grad_ref, 0, head, slice(0, span))
        if live < span:
            empty = jnp.zeros((per_step * HEAD, span - live), BF)
            grad_ref[1, :, live:] = empty
            grad_ref[2, :, live:] = empty

    def body(length_ref, *refs):
        for live in live_lengths(span):

            @pl.when(length_ref[0] == live)
            def _():
                one_length(live, *refs)

    rows = per_step * HEAD

    def part(c):
        return pl.BlockSpec((1, rows, span), lambda i, n: (c, piece, 0))

    flat = pl.BlockSpec((rows, span), lambda i, n: (piece, 0))
    table = pl.BlockSpec((HALF, span), lambda i, n: (0, 0))
    return call(
        body,
        (1,),
        [part(0), part(1), part(2), flat, flat, pl.BlockSpec((1, per_step, span), lambda i, n: (piece, 0, 0)), table, table],
        [pl.BlockSpec((3, rows, span), lambda i, n: (0, 0, 0))],
        [shaped((3, rows, span), BF)],
        40 * span * span * rows,
        prefetch=1,
        after=after,
    )(length, joined, joined, joined, attended, dattended, totals, cosine, sine)[0]


def middle(attended, tokens, upstream, outs, ups, downs, biases, vectors):
    features = tokens.shape[1]
    width, span = attended.shape
    part = outs[0].shape[0]
    hidden = ups[0].shape[1]
    rows = 256
    columns_each = 256

    def body(att_ref, tok_ref, g_ref, out_a, out_b, up_a, up_b, down_a, down_b, bias_a, bias_b, vec_ref,
             branch_ref, h_ref, db_two, act_a, act_b, du_a, du_b, dmid_ref, db_one, datt_ref, sum_ref, gb_a, gb_b):
        @pl.when(pl.program_id(0) == 0)
        def _():
            sum_ref[...] = jnp.zeros_like(sum_ref)
            gb_a[...] = jnp.zeros_like(gb_a)
            gb_b[...] = jnp.zeros_like(gb_b)

        branch = dot(att_ref[:part], out_a[...], TN) + dot(att_ref[part:], out_b[...], TN)
        branch_ref[...] = branch
        gate = vec_ref[0:1, :]
        hat, inverse = normed_rows(tok_ref[...].astype(F32) + gate * branch)
        h = (hat * vec_ref[1:2, :] + vec_ref[2:3, :]).astype(BF)
        h_ref[...] = h
        g = g_ref[...].astype(F32)
        db = (vec_ref[3:4, :] * g).astype(BF)
        db_two[...] = db
        for up, down, bias, act, du_ref, gb in (
            (up_a, down_a, bias_a, act_a, du_a, gb_a),
            (up_b, down_b, bias_b, act_b, du_b, gb_b),
        ):
            for at in range(0, hidden, columns_each):
                columns = slice(at, at + columns_each)
                upper = dot(h, up[:, columns], NN) + bias[0:1, columns]
                dact = dot(db, down[columns, :], NT)
                inner = GELU_A + (GELU_A * GELU_B) * (upper * upper)
                tanh = jnp.tanh(upper * inner)
                lean = 0.5 + 0.5 * tanh
                value = upper * lean
                act[:, columns] = value.astype(BF)
                slope = lean + value * (1.0 - tanh) * (3.0 * inner - 2.0 * GELU_A)
                du = (dact * slope).astype(BF)
                du_ref[:, columns] = du
                gb[0:1, columns] += jnp.sum(du.astype(F32), axis=0, keepdims=True)
        dh = dot(du_a[...], up_a[...], NT) + dot(du_b[...], up_b[...], NT)
        e = dh * vec_ref[1:2, :]
        e_mean = jnp.mean(e, axis=-1, keepdims=True)
        eh_mean = jnp.mean(e * hat, axis=-1, keepdims=True)
        dmid = g + (e - e_mean - hat * eh_mean) * inverse
        dmid_ref[...] = dmid
        db = (gate * dmid).astype(BF)
        db_one[...] = db
        datt_ref[:part] = dot(out_a[...], db, NT).astype(BF)
        datt_ref[part:] = dot(out_b[...], db, NT).astype(BF)
        sum_ref[0:1, :] += jnp.sum(dh, axis=0, keepdims=True)
        sum_ref[1:2, :] += jnp.sum(dh * hat, axis=0, keepdims=True)
        sum_ref[2:3, :] += jnp.sum(dmid * branch_ref[...], axis=0, keepdims=True)
        sum_ref[3:4, :] += jnp.sum(db_two[...].astype(F32), axis=0, keepdims=True)

    whole = lambda i: (0, 0)
    tok = pl.BlockSpec((rows, features), lambda i: (i, 0))
    wide = pl.BlockSpec((rows, hidden), lambda i: (i, 0))
    att = pl.BlockSpec((width, rows), lambda i: (0, i))
    fixed = lambda a: pl.BlockSpec(a.shape, whole, pipeline_mode=pl.Buffered(1))
    sums = pl.BlockSpec((1, hidden), whole)
    return call(
        body,
        (span // rows,),
        [att, tok, tok] + [fixed(a) for a in (*outs, *ups, *downs, *biases, vectors)],
        [tok, tok, tok, wide, wide, wide, wide, tok, tok, att, pl.BlockSpec((8, features), whole), sums, sums],
        [
            shaped((span, features), F32),
            shaped((span, features), BF),
            shaped((span, features), BF),
            *[shaped((span, hidden), BF)] * 4,
            shaped((span, features), F32),
            shaped((span, features), BF),
            shaped((width, span), BF),
            shaped((8, features), F32),
            shaped((1, hidden), F32),
            shaped((1, hidden), F32),
        ],
        4 * span * features * width + 12 * span * features * hidden,
    )(attended, tokens, upstream, *outs, *ups, *downs, *biases, vectors)


def weight_grad(left, right, out_type, received=None, bit=None, after=()):
    span, height = left.shape
    features = right.shape[1]
    block = height // 2
    count = height // block
    half = count // 2
    flops = 2 * span * height * features
    fixed = pl.BlockSpec(right.shape, lambda i, *n: (0, 0))
    if bit is None:

        def body(left_ref, right_ref, *rest):
            product = dot(left_ref[...], right_ref[...], TN)
            if received is not None:
                product = product + rest[0][...].astype(F32)
            rest[-1][...] = product.astype(out_type)

        row = pl.BlockSpec((block, features), lambda i: (i, 0))
        more = () if received is None else (received,)
        return call(
            body,
            (count,),
            [pl.BlockSpec((span, block), lambda i: (0, i)), fixed] + [row] * len(more),
            [row],
            [shaped((height, features), out_type)],
            flops,
            after=after,
        )(left, right, *more)[0]

    def body(bit_ref, left_ref, right_ref, received_ref, kept_ref, leaving_ref):
        product = dot(left_ref[...], right_ref[...], TN) + received_ref[...].astype(F32)

        @pl.when(pl.program_id(0) < half)
        def _():
            leaving_ref[...] = product.astype(BF)

        @pl.when(pl.program_id(0) >= half)
        def _():
            kept_ref[...] = product

    def place(i, n):
        return jnp.where(i < half, (1 - n[0]) * half + i, n[0] * half + i - half)

    return call(
        body,
        (count,),
        [
            pl.BlockSpec((span, block), lambda i, n: (0, place(i, n))),
            fixed,
            pl.BlockSpec((block, features), lambda i, n: (place(i, n), 0)),
        ],
        [
            pl.BlockSpec((block, features), lambda i, n: (jnp.maximum(i - half, 0), 0)),
            pl.BlockSpec((block, features), lambda i, n: (jnp.minimum(i, half - 1), 0)),
        ],
        [shaped((height // 2, features), F32), shaped((height // 2, features), BF)],
        flops,
        prefetch=1,
        after=after,
    )(bit, left, right, received)


def out_grad(attended, dbranch, which, out_type, received=None, bit=None, after=()):
    width, span = attended.shape
    features = dbranch.shape[1]
    height, block = width // 2, features // 2
    flops = 2 * span * height * features

    def product_of(att_ref, db_ref, received_ref):
        product = dot(att_ref[...], db_ref[...], NN)
        return product if received is None else product + received_ref[...].astype(F32)

    if bit is None:

        def body(att_ref, db_ref, *rest):
            rest[-1][...] = product_of(att_ref, db_ref, rest[0]).astype(out_type)

        part = pl.BlockSpec((height, block), lambda i: (i, 0))
        more = () if received is None else (received,)
        return call(
            body,
            (2,),
            [
                pl.BlockSpec((height, span), lambda i: (which, 0)),
                pl.BlockSpec((span, block), lambda i: (0, i)),
            ]
            + [part] * len(more),
            [part],
            [shaped((2 * height, block), out_type)],
            flops,
            after=after,
        )(attended, dbranch, *more)[0]

    def body(bit_ref, att_ref, db_ref, received_ref, kept_ref, leaving_ref):
        product = product_of(att_ref, db_ref, received_ref)

        @pl.when(pl.program_id(0) == 0)
        def _():
            leaving_ref[...] = product.astype(BF)

        @pl.when(pl.program_id(0) == 1)
        def _():
            kept_ref[...] = product

    def place(i, n):
        return jnp.where(i == 0, 1 - n[0], n[0])

    half = pl.BlockSpec((height, block), lambda i, n: (0, 0))
    return call(
        body,
        (2,),
        [
            pl.BlockSpec((height, span), lambda i, n: (which, 0)),
            pl.BlockSpec((span, block), lambda i, n: (0, place(i, n))),
            pl.BlockSpec((height, block), lambda i, n: (place(i, n), 0)),
        ],
        [half, half],
        [shaped((height, block), F32), shaped((height, block), BF)],
        flops,
        prefetch=1,
        after=after,
    )(bit, attended, dbranch, received)


def sent_first(blocks):
    half = blocks // 2

    def place(i, n):
        return jnp.where(i < half, (1 - n[0]) * half + i, n[0] * half + i - half)

    def gone(i, n):
        return (jnp.minimum(i, half - 1), 0)

    def kept(i, n):
        return (n[0], jnp.maximum(i - half, 0), 0)

    return place, gone, kept


def finish_forward(mine, acts, downs, branch, tokens, upstream, vectors, after=()):
    span, hidden = acts[0].shape
    features = tokens.shape[1]
    rows = 256
    count = span // rows
    place, gone, kept = sent_first(count)

    def body(mine_ref, act_a, act_b, down_a, down_b, branch_ref, tok_ref, g_ref, vec_ref, gone_ref, kept_ref, sum_ref):
        second = dot(act_a[...], down_a[...], NN) + dot(act_b[...], down_b[...], NN) + vec_ref[2:3, :]
        middle = tok_ref[...].astype(F32) + vec_ref[0:1, :] * branch_ref[...]
        out = (middle + vec_ref[1:2, :] * second).astype(BF)
        sums = jnp.sum(g_ref[...].astype(F32) * second, axis=0, keepdims=True)

        @pl.when(pl.program_id(0) == 0)
        def _():
            sum_ref[...] = sums

        @pl.when(pl.program_id(0) > 0)
        def _():
            sum_ref[...] += sums

        @pl.when(pl.program_id(0) < count // 2)
        def _():
            gone_ref[...] = out

        @pl.when(pl.program_id(0) >= count // 2)
        def _():
            kept_ref[0] = out

    whole = lambda i, n: (0, 0)
    tok = pl.BlockSpec((rows, features), lambda i, n: (place(i, n), 0))
    wide = pl.BlockSpec((rows, hidden), lambda i, n: (place(i, n), 0))
    fixed = lambda a: pl.BlockSpec(a.shape, whole)
    return call(
        body,
        (count,),
        [wide, wide] + [fixed(a) for a in downs] + [tok, tok, tok, fixed(vectors)],
        [
            pl.BlockSpec((rows, features), gone),
            pl.BlockSpec((1, rows, features), kept),
            pl.BlockSpec((1, features), whole),
        ],
        [
            shaped((span // 2, features), BF),
            shaped((2, span // 2, features), BF),
            shaped((1, features), F32),
        ],
        4 * span * features * hidden,
        prefetch=1,
        after=after,
    )(mine, *acts, *downs, branch, tokens, upstream, vectors)


def project_weight_back(h, pieces, out_type, received=None, bit=None, after=()):
    span, features = h.shape
    _, rows, _ = pieces[0].shape
    width = rows * len(pieces)
    block = features // 2
    flops = 6 * span * features * width
    if bit is None:

        def body(h_ref, *refs):
            joined = jnp.concatenate([ref[0] for ref in refs[: len(pieces)]], axis=0)
            product = dot(h_ref[...], joined, TT)
            if received is not None:
                product = product + refs[-2][...].astype(F32)
            refs[-1][...] = product.astype(out_type)

        row = pl.BlockSpec((features, width), lambda c: (c, 0))
        more = () if received is None else (received,)
        return call(
            body,
            (3,),
            [pl.BlockSpec((span, features), lambda c: (0, 0))]
            + [pl.BlockSpec((1, rows, span), lambda c: (c, 0, 0))] * len(pieces)
            + [row] * len(more),
            [row],
            [shaped((3 * features, width), out_type)],
            flops,
            after=after,
        )(h, *pieces, *more)[0]

    def body(bit_ref, h_ref, *refs):
        joined = jnp.concatenate([ref[0] for ref in refs[: len(pieces)]], axis=0)
        received_ref, kept_ref, leaving_ref = refs[len(pieces) :]
        product = dot(h_ref[...], joined, TT) + received_ref[...].astype(F32)

        @pl.when(pl.program_id(0) < 3)
        def _():
            leaving_ref[...] = product.astype(BF)

        @pl.when(pl.program_id(0) >= 3)
        def _():
            kept_ref[...] = product

    def place(i, n):
        return jnp.where(i < 3, (1 - n[0]) * 3 + i, n[0] * 3 + i - 3)

    return call(
        body,
        (6,),
        [pl.BlockSpec((span, block), lambda i, n: (0, place(i, n) % 2))]
        + [pl.BlockSpec((1, rows, span), lambda i, n: (place(i, n) // 2, 0, 0))] * len(pieces)
        + [pl.BlockSpec((block, width), lambda i, n: (place(i, n), 0))],
        [
            pl.BlockSpec((block, width), lambda i, n: (jnp.maximum(i - 3, 0), 0)),
            pl.BlockSpec((block, width), lambda i, n: (jnp.minimum(i, 2), 0)),
        ],
        [shaped((3 * block, width), F32), shaped((3 * block, width), BF)],
        flops,
        prefetch=1,
        after=after,
    )(bit, h, *pieces, received)


def project_back(mine, pieces, weights, tokens, dmiddle, vectors, after=()):
    _, part, span = pieces[0].shape
    features = tokens.shape[1]
    width = weights[0].shape[2]
    rows = 256
    count = span // rows
    each = len(pieces) // 2
    place, gone, kept = sent_first(count)

    def body(mine_ref, *refs):
        pieces, rest = refs[: 2 * each], refs[2 * each :]
        w_a, w_b, tok_ref, dmid_ref, vec_ref, gone_ref, kept_ref, sum_ref = rest
        dh = jnp.zeros((rows, features), F32)
        for c in range(3):
            for weight, held in ((w_a, pieces[:each]), (w_b, pieces[each:])):
                joined = jnp.concatenate([ref[c] for ref in held], axis=0)
                dh = dh + dot(joined, weight[c], TT)
        hat, inverse = normed_rows(tok_ref[...].astype(F32))
        e = dh * vec_ref[0:1, :]
        e_mean = jnp.mean(e, axis=-1, keepdims=True)
        eh_mean = jnp.mean(e * hat, axis=-1, keepdims=True)
        out = dmid_ref[...] + (e - e_mean - hat * eh_mean) * inverse
        sums = jnp.concatenate(
            [
                jnp.sum(dh, axis=0, keepdims=True),
                jnp.sum(dh * hat, axis=0, keepdims=True),
                jnp.zeros((6, features), F32),
            ],
            axis=0,
        )

        @pl.when(pl.program_id(0) == 0)
        def _():
            sum_ref[...] = sums

        @pl.when(pl.program_id(0) > 0)
        def _():
            sum_ref[...] += sums

        @pl.when(pl.program_id(0) < count // 2)
        def _():
            gone_ref[...] = out

        @pl.when(pl.program_id(0) >= count // 2)
        def _():
            kept_ref[0] = out

    whole = lambda i, n: (0, 0)
    tok = pl.BlockSpec((rows, features), lambda i, n: (place(i, n), 0))
    joined = pl.BlockSpec((3, part, rows), lambda i, n: (0, 0, place(i, n)))
    weight = pl.BlockSpec((3, features, width), lambda i, n: (0, 0, 0))
    return call(
        body,
        (count,),
        [joined] * len(pieces) + [weight, weight, tok, tok, pl.BlockSpec(vectors.shape, whole)],
        [
            pl.BlockSpec((rows, features), gone),
            pl.BlockSpec((1, rows, features), kept),
            pl.BlockSpec((8, features), whole),
        ],
        [
            shaped((span // 2, features), F32),
            shaped((2, span // 2, features), F32),
            shaped((8, features), F32),
        ],
        12 * span * features * width,
        prefetch=1,
        after=after,
    )(mine, *pieces, *weights, tokens, dmiddle, vectors)


def halving_steps(size):
    if size == 16:
        return [
            (1, lambda d: d & 1),
            (2, lambda d: (d >> 1) & 1),
            (4, lambda d: ((d >> 2) ^ (d >> 3)) & 1),
            (12, lambda d: (d >> 3) & 1),
        ]
    steps, mask = [], 1
    while mask < size:
        steps.append((mask, partial(lambda shift, d: (d >> shift) & 1, len(steps))))
        mask *= 2
    return steps


def fold(kept, arrived, bit, after=()):
    count = len(kept)

    def body(bit_ref, *refs):
        for at in range(count):
            kept_ref, arrived_ref, stay_ref, leave_ref = refs[at::count]
            total = kept_ref[...] + arrived_ref[...].astype(F32)

            @pl.when(pl.program_id(0) == 0)
            def _():
                leave_ref[...] = total.astype(BF)

            @pl.when(pl.program_id(0) == 1)
            def _():
                stay_ref[...] = total

    def place(at, i, n):
        return (jnp.where(i == 0, 1 - n[at], n[at]), 0)

    halves = [(a.shape[0] // 2, a.shape[1]) for a in kept]
    blocks = [pl.BlockSpec(half, partial(place, at)) for at, half in enumerate(halves)]
    fixed = [pl.BlockSpec(half, lambda i, n: (0, 0)) for half in halves]
    out = call(
        body,
        (2,),
        blocks * 2,
        fixed * 2,
        [shaped(half, F32) for half in halves] + [shaped(half, BF) for half in halves],
        sum(a.size for a in kept),
        prefetch=1,
        after=after,
    )(bit, *kept, *arrived)
    return out[:count], out[count:]


def fold_last(kept, arrived, after=()):
    count = len(kept)

    def body(*refs):
        for at in range(count):
            kept_ref, arrived_ref, out_ref = refs[at::count]
            out_ref[...] = (kept_ref[...].astype(F32) + arrived_ref[...].astype(F32)).astype(BF)

    whole = [pl.BlockSpec(a.shape, lambda i: (0, 0)) for a in kept]
    return call(
        body,
        (1,),
        whole * 2,
        whole,
        [shaped(a.shape, BF) for a in kept],
        sum(a.size for a in kept),
        after=after,
    )(*kept, *arrived)


def join(held, arrived, bit, out_type=BF, ways=(), after=()):
    count = len(held)
    ways = ways or ("above",) * count

    def body(bit_ref, *refs):
        for at in range(count):
            own = pl.program_id(0) == bit_ref[at]
            held_ref, arrived_ref, out_ref = refs[at::count]

            def lay(ref, at=at, out_ref=out_ref):
                value = ref[...].astype(out_type)
                out_ref[...] = value.T if ways[at] == "turned" else value

            pl.when(own)(partial(lay, held_ref))
            pl.when(jnp.logical_not(own))(partial(lay, arrived_ref))

    fixed = [pl.BlockSpec(a.shape, lambda i, n: (0, 0)) for a in held]
    blocks, shapes = [], []
    for a, way in zip(held, ways):
        rows, width = a.shape[::-1] if way == "turned" else a.shape
        if way == "above":
            blocks.append(pl.BlockSpec((rows, width), lambda i, n: (i, 0)))
            shapes.append(shaped((2 * rows, width), out_type))
        else:
            blocks.append(pl.BlockSpec((rows, width), lambda i, n: (0, i)))
            shapes.append(shaped((rows, 2 * width), out_type))
    return call(
        body,
        (2,),
        fixed * 2,
        blocks,
        shapes,
        sum(a.size for a in held),
        prefetch=1,
        after=after,
    )(bit, *held, *arrived)


HALVED = 2


class Halving:
    def __init__(self, dp_size, tensor_size, dp_index, tensor_index, orders):
        steps = halving_steps(dp_size)
        self.count = len(steps)
        self.pairs, bits = [], []
        for at in range(self.count):
            self.pairs.append([])
            bits.append([])
            for order in orders:
                chosen = [steps[order[t][at]] for t in range(tensor_size)]
                self.pairs[at].append(
                    [
                        (d * tensor_size + t, (d ^ chosen[t][0]) * tensor_size + t)
                        for d in range(dp_size)
                        for t in range(tensor_size)
                    ]
                )
                bit = chosen[0][1](dp_index)
                for t in range(1, tensor_size):
                    bit = jnp.where(tensor_index == t, chosen[t][1](dp_index), bit)
                bits[at].append(bit.astype(jnp.int32).reshape(1))
        self.single = bits
        self.bits = [jnp.concatenate(row) if len(row) > 1 else row[0] for row in bits]
        table = None
        for t, order in enumerate(orders[0]):
            places = np.zeros((dp_size, dp_size), np.float32)
            for d in range(dp_size):
                at = 0
                for step in order[:HALVED] + order[HALVED:][::-1]:
                    at = 2 * at + steps[step][1](d)
                places[d, at] = 1.0
            table = places if t == 0 else jnp.where(tensor_index == t, places, table)
        self.table = table
        self.at = 0
        self.payload = None

    def begin(self, *parts):
        self.kept, self.leaving = zip(*parts)
        return tuple(self.leaving)

    def exchange(self, place):
        if self.payload is not None:
            arrived = lax.ppermute(self.payload, ("dp", "tensor"), self.pairs[place][0])
            self.payload = jnp.where(
                self.single[place][0][0] == 0,
                jnp.concatenate([self.payload, arrived], axis=0),
                jnp.concatenate([arrived, self.payload], axis=0),
            )
        return [
            lax.ppermute(part, ("dp", "tensor"), pairs)
            for part, pairs in zip(self.leaving, self.pairs[place])
        ]

    def move(self, after=()):
        if self.at < HALVED:
            arrived = self.exchange(self.at)
            self.at += 1
            if self.at < HALVED:
                self.kept, self.leaving = fold(self.kept, arrived, self.bits[self.at], after)
            else:
                self.leaving = fold_last(self.kept, arrived, after)
        elif self.at < self.count:
            arrived = self.exchange(self.at)
            self.at += 1
            self.leaving = fold_last(self.leaving, arrived, after)
        else:
            place = self.count + HALVED - 1 - self.at
            arrived = self.exchange(place)
            self.at += 1
            self.leaving = join(self.leaving, arrived, self.bits[place], after=after)
        return tuple(self.leaving)

    def finish(self, ways=(), after=()):
        while self.at < self.count + HALVED - 1:
            self.move()
        return join(self.leaving, self.exchange(0), self.bits[0], F32, ways, after)

    def spread(self, value):
        self.payload = value[None]

    def spreaded(self):
        flat = self.payload.reshape(self.payload.shape[0], -1)
        return dot(jnp.asarray(self.table).astype(BF), flat, NN).astype(BF)


def per_device(
    dp_size,
    tensor_size,
    tokens,
    condition,
    lengths,
    modulation_weight,
    modulation_bias,
    first_gain,
    query_key_value_weight,
    attention_out_weight,
    second_gain,
    up_projection_weight,
    upward_bias,
    down_projection_weight,
    downward_bias,
    cotangent,
):
    sequences, span, features = tokens.shape
    hidden = up_projection_weight.shape[1]
    width = attention_out_weight.shape[0]
    dp_index = lax.axis_index("dp")
    mine = lax.axis_index("tensor")
    swap = [(0, 1), (1, 0)]

    def from_sibling(value):
        return lax.ppermute(value, "tensor", swap)

    def ordered(own, other, axis):
        return jnp.where(
            mine == 0,
            jnp.concatenate([own, other], axis=axis),
            jnp.concatenate([other, own], axis=axis),
        )

    qkv_own = query_key_value_weight.transpose(1, 0, 2)
    qkv_weights = (qkv_own, from_sibling(qkv_own))
    out_weights = (attention_out_weight, from_sibling(attention_out_weight))
    up_weights = (up_projection_weight, from_sibling(up_projection_weight))
    up_biases = (upward_bias[None], from_sibling(upward_bias)[None])
    down_weights = (down_projection_weight, from_sibling(down_projection_weight))
    gone = lax.dynamic_index_in_dim(cotangent, 1 - mine, 0, keepdims=False)
    kept = lax.dynamic_index_in_dim(cotangent, mine, 0, keepdims=False)
    upstream = ordered(kept, from_sibling(gone), 0)
    rows = lax.dynamic_index_in_dim(tokens, mine, 0, keepdims=False)
    length = lax.dynamic_slice_in_dim(lengths, mine, 1, 0)

    cond_float = condition.astype(F32)
    silu_values, silu_pull = jax.vjp(jax.nn.silu, cond_float)
    silu_cond = silu_values.astype(BF)
    mods = dot(silu_cond, modulation_weight, NN) + modulation_bias
    mods = lax.dynamic_index_in_dim(mods, mine, 0, keepdims=False).reshape(6, features)
    shift_one, scale_one, gate_one, shift_two, scale_two, gate_two = mods
    empty = jnp.zeros((features,), F32)
    gain_one = first_gain * (1.0 + scale_one)
    gain_two = second_gain * (1.0 + scale_two)
    vectors_one = jnp.stack([gain_one, shift_one] + [empty] * 6)
    vectors_two = jnp.stack([gate_one, gain_two, shift_two, gate_two] + [empty] * 4)
    vectors_three = jnp.stack([gate_one, gate_two, downward_bias] + [empty] * 5)
    cosine, sine = (jnp.asarray(table) for table in rotary_tables(span))

    leading, joined = project(rows, qkv_weights, vectors_one, cosine, sine)
    attended, totals = attend(length, joined)
    (
        branch_one, trailing, dbranch, act_own, act_other, dupper_own, dupper_other,
        dmiddle, dbranch_one, dattended, sums_two, gb_own, gb_other,
    ) = middle(
        attended, rows, upstream, out_weights, up_weights, down_weights, up_biases, vectors_two
    )
    halving = dp_size == 16
    gd_other = from_sibling(weight_grad(act_other, dbranch, BF))
    gu_other = from_sibling(weight_grad(dupper_other, trailing, BF))
    go_other = from_sibling(out_grad(attended, dbranch_one, 1, BF))
    if halving:
        first, second = ((0, 1, 2, 3), (1, 0, 3, 2)), ((2, 3, 0, 1), (3, 2, 1, 0))
        sum_early = Halving(dp_size, tensor_size, dp_index, mine, (second, first, first))
        sum_input = Halving(dp_size, tensor_size, dp_index, mine, (first,))
        bits = sum_early.single[0]
        sent = sum_early.begin(
            weight_grad(act_own, dbranch, F32, gd_other, bits[0]),
            weight_grad(dupper_own, trailing, F32, gu_other, bits[1]),
            out_grad(attended, dbranch_one, 0, F32, go_other, bits[2]),
        )
    else:
        grad_downward_weight = lax.psum(weight_grad(act_own, dbranch, F32, gd_other), "dp")
        grad_upward_weight = lax.psum(weight_grad(dupper_own, trailing, F32, gu_other), "dp").T
        both = lax.psum(out_grad(attended, dbranch_one, 0, F32, go_other), "dp")
        grad_output_weight = jnp.concatenate([both[:width], both[width:]], axis=1)
        sum_early, sum_input, sent = None, None, ()

    def advance(job, *after):
        return job.move(after) if halving else ()

    def back(piece, sent):
        return attend_back(
            length, joined, attended, dattended, totals, cosine, sine, piece, after=sent
        )

    count = width // (2 * HEAD)
    backs = [None] * (2 * count)
    for piece in range(count, 2 * count):
        backs[piece] = back(piece, sent)
        if piece > count:
            sent = advance(sum_early, backs[piece])
    product = project_weight_back(leading, backs[count:], BF, after=sent)
    gq_other = from_sibling(product)
    sent = advance(sum_early, product)
    for piece in range(count):
        backs[piece] = back(piece, sent)
        if piece < count - 1:
            sent = advance(sum_early, backs[piece])
    if halving:
        parts = project_weight_back(
            leading, backs[:count], F32, gq_other, sum_input.bits[0], after=sent
        )
        sent = sum_input.begin(parts)
    else:
        grad_input_weight = lax.psum(project_weight_back(leading, backs[:count], F32, gq_other), "dp")
    which = mine.astype(jnp.int32).reshape(1)
    gone, grad_tokens, sums_one = project_back(
        which, backs, qkv_weights, rows, dmiddle, vectors_one, after=sent
    )
    sent = advance(sum_input, gone)
    grad_tokens = lax.dynamic_update_index_in_dim(grad_tokens, from_sibling(gone), 1 - mine, 0)
    gone, output, dgate_two = finish_forward(
        which, (act_own, act_other), down_weights, branch_one, rows, upstream, vectors_three, after=sent
    )
    sent = advance(sum_input, gone)
    output = lax.dynamic_update_index_in_dim(output, from_sibling(gone), 1 - mine, 0)

    dmods_low = jnp.concatenate(
        [
            sums_one[0],
            sums_one[1] * first_gain,
            sums_two[2],
            sums_two[0],
            sums_two[1] * second_gain,
            dgate_two[0],
        ]
    ).astype(BF)
    wide = 6 * features
    other_bias = from_sibling(gb_other[0])
    sums = jnp.concatenate(
        [
            sums_one[1] * (1.0 + scale_one),
            sums_two[1] * (1.0 + scale_two),
            sums_two[3],
        ]
    )
    held = jnp.concatenate(
        [
            sums,
            dmods_low.astype(F32),
            lax.dynamic_index_in_dim(silu_cond, mine, 0, keepdims=False).astype(F32),
        ]
    )
    held = ordered(held[None], from_sibling(held)[None], 0)
    sums = (held[0, : 3 * features] + held[1, : 3 * features])[None]
    sums = jnp.concatenate([sums, (gb_own + other_bias[None])], axis=1)
    dmods_low = held[:, 3 * features : 3 * features + wide].astype(BF)
    silu_pair = held[:, 3 * features + wide :].astype(BF)
    grad_condition = silu_pull(dot(dmods_low, modulation_weight, NT))[0]
    if halving:
        high = sums.astype(BF)
        low = (sums - high.astype(F32)).astype(BF)
        payload = jnp.concatenate(
            [dmods_low.reshape(-1), silu_pair.reshape(-1), high.reshape(-1), low.reshape(-1)]
        )
        sum_input.spread(payload.reshape(-1, 128))
        (grad_input_weight,) = sum_input.finish()
        gathered = sum_input.spreaded()
        grad_downward_weight, grad_upward_weight, grad_output_weight = sum_early.finish(
            ("above", "turned", "beside")
        )
        split = sequences * wide
        silu_split = split + silu_pair.size
        sums_split = silu_split + sums.size
        dmods_low = gathered[:, :split].reshape(-1, wide)
        everyone = gathered[:, split:silu_split].reshape(-1, silu_pair.shape[1])
        sums = jnp.sum(
            gathered[:, silu_split:sums_split].astype(F32) + gathered[:, sums_split:].astype(F32),
            axis=0,
        )
    else:
        dmods_low = lax.all_gather(dmods_low, "dp", axis=0, tiled=True)
        everyone = lax.all_gather(silu_pair, "dp", axis=0, tiled=True)
        sums = lax.psum(sums, "dp")[0]
    grad_input_weight = grad_input_weight.reshape(3, features, width).transpose(1, 0, 2)
    grad_modulation_bias = jnp.sum(dmods_low, axis=0, dtype=F32)
    grad_modulation_weight = dot(everyone, dmods_low, TN)
    grad_first_gain = sums[:features]
    grad_second_gain = sums[features : 2 * features]
    grad_downward_bias = sums[2 * features : 3 * features]
    grad_upward_bias = sums[3 * features :]
    return (
        output,
        grad_tokens,
        grad_condition,
        grad_modulation_weight,
        grad_modulation_bias,
        grad_first_gain,
        grad_input_weight,
        grad_output_weight,
        grad_second_gain,
        grad_upward_weight,
        grad_upward_bias,
        grad_downward_weight,
        grad_downward_bias,
    )


def solution(mesh):
    placed = (
        P("dp", None, None),
        P("dp", None),
        P("dp"),
        P(),
        P(),
        P(),
        P(None, None, "tensor"),
        P("tensor", None),
        P(),
        P(None, "tensor"),
        P("tensor"),
        P("tensor", None),
        P(),
        P("dp", "tensor", None),
    )
    return jax.shard_map(
        partial(per_device, mesh.shape["dp"], mesh.shape["tensor"]),
        mesh=mesh,
        in_specs=placed,
        out_specs=(
            P("dp", "tensor", None),
            P("dp", "tensor", None),
            P("dp", None),
            P(),
            P(),
            P(),
            P(None, None, "tensor"),
            P("tensor", None),
            P(),
            P(None, "tensor"),
            P("tensor"),
            P("tensor", None),
            P(),
        ),
        check_vma=False,
    )
```

```python
import math
from functools import partial

import jax
import jax.numpy as jnp
import numpy as np
from jax import lax
from jax.experimental import pallas as pl
from jax.experimental.pallas import tpu as pltpu
from jax.sharding import PartitionSpec as P

HEAD = 64
HALF = HEAD // 2
EPS = 1e-05
LOG2_SCALE = math.log2(math.e) * HEAD ** (-0.5)
SAFE_BOUND = 70.0
GELU_A = math.sqrt(2.0 / math.pi)
GELU_B = 0.044715
BF = jnp.bfloat16
F32 = jnp.float32

NN = (((1,), (0,)), ((), ()))
NT = (((1,), (1,)), ((), ()))
TN = (((0,), (0,)), ((), ()))
TT = (((0,), (1,)), ((), ()))
dot = partial(lax.dot_general, preferred_element_type=F32)


def call(body, grid, in_specs, out_specs, out_shape, flops, scratch=(), prefetch=0, spare=8, after=()):
    known = prefetch + len(in_specs)

    def with_after(*refs):
        return body(*refs[:known], *refs[known + len(after) :])

    def run(*operands):
        held = 0
        for spec, array in zip(
            list(in_specs) + list(out_specs), list(operands[prefetch:]) + list(out_shape)
        ):
            size = math.prod(spec.block_shape) * array.dtype.itemsize
            held += size if spec.pipeline_mode is not None else 2 * size
        moved = sum(a.size * a.dtype.itemsize for a in operands)
        moved += sum(math.prod(a.shape) * a.dtype.itemsize for a in out_shape)
        return pl.pallas_call(
            with_after if after else body,
            grid_spec=pltpu.PrefetchScalarGridSpec(
                num_scalar_prefetch=prefetch,
                grid=grid,
                in_specs=list(in_specs) + [pl.BlockSpec(memory_space=pl.ANY)] * len(after),
                out_specs=out_specs,
                scratch_shapes=list(scratch),
            ),
            out_shape=out_shape,
            compiler_params=pltpu.CompilerParams(
                vmem_limit_bytes=min(held + spare * 2**20, 60 * 2**20)
            ),
            cost_estimate=pl.CostEstimate(
                flops=int(flops), bytes_accessed=int(moved), transcendentals=0
            ),
        )(*operands, *after)

    return run


def shaped(shape, dtype):
    return jax.ShapeDtypeStruct(shape, dtype)


def rotary_tables(span):
    frequency = (
        np.float32(10000.0) ** (-(np.arange(HALF, dtype=np.float32) * np.float32(2.0 / HEAD)))
    ).astype(np.float32)
    angles = (np.arange(span, dtype=np.float32)[None, :] * frequency[:, None]).astype(np.float32)
    angles = angles.astype(np.float64)
    return np.cos(angles).astype(np.float32), np.sin(angles).astype(np.float32)


def normed_rows(rows):
    centre = jnp.mean(rows, axis=-1, keepdims=True)
    centred = rows - centre
    spread = jnp.mean(centred * centred, axis=-1, keepdims=True)
    inverse = lax.rsqrt(spread + EPS)
    return centred * inverse, inverse


def project(source, weights, vectors, cosine, sine):
    span, features = source.shape
    width = weights[0].shape[2]

    def body(source_ref, own_ref, other_ref, vector_ref, cos_ref, sin_ref, rows_ref, out_ref):
        step = pl.program_id(0)

        @pl.when(step == 0)
        def _():
            for start in range(0, span, 128):
                hat, _ = normed_rows(source_ref[start : start + 128, :].astype(F32))
                rows_ref[start : start + 128, :] = (
                    hat * vector_ref[0:1, :] + vector_ref[1:2, :]
                ).astype(BF)

        def emit(weight_ref):
            joined = dot(weight_ref[0], rows_ref[...], TT)

            @pl.when(step % 3 < 2)
            def _():
                cos, sin = cos_ref[...], sin_ref[...]
                for at in range(0, width, HEAD):
                    low, high = joined[at : at + HALF], joined[at + HALF : at + HEAD]
                    out_ref[0, at : at + HALF, :] = (low * cos - high * sin).astype(BF)
                    out_ref[0, at + HALF : at + HEAD, :] = (high * cos + low * sin).astype(BF)

            @pl.when(step % 3 == 2)
            def _():
                out_ref[0] = joined.astype(BF)

        @pl.when(step < 3)
        def _():
            emit(own_ref)

        @pl.when(step >= 3)
        def _():
            emit(other_ref)

    whole = lambda i: (0, 0)
    return call(
        body,
        (6,),
        [
            pl.BlockSpec((span, features), whole),
            pl.BlockSpec((1, features, width), lambda i: (jnp.minimum(i, 2), 0, 0)),
            pl.BlockSpec((1, features, width), lambda i: (jnp.maximum(i - 3, 0), 0, 0)),
            pl.BlockSpec(vectors.shape, whole),
            pl.BlockSpec(cosine.shape, whole),
            pl.BlockSpec(sine.shape, whole),
        ],
        [
            pl.BlockSpec((span, features), whole),
            pl.BlockSpec((1, width, span), lambda i: (i % 3, i // 3, 0)),
        ],
        [shaped((span, features), BF), shaped((3, 2 * width, span), BF)],
        12 * span * features * width,
    )(source, *weights, vectors, cosine, sine)


def live_lengths(span):
    return (span, span // 2, span // 8)


def attend(length, joined):
    _, width, span = joined.shape
    per_step = 2
    query_block = min(512, span)

    def one_length(live, query_ref, key_ref, value_ref, out_ref, total_ref):
        key_block = min(512, live)
        for head in range(per_step):
            at = slice(head * HEAD, (head + 1) * HEAD)
            keys = key_ref[0, at, :live].T
            query_size = jnp.sum(jnp.square(query_ref[0, at, :].astype(F32)), axis=0)
            key_size = jnp.sum(jnp.square(key_ref[0, at, :live].astype(F32)), axis=0)
            largest = jnp.max(query_size) * jnp.max(key_size)
            safe = largest < (SAFE_BOUND / HEAD ** (-0.5)) ** 2

            @pl.when(safe)
            def _():
                for first in range(0, span, query_block):
                    columns = slice(first, first + query_block)
                    queries = query_ref[0, at, columns]
                    result = jnp.zeros((HEAD, query_block), F32)
                    total = jnp.zeros((1, query_block), F32)
                    for start in range(0, live, key_block):
                        rows = slice(start, start + key_block)
                        probs = jnp.exp2(dot(keys[rows], queries, NN) * LOG2_SCALE)
                        total = total + jnp.sum(probs, axis=0, keepdims=True)
                        result = result + dot(value_ref[0, at, rows], probs.astype(BF), NN)
                    out_ref[at, columns] = (result * (1.0 / total)).astype(BF)
                    total_ref[0, head : head + 1, columns] = jnp.log2(total)

            @pl.when(jnp.logical_not(safe))
            def _():
                for first in range(0, span, query_block):
                    columns = slice(first, first + query_block)
                    scores = dot(keys, query_ref[0, at, columns], NN) * LOG2_SCALE
                    highest = jnp.max(scores, axis=0, keepdims=True)
                    probs = jnp.exp2(scores - highest)
                    total = jnp.sum(probs, axis=0, keepdims=True)
                    result = dot(value_ref[0, at, :live], probs.astype(BF), NN)
                    out_ref[at, columns] = (result * (1.0 / total)).astype(BF)
                    total_ref[0, head : head + 1, columns] = highest + jnp.log2(total)

    def body(length_ref, query_ref, key_ref, value_ref, out_ref, total_ref):
        for live in live_lengths(span):

            @pl.when(length_ref[0] == live)
            def _():
                one_length(live, query_ref, key_ref, value_ref, out_ref, total_ref)

    rows = per_step * HEAD

    def part(c):
        return pl.BlockSpec((1, rows, span), lambda i, n: (c, i, 0))

    return call(
        body,
        (width // rows,),
        [part(0), part(1), part(2)],
        [
            pl.BlockSpec((rows, span), lambda i, n: (i, 0)),
            pl.BlockSpec((1, per_step, span), lambda i, n: (i, 0, 0)),
        ],
        [shaped((width, span), BF), shaped((width // rows, per_step, span), F32)],
        16 * span * span * width,
        prefetch=1,
    )(length, joined, joined, joined)


def attend_back(length, joined, attended, dattended, totals, cosine, sine, piece, after=()):
    _, width, span = joined.shape
    per_step = 2
    key_block_most = 256

    def turned(grads, cos, sin, out_ref, part, head, columns):
        low, high = grads[:HALF], grads[HALF:]
        top = head * HEAD
        out_ref[part, top : top + HALF, columns] = (low * cos + high * sin).astype(BF)
        out_ref[part, top + HALF : top + HEAD, columns] = (high * cos - low * sin).astype(BF)

    def one_length(live, query_ref, key_ref, value_ref, out_ref, dout_ref, total_ref, cos_ref, sin_ref, grad_ref):
        key_block = min(key_block_most, live)
        for head in range(per_step):
            at = slice(head * HEAD, (head + 1) * HEAD)
            keys = key_ref[0, at, :live].T
            values = value_ref[0, at, :live].T
            queries = query_ref[0, at, :]
            dout = dout_ref[at, :]
            weighted = jnp.sum(
                dout.astype(F32) * out_ref[at, :].astype(F32), axis=0, keepdims=True
            )
            totals = total_ref[0, head : head + 1, :]
            dquery = jnp.zeros((HEAD, span), F32)
            for start in range(0, live, key_block):
                rows = slice(start, start + key_block)
                probs = jnp.exp2(dot(keys[rows], queries, NN) * LOG2_SCALE - totals)
                dprobs = dot(values[rows], dout, NN)
                dscores = (probs * (dprobs - weighted)).astype(BF)
                dvalue = dot(dout, probs.astype(BF), NT)
                dkey = dot(queries, dscores, NT) * HEAD ** (-0.5)
                dquery = dquery + dot(key_ref[0, at, rows], dscores, NN)
                turned(dkey, cos_ref[:, rows], sin_ref[:, rows], grad_ref, 1, head, rows)
                grad_ref[2, at, rows] = dvalue.astype(BF)
            turned(dquery * HEAD ** (-0.5), cos_ref[...], sin_ref[...], grad_ref, 0, head, slice(0, span))
        if live < span:
            empty = jnp.zeros((per_step * HEAD, span - live), BF)
            grad_ref[1, :, live:] = empty
            grad_ref[2, :, live:] = empty

    def body(length_ref, *refs):
        for live in live_lengths(span):

            @pl.when(length_ref[0] == live)
            def _():
                one_length(live, *refs)

    rows = per_step * HEAD

    def part(c):
        return pl.BlockSpec((1, rows, span), lambda i, n: (c, piece, 0))

    flat = pl.BlockSpec((rows, span), lambda i, n: (piece, 0))
    table = pl.BlockSpec((HALF, span), lambda i, n: (0, 0))
    return call(
        body,
        (1,),
        [part(0), part(1), part(2), flat, flat, pl.BlockSpec((1, per_step, span), lambda i, n: (piece, 0, 0)), table, table],
        [pl.BlockSpec((3, rows, span), lambda i, n: (0, 0, 0))],
        [shaped((3, rows, span), BF)],
        40 * span * span * rows,
        prefetch=1,
        after=after,
    )(length, joined, joined, joined, attended, dattended, totals, cosine, sine)[0]


def middle(attended, tokens, upstream, outs, ups, downs, biases, vectors):
    features = tokens.shape[1]
    width, span = attended.shape
    part = outs[0].shape[0]
    hidden = ups[0].shape[1]
    rows = 256
    columns_each = 256

    def body(att_ref, tok_ref, g_ref, out_a, out_b, up_a, up_b, down_a, down_b, bias_a, bias_b, vec_ref,
             branch_ref, h_ref, db_two, act_a, act_b, du_a, du_b, dmid_ref, db_one, datt_ref, sum_ref, gb_a, gb_b):
        @pl.when(pl.program_id(0) == 0)
        def _():
            sum_ref[...] = jnp.zeros_like(sum_ref)
            gb_a[...] = jnp.zeros_like(gb_a)
            gb_b[...] = jnp.zeros_like(gb_b)

        branch = dot(att_ref[:part], out_a[...], TN) + dot(att_ref[part:], out_b[...], TN)
        branch_ref[...] = branch
        gate = vec_ref[2:3, :]
        hat, inverse = normed_rows(tok_ref[...].astype(F32) + gate * branch)
        h = (hat * vec_ref[3:4, :] + vec_ref[4:5, :]).astype(BF)
        h_ref[...] = h
        g = g_ref[...].astype(F32)
        db = (vec_ref[5:6, :] * g).astype(BF)
        db_two[...] = db
        for up, down, bias, act, du_ref, gb in (
            (up_a, down_a, bias_a, act_a, du_a, gb_a),
            (up_b, down_b, bias_b, act_b, du_b, gb_b),
        ):
            for at in range(0, hidden, columns_each):
                columns = slice(at, at + columns_each)
                upper = dot(h, up[:, columns], NN) + bias[0:1, columns]
                dact = dot(db, down[columns, :], NT)
                inner = GELU_A + (GELU_A * GELU_B) * (upper * upper)
                tanh = jnp.tanh(upper * inner)
                lean = 0.5 + 0.5 * tanh
                value = upper * lean
                act[:, columns] = value.astype(BF)
                slope = lean + value * (1.0 - tanh) * (3.0 * inner - 2.0 * GELU_A)
                du = (dact * slope).astype(BF)
                du_ref[:, columns] = du
                gb[0:1, columns] += jnp.sum(du.astype(F32), axis=0, keepdims=True)
        dh = dot(du_a[...], up_a[...], NT) + dot(du_b[...], up_b[...], NT)
        e = dh * vec_ref[3:4, :]
        e_mean = jnp.mean(e, axis=-1, keepdims=True)
        eh_mean = jnp.mean(e * hat, axis=-1, keepdims=True)
        dmid = g + (e - e_mean - hat * eh_mean) * inverse
        dmid_ref[...] = dmid
        db = (gate * dmid).astype(BF)
        db_one[...] = db
        datt_ref[:part] = dot(out_a[...], db, NT).astype(BF)
        datt_ref[part:] = dot(out_b[...], db, NT).astype(BF)
        sum_ref[0:1, :] += jnp.sum(dh, axis=0, keepdims=True)
        sum_ref[1:2, :] += jnp.sum(dh * hat, axis=0, keepdims=True)
        sum_ref[2:3, :] += jnp.sum(dmid * branch_ref[...], axis=0, keepdims=True)
        sum_ref[3:4, :] += jnp.sum(db_two[...].astype(F32), axis=0, keepdims=True)

    whole = lambda i: (0, 0)
    tok = pl.BlockSpec((rows, features), lambda i: (i, 0))
    wide = pl.BlockSpec((rows, hidden), lambda i: (i, 0))
    att = pl.BlockSpec((width, rows), lambda i: (0, i))
    fixed = lambda a: pl.BlockSpec(a.shape, whole, pipeline_mode=pl.Buffered(1))
    sums = pl.BlockSpec((1, hidden), whole)
    return call(
        body,
        (span // rows,),
        [att, tok, tok] + [fixed(a) for a in (*outs, *ups, *downs, *biases, vectors)],
        [tok, tok, tok, wide, wide, wide, wide, tok, tok, att, pl.BlockSpec((8, features), whole), sums, sums],
        [
            shaped((span, features), F32),
            shaped((span, features), BF),
            shaped((span, features), BF),
            *[shaped((span, hidden), BF)] * 4,
            shaped((span, features), F32),
            shaped((span, features), BF),
            shaped((width, span), BF),
            shaped((8, features), F32),
            shaped((1, hidden), F32),
            shaped((1, hidden), F32),
        ],
        4 * span * features * width + 12 * span * features * hidden,
    )(attended, tokens, upstream, *outs, *ups, *downs, *biases, vectors)


def weight_grad(left, right, out_type, received=None, bit=None, after=()):
    span, height = left.shape
    features = right.shape[1]
    block = height // 2
    count = height // block
    half = count // 2
    flops = 2 * span * height * features
    fixed = pl.BlockSpec(right.shape, lambda i, *n: (0, 0))
    if bit is None:

        def body(left_ref, right_ref, *rest):
            product = dot(left_ref[...], right_ref[...], TN)
            if received is not None:
                product = product + rest[0][...].astype(F32)
            rest[-1][...] = product.astype(out_type)

        row = pl.BlockSpec((block, features), lambda i: (i, 0))
        more = () if received is None else (received,)
        return call(
            body,
            (count,),
            [pl.BlockSpec((span, block), lambda i: (0, i)), fixed] + [row] * len(more),
            [row],
            [shaped((height, features), out_type)],
            flops,
            after=after,
        )(left, right, *more)[0]

    def body(bit_ref, left_ref, right_ref, received_ref, kept_ref, leaving_ref):
        product = dot(left_ref[...], right_ref[...], TN) + received_ref[...].astype(F32)

        @pl.when(pl.program_id(0) < half)
        def _():
            leaving_ref[...] = product.astype(BF)

        @pl.when(pl.program_id(0) >= half)
        def _():
            kept_ref[...] = product

    def place(i, n):
        return jnp.where(i < half, (1 - n[0]) * half + i, n[0] * half + i - half)

    return call(
        body,
        (count,),
        [
            pl.BlockSpec((span, block), lambda i, n: (0, place(i, n))),
            fixed,
            pl.BlockSpec((block, features), lambda i, n: (place(i, n), 0)),
        ],
        [
            pl.BlockSpec((block, features), lambda i, n: (jnp.maximum(i - half, 0), 0)),
            pl.BlockSpec((block, features), lambda i, n: (jnp.minimum(i, half - 1), 0)),
        ],
        [shaped((height // 2, features), F32), shaped((height // 2, features), BF)],
        flops,
        prefetch=1,
        after=after,
    )(bit, left, right, received)


def out_grad(attended, dbranch, which, out_type, received=None, bit=None, after=()):
    width, span = attended.shape
    features = dbranch.shape[1]
    height, block = width // 2, features // 2
    flops = 2 * span * height * features

    def product_of(att_ref, db_ref, received_ref):
        product = dot(att_ref[...], db_ref[...], NN)
        return product if received is None else product + received_ref[...].astype(F32)

    if bit is None:

        def body(att_ref, db_ref, *rest):
            rest[-1][...] = product_of(att_ref, db_ref, rest[0]).astype(out_type)

        part = pl.BlockSpec((height, block), lambda i: (i, 0))
        more = () if received is None else (received,)
        return call(
            body,
            (2,),
            [
                pl.BlockSpec((height, span), lambda i: (which, 0)),
                pl.BlockSpec((span, block), lambda i: (0, i)),
            ]
            + [part] * len(more),
            [part],
            [shaped((2 * height, block), out_type)],
            flops,
            after=after,
        )(attended, dbranch, *more)[0]

    def body(bit_ref, att_ref, db_ref, received_ref, kept_ref, leaving_ref):
        product = product_of(att_ref, db_ref, received_ref)

        @pl.when(pl.program_id(0) == 0)
        def _():
            leaving_ref[...] = product.astype(BF)

        @pl.when(pl.program_id(0) == 1)
        def _():
            kept_ref[...] = product

    def place(i, n):
        return jnp.where(i == 0, 1 - n[0], n[0])

    half = pl.BlockSpec((height, block), lambda i, n: (0, 0))
    return call(
        body,
        (2,),
        [
            pl.BlockSpec((height, span), lambda i, n: (which, 0)),
            pl.BlockSpec((span, block), lambda i, n: (0, place(i, n))),
            pl.BlockSpec((height, block), lambda i, n: (place(i, n), 0)),
        ],
        [half, half],
        [shaped((height, block), F32), shaped((height, block), BF)],
        flops,
        prefetch=1,
        after=after,
    )(bit, attended, dbranch, received)


def sent_first(blocks):
    half = blocks // 2

    def place(i, n):
        return jnp.where(i < half, (1 - n[0]) * half + i, n[0] * half + i - half)

    def gone(i, n):
        return (jnp.minimum(i, half - 1), 0)

    def kept(i, n):
        return (n[0], jnp.maximum(i - half, 0), 0)

    return place, gone, kept


def finish_forward(mine, acts, downs, branch, tokens, upstream, vectors, after=()):
    span, hidden = acts[0].shape
    features = tokens.shape[1]
    rows = 256
    count = span // rows
    place, gone, kept = sent_first(count)

    def body(mine_ref, act_a, act_b, down_a, down_b, branch_ref, tok_ref, g_ref, vec_ref, gone_ref, kept_ref, sum_ref):
        second = dot(act_a[...], down_a[...], NN) + dot(act_b[...], down_b[...], NN) + vec_ref[6:7, :]
        middle = tok_ref[...].astype(F32) + vec_ref[2:3, :] * branch_ref[...]
        out = (middle + vec_ref[5:6, :] * second).astype(BF)
        sums = jnp.sum(g_ref[...].astype(F32) * second, axis=0, keepdims=True)

        @pl.when(pl.program_id(0) == 0)
        def _():
            sum_ref[...] = sums

        @pl.when(pl.program_id(0) > 0)
        def _():
            sum_ref[...] += sums

        @pl.when(pl.program_id(0) < count // 2)
        def _():
            gone_ref[...] = out

        @pl.when(pl.program_id(0) >= count // 2)
        def _():
            kept_ref[0] = out

    whole = lambda i, n: (0, 0)
    tok = pl.BlockSpec((rows, features), lambda i, n: (place(i, n), 0))
    wide = pl.BlockSpec((rows, hidden), lambda i, n: (place(i, n), 0))
    fixed = lambda a: pl.BlockSpec(a.shape, whole)
    return call(
        body,
        (count,),
        [wide, wide] + [fixed(a) for a in downs] + [tok, tok, tok, fixed(vectors)],
        [
            pl.BlockSpec((rows, features), gone),
            pl.BlockSpec((1, rows, features), kept),
            pl.BlockSpec((1, features), whole),
        ],
        [
            shaped((span // 2, features), BF),
            shaped((2, span // 2, features), BF),
            shaped((1, features), F32),
        ],
        4 * span * features * hidden,
        prefetch=1,
        after=after,
    )(mine, *acts, *downs, branch, tokens, upstream, vectors)


def project_weight_back(h, pieces, out_type, received=None, bit=None, after=()):
    span, features = h.shape
    _, rows, _ = pieces[0].shape
    width = rows * len(pieces)
    block = features // 2
    flops = 6 * span * features * width
    if bit is None:

        def body(h_ref, *refs):
            joined = jnp.concatenate([ref[0] for ref in refs[: len(pieces)]], axis=0)
            product = dot(h_ref[...], joined, TT)
            if received is not None:
                product = product + refs[-2][...].astype(F32)
            refs[-1][...] = product.astype(out_type)

        row = pl.BlockSpec((features, width), lambda c: (c, 0))
        more = () if received is None else (received,)
        return call(
            body,
            (3,),
            [pl.BlockSpec((span, features), lambda c: (0, 0))]
            + [pl.BlockSpec((1, rows, span), lambda c: (c, 0, 0))] * len(pieces)
            + [row] * len(more),
            [row],
            [shaped((3 * features, width), out_type)],
            flops,
            after=after,
        )(h, *pieces, *more)[0]

    def body(bit_ref, h_ref, *refs):
        joined = jnp.concatenate([ref[0] for ref in refs[: len(pieces)]], axis=0)
        received_ref, kept_ref, leaving_ref = refs[len(pieces) :]
        product = dot(h_ref[...], joined, TT) + received_ref[...].astype(F32)

        @pl.when(pl.program_id(0) < 3)
        def _():
            leaving_ref[...] = product.astype(BF)

        @pl.when(pl.program_id(0) >= 3)
        def _():
            kept_ref[...] = product

    def place(i, n):
        return jnp.where(i < 3, (1 - n[0]) * 3 + i, n[0] * 3 + i - 3)

    return call(
        body,
        (6,),
        [pl.BlockSpec((span, block), lambda i, n: (0, place(i, n) % 2))]
        + [pl.BlockSpec((1, rows, span), lambda i, n: (place(i, n) // 2, 0, 0))] * len(pieces)
        + [pl.BlockSpec((block, width), lambda i, n: (place(i, n), 0))],
        [
            pl.BlockSpec((block, width), lambda i, n: (jnp.maximum(i - 3, 0), 0)),
            pl.BlockSpec((block, width), lambda i, n: (jnp.minimum(i, 2), 0)),
        ],
        [shaped((3 * block, width), F32), shaped((3 * block, width), BF)],
        flops,
        prefetch=1,
        after=after,
    )(bit, h, *pieces, received)


def project_back(mine, pieces, weights, tokens, dmiddle, vectors, after=()):
    _, part, span = pieces[0].shape
    features = tokens.shape[1]
    width = weights[0].shape[2]
    rows = 256
    count = span // rows
    each = len(pieces) // 2
    place, gone, kept = sent_first(count)

    def body(mine_ref, *refs):
        pieces, rest = refs[: 2 * each], refs[2 * each :]
        w_a, w_b, tok_ref, dmid_ref, vec_ref, gone_ref, kept_ref, sum_ref = rest
        dh = jnp.zeros((rows, features), F32)
        for c in range(3):
            for weight, held in ((w_a, pieces[:each]), (w_b, pieces[each:])):
                joined = jnp.concatenate([ref[c] for ref in held], axis=0)
                dh = dh + dot(joined, weight[c], TT)
        hat, inverse = normed_rows(tok_ref[...].astype(F32))
        e = dh * vec_ref[0:1, :]
        e_mean = jnp.mean(e, axis=-1, keepdims=True)
        eh_mean = jnp.mean(e * hat, axis=-1, keepdims=True)
        out = dmid_ref[...] + (e - e_mean - hat * eh_mean) * inverse
        sums = jnp.concatenate(
            [
                jnp.sum(dh, axis=0, keepdims=True),
                jnp.sum(dh * hat, axis=0, keepdims=True),
                jnp.zeros((6, features), F32),
            ],
            axis=0,
        )

        @pl.when(pl.program_id(0) == 0)
        def _():
            sum_ref[...] = sums

        @pl.when(pl.program_id(0) > 0)
        def _():
            sum_ref[...] += sums

        @pl.when(pl.program_id(0) < count // 2)
        def _():
            gone_ref[...] = out

        @pl.when(pl.program_id(0) >= count // 2)
        def _():
            kept_ref[0] = out

    whole = lambda i, n: (0, 0)
    tok = pl.BlockSpec((rows, features), lambda i, n: (place(i, n), 0))
    joined = pl.BlockSpec((3, part, rows), lambda i, n: (0, 0, place(i, n)))
    weight = pl.BlockSpec((3, features, width), lambda i, n: (0, 0, 0))
    return call(
        body,
        (count,),
        [joined] * len(pieces) + [weight, weight, tok, tok, pl.BlockSpec(vectors.shape, whole)],
        [
            pl.BlockSpec((rows, features), gone),
            pl.BlockSpec((1, rows, features), kept),
            pl.BlockSpec((8, features), whole),
        ],
        [
            shaped((span // 2, features), F32),
            shaped((2, span // 2, features), F32),
            shaped((8, features), F32),
        ],
        12 * span * features * width,
        prefetch=1,
        after=after,
    )(mine, *pieces, *weights, tokens, dmiddle, vectors)


def collect(sums_one, sums_two, dgate_two, bias_other, vectors):
    features = vectors.shape[1]

    def body(one_ref, two_ref, gate_ref, bias_ref, vec_ref, out_ref):
        def rounded(value):
            return value.astype(BF).astype(F32)

        one, two = one_ref[...], two_ref[...]
        out_ref[...] = jnp.concatenate(
            [
                one[1:2] * vec_ref[7:8, :],
                two[1:2] * vec_ref[8:9, :],
                two[3:4],
                rounded(one[0:1]),
                rounded(one[1:2] * vec_ref[9:10, :]),
                rounded(two[2:3]),
                rounded(two[0:1]),
                rounded(two[1:2] * vec_ref[10:11, :]),
                rounded(gate_ref[...]),
                vec_ref[11:12, :],
                bias_ref[:, :features],
                bias_ref[:, features:],
                jnp.zeros((4, features), F32),
            ],
            axis=0,
        )

    whole = lambda a: pl.BlockSpec(a.shape, lambda i: (0, 0))
    operands = (sums_one, sums_two, dgate_two, bias_other, vectors)
    out = shaped((16, features), F32)
    return call(body, (1,), [whole(a) for a in operands], [whole(out)], [out], 1000)(*operands)[0]


def chip_rows(mine, held, arrived, bias_own):
    features = held.shape[1]

    def body(mine_ref, held_ref, arrived_ref, bias_ref, out_ref):
        held, arrived = held_ref[...], arrived_ref[...]
        first = mine_ref[0] == 0
        low = jnp.where(first, held, arrived)
        high = jnp.where(first, arrived, held)
        sums = jnp.concatenate(
            [
                held[0:3] + arrived[0:3],
                bias_ref[:, :features] + arrived[10:11],
                bias_ref[:, features:] + arrived[11:12],
            ],
            axis=0,
        )
        top = sums.astype(BF).astype(F32)
        out_ref[...] = jnp.concatenate(
            [low[3:9], high[3:9], low[9:10], high[9:10], top, sums - top], axis=0
        ).astype(BF)

    whole = lambda a: pl.BlockSpec(a.shape, lambda i, n: (0, 0))
    operands = (held, arrived, bias_own)
    out = shaped((24, features), BF)
    return call(
        body, (1,), [whole(a) for a in operands], [whole(out)], [out], 1000, prefetch=1
    )(mine, *operands)[0]


def halving_steps(size):
    if size == 16:
        return [
            (1, lambda d: d & 1),
            (2, lambda d: (d >> 1) & 1),
            (4, lambda d: ((d >> 2) ^ (d >> 3)) & 1),
            (12, lambda d: (d >> 3) & 1),
        ]
    steps, mask = [], 1
    while mask < size:
        steps.append((mask, partial(lambda shift, d: (d >> shift) & 1, len(steps))))
        mask *= 2
    return steps


def fold(kept, arrived, bit, after=()):
    count = len(kept)

    def body(bit_ref, *refs):
        for at in range(count):
            kept_ref, arrived_ref, stay_ref, leave_ref = refs[at::count]
            total = kept_ref[...] + arrived_ref[...].astype(F32)

            @pl.when(pl.program_id(0) == 0)
            def _():
                leave_ref[...] = total.astype(BF)

            @pl.when(pl.program_id(0) == 1)
            def _():
                stay_ref[...] = total

    def place(at, i, n):
        return (jnp.where(i == 0, 1 - n[at], n[at]), 0)

    halves = [(a.shape[0] // 2, a.shape[1]) for a in kept]
    blocks = [pl.BlockSpec(half, partial(place, at)) for at, half in enumerate(halves)]
    fixed = [pl.BlockSpec(half, lambda i, n: (0, 0)) for half in halves]
    out = call(
        body,
        (2,),
        blocks * 2,
        fixed * 2,
        [shaped(half, F32) for half in halves] + [shaped(half, BF) for half in halves],
        sum(a.size for a in kept),
        prefetch=1,
        after=after,
    )(bit, *kept, *arrived)
    return out[:count], out[count:]


def fold_last(kept, arrived, after=()):
    count = len(kept)

    def body(*refs):
        for at in range(count):
            kept_ref, arrived_ref, out_ref = refs[at::count]
            out_ref[...] = (kept_ref[...].astype(F32) + arrived_ref[...].astype(F32)).astype(BF)

    whole = [pl.BlockSpec(a.shape, lambda i: (0, 0)) for a in kept]
    return call(
        body,
        (1,),
        whole * 2,
        whole,
        [shaped(a.shape, BF) for a in kept],
        sum(a.size for a in kept),
        after=after,
    )(*kept, *arrived)


def join(held, arrived, bit, out_type=BF, ways=(), after=()):
    count = len(held)
    ways = ways or ("above",) * count

    def body(bit_ref, *refs):
        for at in range(count):
            own = pl.program_id(0) == bit_ref[at]
            held_ref, arrived_ref, out_ref = refs[at::count]

            def lay(ref, at=at, out_ref=out_ref):
                value = ref[...].astype(out_type)
                out_ref[...] = value.T if ways[at] == "turned" else value

            pl.when(own)(partial(lay, held_ref))
            pl.when(jnp.logical_not(own))(partial(lay, arrived_ref))

    fixed = [pl.BlockSpec(a.shape, lambda i, n: (0, 0)) for a in held]
    blocks, shapes = [], []
    for a, way in zip(held, ways):
        rows, width = a.shape[::-1] if way == "turned" else a.shape
        if way == "above":
            blocks.append(pl.BlockSpec((rows, width), lambda i, n: (i, 0)))
            shapes.append(shaped((2 * rows, width), out_type))
        else:
            blocks.append(pl.BlockSpec((rows, width), lambda i, n: (0, i)))
            shapes.append(shaped((rows, 2 * width), out_type))
    return call(
        body,
        (2,),
        fixed * 2,
        blocks,
        shapes,
        sum(a.size for a in held),
        prefetch=1,
        after=after,
    )(bit, *held, *arrived)


HALVED = 3


class Halving:
    def __init__(self, dp_size, tensor_size, dp_index, tensor_index, orders):
        steps = halving_steps(dp_size)
        self.count = len(steps)
        self.pairs, bits = [], []
        for at in range(self.count):
            self.pairs.append([])
            bits.append([])
            for order in orders:
                chosen = [steps[order[t][at]] for t in range(tensor_size)]
                self.pairs[at].append(
                    [
                        (d * tensor_size + t, (d ^ chosen[t][0]) * tensor_size + t)
                        for d in range(dp_size)
                        for t in range(tensor_size)
                    ]
                )
                bit = chosen[0][1](dp_index)
                for t in range(1, tensor_size):
                    bit = jnp.where(tensor_index == t, chosen[t][1](dp_index), bit)
                bits[at].append(bit.astype(jnp.int32).reshape(1))
        self.single = bits
        self.bits = [jnp.concatenate(row) if len(row) > 1 else row[0] for row in bits]
        table = None
        for t, order in enumerate(orders[0]):
            places = np.zeros((dp_size, dp_size), np.float32)
            for d in range(dp_size):
                at = 0
                for step in order[:HALVED] + order[HALVED:][::-1]:
                    at = 2 * at + steps[step][1](d)
                places[d, at] = 1.0
            table = places if t == 0 else jnp.where(tensor_index == t, places, table)
        self.table = table
        self.at = 0
        self.payload = None

    def begin(self, *parts):
        self.kept, self.leaving = zip(*parts)
        return tuple(self.leaving)

    def exchange(self, place):
        if self.payload is not None:
            arrived = lax.ppermute(self.payload, ("dp", "tensor"), self.pairs[place][0])
            self.payload = jnp.where(
                self.single[place][0][0] == 0,
                jnp.concatenate([self.payload, arrived], axis=0),
                jnp.concatenate([arrived, self.payload], axis=0),
            )
        return [
            lax.ppermute(part, ("dp", "tensor"), pairs)
            for part, pairs in zip(self.leaving, self.pairs[place])
        ]

    def move(self, after=()):
        if self.at < HALVED:
            arrived = self.exchange(self.at)
            self.at += 1
            if self.at < HALVED:
                self.kept, self.leaving = fold(self.kept, arrived, self.bits[self.at], after)
            else:
                self.leaving = fold_last(self.kept, arrived, after)
        elif self.at < self.count:
            arrived = self.exchange(self.at)
            self.at += 1
            self.leaving = fold_last(self.leaving, arrived, after)
        else:
            place = self.count + HALVED - 1 - self.at
            arrived = self.exchange(place)
            self.at += 1
            self.leaving = join(self.leaving, arrived, self.bits[place], after=after)
        return tuple(self.leaving)

    def last(self):
        self.arrived = self.exchange(0)
        return tuple(self.arrived)

    def finish(self, ways=(), after=()):
        return join(self.leaving, self.arrived, self.bits[0], F32, ways, after)

    def spread(self, value):
        self.payload = value[None]

    def spreaded(self):
        flat = self.payload.reshape(self.payload.shape[0], -1)
        return dot(jnp.asarray(self.table).astype(BF), flat, NN).astype(BF)


def per_device(
    dp_size,
    tensor_size,
    tokens,
    condition,
    lengths,
    modulation_weight,
    modulation_bias,
    first_gain,
    query_key_value_weight,
    attention_out_weight,
    second_gain,
    up_projection_weight,
    upward_bias,
    down_projection_weight,
    downward_bias,
    cotangent,
):
    sequences, span, features = tokens.shape
    hidden = up_projection_weight.shape[1]
    width = attention_out_weight.shape[0]
    dp_index = lax.axis_index("dp")
    mine = lax.axis_index("tensor")
    swap = [(0, 1), (1, 0)]

    def from_sibling(value):
        return lax.ppermute(value, "tensor", swap)

    def ordered(own, other, axis):
        return jnp.where(
            mine == 0,
            jnp.concatenate([own, other], axis=axis),
            jnp.concatenate([other, own], axis=axis),
        )

    qkv_own = query_key_value_weight.transpose(1, 0, 2)
    qkv_weights = (qkv_own, from_sibling(qkv_own))
    out_weights = (attention_out_weight, from_sibling(attention_out_weight))
    up_weights = (up_projection_weight, from_sibling(up_projection_weight))
    up_biases = (upward_bias[None], from_sibling(upward_bias)[None])
    down_weights = (down_projection_weight, from_sibling(down_projection_weight))
    gone = lax.dynamic_index_in_dim(cotangent, 1 - mine, 0, keepdims=False)
    kept = lax.dynamic_index_in_dim(cotangent, mine, 0, keepdims=False)
    upstream = ordered(kept, from_sibling(gone), 0)
    rows = lax.dynamic_index_in_dim(tokens, mine, 0, keepdims=False)
    length = lax.dynamic_slice_in_dim(lengths, mine, 1, 0)

    cond_float = condition.astype(F32)
    silu_values, silu_pull = jax.vjp(jax.nn.silu, cond_float)
    silu_cond = silu_values.astype(BF)
    mods = dot(silu_cond, modulation_weight, NN) + modulation_bias
    mods = lax.dynamic_index_in_dim(mods, mine, 0, keepdims=False).reshape(6, features)
    shift_one, scale_one, gate_one, shift_two, scale_two, gate_two = mods
    silu_row = lax.dynamic_index_in_dim(silu_cond, mine, 0, keepdims=False).astype(F32)
    vectors = jnp.stack(
        [
            first_gain * (1.0 + scale_one),
            shift_one,
            gate_one,
            second_gain * (1.0 + scale_two),
            shift_two,
            gate_two,
            downward_bias,
            1.0 + scale_one,
            1.0 + scale_two,
            first_gain,
            second_gain,
            jnp.pad(silu_row, (0, features - silu_row.shape[0])),
        ]
        + [jnp.zeros((features,), F32)] * 4
    )
    cosine, sine = (jnp.asarray(table) for table in rotary_tables(span))

    leading, joined = project(rows, qkv_weights, vectors, cosine, sine)
    attended, totals = attend(length, joined)
    (
        branch_one, trailing, dbranch, act_own, act_other, dupper_own, dupper_other,
        dmiddle, dbranch_one, dattended, sums_two, gb_own, gb_other,
    ) = middle(
        attended, rows, upstream, out_weights, up_weights, down_weights, up_biases, vectors
    )
    halving = dp_size == 16
    orders = ((0, 1, 2, 3), (1, 0, 2, 3))

    def job(parts):
        return Halving(dp_size, tensor_size, dp_index, mine, (orders,) * parts) if halving else None

    def advance(work, *after):
        return work.move(after) if halving else ()

    def back(piece, after):
        return attend_back(
            length, joined, attended, dattended, totals, cosine, sine, piece, after=after
        )

    sum_down, sum_up, sum_input = job(1), job(2), job(1)
    gd_other = weight_grad(act_other, dbranch, BF)
    gu_other = weight_grad(dupper_other, trailing, BF, after=(gd_other,))
    go_other = out_grad(attended, dbranch_one, 1, BF, after=(gu_other,))
    gd_other, gu_other, go_other = (from_sibling(value) for value in (gd_other, gu_other, go_other))
    count = width // (2 * HEAD)
    backs = [None] * (2 * count)
    other, own = list(range(count, 2 * count)), list(range(count))
    if halving:
        sent = sum_down.begin(weight_grad(act_own, dbranch, F32, gd_other, sum_down.single[0][0]))
        for piece in other[:-1]:
            backs[piece] = back(piece, sent)
            sent = (backs[piece],)
        sent = advance(sum_down, *sent)
        bits = sum_up.single[0]
        up_parts = weight_grad(dupper_own, trailing, F32, gu_other, bits[0], after=sent)
        out_parts = out_grad(attended, dbranch_one, 0, F32, go_other, bits[1], after=up_parts[1:])
        sent = sum_up.begin(up_parts, out_parts)
        sent = sent + advance(sum_down, out_parts[1])
    else:
        grad_downward_weight = lax.psum(weight_grad(act_own, dbranch, F32, gd_other), "dp")
        grad_upward_weight = lax.psum(weight_grad(dupper_own, trailing, F32, gu_other), "dp").T
        both = lax.psum(out_grad(attended, dbranch_one, 0, F32, go_other), "dp")
        grad_output_weight = jnp.concatenate([both[:width], both[width:]], axis=1)
        sent = ()
        for piece in other[:-1]:
            backs[piece] = back(piece, sent)

    piece = other[-1]
    backs[piece] = back(piece, sent)
    sent = (backs[piece],) + advance(sum_down, backs[piece])
    product = project_weight_back(leading, backs[count:], BF, after=sent)
    gq_other = from_sibling(product)
    sent = (product,) + advance(sum_up, product)
    plan = [(sum_down,), (sum_up, sum_down), (sum_up, sum_down)]
    for place, piece in enumerate(own):
        backs[piece] = back(piece, sent)
        sent = (backs[piece],)
        for work in plan[place % len(plan)]:
            sent = sent + advance(work, backs[piece])
    if halving:
        parts = project_weight_back(
            leading, backs[:count], F32, gq_other, sum_input.single[0][0], after=sent
        )
        sent = sum_input.begin(parts)
        sent = sent + advance(sum_up, *sent)
    else:
        grad_input_weight = lax.psum(project_weight_back(leading, backs[:count], F32, gq_other), "dp")
    which = mine.astype(jnp.int32).reshape(1)
    gone_tokens, grad_tokens, sums_one = project_back(
        which, backs, qkv_weights, rows, dmiddle, vectors, after=sent
    )
    sent = advance(sum_input, gone_tokens) + advance(sum_up, gone_tokens)
    if halving:
        sent = sent + sum_down.last()
    gone_output, output, dgate_two = finish_forward(
        which, (act_own, act_other), down_weights, branch_one, rows, upstream, vectors, after=sent
    )
    sent = advance(sum_input, gone_output) + advance(sum_up, gone_output)

    grad_tokens = lax.dynamic_update_index_in_dim(
        grad_tokens, from_sibling(gone_tokens), 1 - mine, 0
    )
    output = lax.dynamic_update_index_in_dim(output, from_sibling(gone_output), 1 - mine, 0)

    held = collect(sums_one, sums_two, dgate_two, gb_other, vectors)
    chip = chip_rows(which, held, from_sibling(held), gb_own)
    wide, six = 6 * features, 6 * sequences
    sums_at, sums_count = six + sequences, 3 + hidden // features
    pair = chip[:six].reshape(sequences, wide)
    grad_condition = silu_pull(dot(pair, modulation_weight, NT))[0]
    if halving:
        (grad_downward_weight,) = sum_down.finish(after=sent)
        sent = advance(sum_input, grad_downward_weight)
        sum_input.spread(chip)
        sum_up.last()
        grad_upward_weight, grad_output_weight = sum_up.finish(("turned", "beside"), after=sent)
        advance(sum_input, grad_upward_weight)
        advance(sum_input, grad_tokens, output)
        advance(sum_input)
        sum_input.last()
        (grad_input_weight,) = sum_input.finish()
        gathered = sum_input.spreaded().reshape(dp_size, chip.shape[0], features)
    else:
        gathered = lax.all_gather(chip, "dp", axis=0)
    dmods_low = gathered[:, :six].reshape(-1, wide)
    everyone = gathered[:, six:sums_at, : silu_row.shape[0]].reshape(-1, silu_row.shape[0])
    sums = gathered[:, sums_at : sums_at + sums_count].astype(F32)
    sums = jnp.sum(sums + gathered[:, sums_at + sums_count :].astype(F32), axis=0)
    grad_input_weight = grad_input_weight.reshape(3, features, width).transpose(1, 0, 2)
    grad_modulation_bias = jnp.sum(dmods_low, axis=0, dtype=F32)
    grad_modulation_weight = dot(everyone, dmods_low, TN)
    grad_first_gain, grad_second_gain, grad_downward_bias = sums[0], sums[1], sums[2]
    grad_upward_bias = sums[3:].reshape(hidden)
    return (
        output,
        grad_tokens,
        grad_condition,
        grad_modulation_weight,
        grad_modulation_bias,
        grad_first_gain,
        grad_input_weight,
        grad_output_weight,
        grad_second_gain,
        grad_upward_weight,
        grad_upward_bias,
        grad_downward_weight,
        grad_downward_bias,
    )


def solution(mesh):
    placed = (
        P("dp", None, None),
        P("dp", None),
        P("dp"),
        P(),
        P(),
        P(),
        P(None, None, "tensor"),
        P("tensor", None),
        P(),
        P(None, "tensor"),
        P("tensor"),
        P("tensor", None),
        P(),
        P("dp", "tensor", None),
    )
    return jax.shard_map(
        partial(per_device, mesh.shape["dp"], mesh.shape["tensor"]),
        mesh=mesh,
        in_specs=placed,
        out_specs=(
            P("dp", "tensor", None),
            P("dp", "tensor", None),
            P("dp", None),
            P(),
            P(),
            P(),
            P(None, None, "tensor"),
            P("tensor", None),
            P(),
            P(None, "tensor"),
            P("tensor"),
            P("tensor", None),
            P(),
        ),
        check_vma=False,
    )
```

```python
import math
from functools import partial

import jax
import jax.numpy as jnp
import numpy as np
from jax import lax
from jax.experimental import pallas as pl
from jax.experimental.pallas import tpu as pltpu
from jax.sharding import PartitionSpec as P

HEAD = 64
HALF = HEAD // 2
EPS = 1e-05
LOG2_SCALE = math.log2(math.e) * HEAD ** (-0.5)
SAFE_BOUND = 70.0
GELU_A = math.sqrt(2.0 / math.pi)
GELU_B = 0.044715
BF = jnp.bfloat16
F32 = jnp.float32

NN = (((1,), (0,)), ((), ()))
NT = (((1,), (1,)), ((), ()))
TN = (((0,), (0,)), ((), ()))
TT = (((0,), (1,)), ((), ()))
dot = partial(lax.dot_general, preferred_element_type=F32)


def call(body, grid, in_specs, out_specs, out_shape, flops, scratch=(), prefetch=0, spare=8, after=()):
    known = prefetch + len(in_specs)

    def with_after(*refs):
        return body(*refs[:known], *refs[known + len(after) :])

    def run(*operands):
        held = 0
        for spec, array in zip(
            list(in_specs) + list(out_specs), list(operands[prefetch:]) + list(out_shape)
        ):
            size = math.prod(spec.block_shape) * array.dtype.itemsize
            held += size if spec.pipeline_mode is not None else 2 * size
        moved = sum(a.size * a.dtype.itemsize for a in operands)
        moved += sum(math.prod(a.shape) * a.dtype.itemsize for a in out_shape)
        return pl.pallas_call(
            with_after if after else body,
            grid_spec=pltpu.PrefetchScalarGridSpec(
                num_scalar_prefetch=prefetch,
                grid=grid,
                in_specs=list(in_specs) + [pl.BlockSpec(memory_space=pl.ANY)] * len(after),
                out_specs=out_specs,
                scratch_shapes=list(scratch),
            ),
            out_shape=out_shape,
            compiler_params=pltpu.CompilerParams(
                vmem_limit_bytes=min(held + spare * 2**20, 60 * 2**20)
            ),
            cost_estimate=pl.CostEstimate(
                flops=int(flops), bytes_accessed=int(moved), transcendentals=0
            ),
        )(*operands, *after)

    return run


def shaped(shape, dtype):
    return jax.ShapeDtypeStruct(shape, dtype)


def rotary_tables(span):
    frequency = (
        np.float32(10000.0) ** (-(np.arange(HALF, dtype=np.float32) * np.float32(2.0 / HEAD)))
    ).astype(np.float32)
    angles = (np.arange(span, dtype=np.float32)[None, :] * frequency[:, None]).astype(np.float32)
    angles = angles.astype(np.float64)
    return np.cos(angles).astype(np.float32), np.sin(angles).astype(np.float32)


def normed_rows(rows):
    centre = jnp.mean(rows, axis=-1, keepdims=True)
    centred = rows - centre
    spread = jnp.mean(centred * centred, axis=-1, keepdims=True)
    inverse = lax.rsqrt(spread + EPS)
    return centred * inverse, inverse


def project(source, weights, vectors, cosine, sine):
    span, features = source.shape
    width = weights[0].shape[2]

    def body(source_ref, own_ref, other_ref, vector_ref, cos_ref, sin_ref, rows_ref, out_ref):
        step = pl.program_id(0)

        @pl.when(step == 0)
        def _():
            for start in range(0, span, 128):
                hat, _ = normed_rows(source_ref[start : start + 128, :].astype(F32))
                rows_ref[start : start + 128, :] = (
                    hat * vector_ref[0:1, :] + vector_ref[1:2, :]
                ).astype(BF)

        def emit(weight_ref):
            joined = dot(weight_ref[0], rows_ref[...], TT)

            @pl.when(step % 3 < 2)
            def _():
                cos, sin = cos_ref[...], sin_ref[...]
                for at in range(0, width, HEAD):
                    low, high = joined[at : at + HALF], joined[at + HALF : at + HEAD]
                    out_ref[0, at : at + HALF, :] = (low * cos - high * sin).astype(BF)
                    out_ref[0, at + HALF : at + HEAD, :] = (high * cos + low * sin).astype(BF)

            @pl.when(step % 3 == 2)
            def _():
                out_ref[0] = joined.astype(BF)

        @pl.when(step < 3)
        def _():
            emit(own_ref)

        @pl.when(step >= 3)
        def _():
            emit(other_ref)

    whole = lambda i: (0, 0)
    return call(
        body,
        (6,),
        [
            pl.BlockSpec((span, features), whole),
            pl.BlockSpec((1, features, width), lambda i: (jnp.minimum(i, 2), 0, 0)),
            pl.BlockSpec((1, features, width), lambda i: (jnp.maximum(i - 3, 0), 0, 0)),
            pl.BlockSpec(vectors.shape, whole),
            pl.BlockSpec(cosine.shape, whole),
            pl.BlockSpec(sine.shape, whole),
        ],
        [
            pl.BlockSpec((span, features), whole),
            pl.BlockSpec((1, width, span), lambda i: (i % 3, i // 3, 0)),
        ],
        [shaped((span, features), BF), shaped((3, 2 * width, span), BF)],
        12 * span * features * width,
    )(source, *weights, vectors, cosine, sine)


def live_lengths(span):
    return (span, span // 2, span // 8)


def attend(length, joined):
    _, width, span = joined.shape
    per_step = 2
    query_block = min(512, span)

    def one_length(live, query_ref, key_ref, value_ref, out_ref, total_ref):
        key_block = min(512, live)
        for head in range(per_step):
            at = slice(head * HEAD, (head + 1) * HEAD)
            keys = key_ref[0, at, :live].T
            query_size = jnp.sum(jnp.square(query_ref[0, at, :].astype(F32)), axis=0)
            key_size = jnp.sum(jnp.square(key_ref[0, at, :live].astype(F32)), axis=0)
            largest = jnp.max(query_size) * jnp.max(key_size)
            safe = largest < (SAFE_BOUND / HEAD ** (-0.5)) ** 2

            @pl.when(safe)
            def _():
                for first in range(0, span, query_block):
                    columns = slice(first, first + query_block)
                    queries = query_ref[0, at, columns]
                    result = jnp.zeros((HEAD, query_block), F32)
                    total = jnp.zeros((1, query_block), F32)
                    for start in range(0, live, key_block):
                        rows = slice(start, start + key_block)
                        probs = jnp.exp2(dot(keys[rows], queries, NN) * LOG2_SCALE)
                        total = total + jnp.sum(probs, axis=0, keepdims=True)
                        result = result + dot(value_ref[0, at, rows], probs.astype(BF), NN)
                    out_ref[at, columns] = (result * (1.0 / total)).astype(BF)
                    total_ref[0, head : head + 1, columns] = jnp.log2(total)

            @pl.when(jnp.logical_not(safe))
            def _():
                for first in range(0, span, query_block):
                    columns = slice(first, first + query_block)
                    scores = dot(keys, query_ref[0, at, columns], NN) * LOG2_SCALE
                    highest = jnp.max(scores, axis=0, keepdims=True)
                    probs = jnp.exp2(scores - highest)
                    total = jnp.sum(probs, axis=0, keepdims=True)
                    result = dot(value_ref[0, at, :live], probs.astype(BF), NN)
                    out_ref[at, columns] = (result * (1.0 / total)).astype(BF)
                    total_ref[0, head : head + 1, columns] = highest + jnp.log2(total)

    def body(length_ref, query_ref, key_ref, value_ref, out_ref, total_ref):
        for live in live_lengths(span):

            @pl.when(length_ref[0] == live)
            def _():
                one_length(live, query_ref, key_ref, value_ref, out_ref, total_ref)

    rows = per_step * HEAD

    def part(c):
        return pl.BlockSpec((1, rows, span), lambda i, n: (c, i, 0))

    return call(
        body,
        (width // rows,),
        [part(0), part(1), part(2)],
        [
            pl.BlockSpec((rows, span), lambda i, n: (i, 0)),
            pl.BlockSpec((1, per_step, span), lambda i, n: (i, 0, 0)),
        ],
        [shaped((width, span), BF), shaped((width // rows, per_step, span), F32)],
        16 * span * span * width,
        prefetch=1,
    )(length, joined, joined, joined)


def attend_back(length, joined, attended, dattended, totals, cosine, sine, piece, after=()):
    _, width, span = joined.shape
    per_step = 2
    key_block_most = 256

    def turned(grads, cos, sin, out_ref, part, head, columns):
        low, high = grads[:HALF], grads[HALF:]
        top = head * HEAD
        out_ref[part, top : top + HALF, columns] = (low * cos + high * sin).astype(BF)
        out_ref[part, top + HALF : top + HEAD, columns] = (high * cos - low * sin).astype(BF)

    def one_length(live, query_ref, key_ref, value_ref, out_ref, dout_ref, total_ref, cos_ref, sin_ref, grad_ref):
        key_block = min(key_block_most, live)
        for head in range(per_step):
            at = slice(head * HEAD, (head + 1) * HEAD)
            keys = key_ref[0, at, :live].T
            values = value_ref[0, at, :live].T
            queries = query_ref[0, at, :]
            dout = dout_ref[at, :]
            weighted = jnp.sum(
                dout.astype(F32) * out_ref[at, :].astype(F32), axis=0, keepdims=True
            )
            totals = total_ref[0, head : head + 1, :]
            dquery = jnp.zeros((HEAD, span), F32)
            for start in range(0, live, key_block):
                rows = slice(start, start + key_block)
                probs = jnp.exp2(dot(keys[rows], queries, NN) * LOG2_SCALE - totals)
                dprobs = dot(values[rows], dout, NN)
                dscores = (probs * (dprobs - weighted)).astype(BF)
                dvalue = dot(dout, probs.astype(BF), NT)
                dkey = dot(queries, dscores, NT) * HEAD ** (-0.5)
                dquery = dquery + dot(key_ref[0, at, rows], dscores, NN)
                turned(dkey, cos_ref[:, rows], sin_ref[:, rows], grad_ref, 1, head, rows)
                grad_ref[2, at, rows] = dvalue.astype(BF)
            turned(dquery * HEAD ** (-0.5), cos_ref[...], sin_ref[...], grad_ref, 0, head, slice(0, span))
        if live < span:
            empty = jnp.zeros((per_step * HEAD, span - live), BF)
            grad_ref[1, :, live:] = empty
            grad_ref[2, :, live:] = empty

    def body(length_ref, *refs):
        for live in live_lengths(span):

            @pl.when(length_ref[0] == live)
            def _():
                one_length(live, *refs)

    rows = per_step * HEAD

    def part(c):
        return pl.BlockSpec((1, rows, span), lambda i, n: (c, piece, 0))

    flat = pl.BlockSpec((rows, span), lambda i, n: (piece, 0))
    table = pl.BlockSpec((HALF, span), lambda i, n: (0, 0))
    return call(
        body,
        (1,),
        [part(0), part(1), part(2), flat, flat, pl.BlockSpec((1, per_step, span), lambda i, n: (piece, 0, 0)), table, table],
        [pl.BlockSpec((3, rows, span), lambda i, n: (0, 0, 0))],
        [shaped((3, rows, span), BF)],
        40 * span * span * rows,
        prefetch=1,
        after=after,
    )(length, joined, joined, joined, attended, dattended, totals, cosine, sine)[0]


def middle(attended, tokens, upstream, outs, ups, downs, biases, vectors):
    features = tokens.shape[1]
    width, span = attended.shape
    part = outs[0].shape[0]
    hidden = ups[0].shape[1]
    rows = 256
    columns_each = 256

    def body(att_ref, tok_ref, g_ref, out_a, out_b, up_a, up_b, down_a, down_b, bias_a, bias_b, vec_ref,
             branch_ref, h_ref, db_two, act_a, act_b, du_a, du_b, dmid_ref, db_one, datt_ref, sum_ref, gb_a, gb_b):
        @pl.when(pl.program_id(0) == 0)
        def _():
            sum_ref[...] = jnp.zeros_like(sum_ref)
            gb_a[...] = jnp.zeros_like(gb_a)
            gb_b[...] = jnp.zeros_like(gb_b)

        branch = dot(att_ref[:part], out_a[...], TN) + dot(att_ref[part:], out_b[...], TN)
        branch_ref[...] = branch
        gate = vec_ref[2:3, :]
        hat, inverse = normed_rows(tok_ref[...].astype(F32) + gate * branch)
        h = (hat * vec_ref[3:4, :] + vec_ref[4:5, :]).astype(BF)
        h_ref[...] = h
        g = g_ref[...].astype(F32)
        db = (vec_ref[5:6, :] * g).astype(BF)
        db_two[...] = db
        for up, down, bias, act, du_ref, gb in (
            (up_a, down_a, bias_a, act_a, du_a, gb_a),
            (up_b, down_b, bias_b, act_b, du_b, gb_b),
        ):
            for at in range(0, hidden, columns_each):
                columns = slice(at, at + columns_each)
                upper = dot(h, up[:, columns], NN) + bias[0:1, columns]
                dact = dot(db, down[columns, :], NT)
                inner = GELU_A + (GELU_A * GELU_B) * (upper * upper)
                tanh = jnp.tanh(upper * inner)
                lean = 0.5 + 0.5 * tanh
                value = upper * lean
                act[:, columns] = value.astype(BF)
                slope = lean + value * (1.0 - tanh) * (3.0 * inner - 2.0 * GELU_A)
                du = (dact * slope).astype(BF)
                du_ref[:, columns] = du
                gb[0:1, columns] += jnp.sum(du.astype(F32), axis=0, keepdims=True)
        dh = dot(du_a[...], up_a[...], NT) + dot(du_b[...], up_b[...], NT)
        e = dh * vec_ref[3:4, :]
        e_mean = jnp.mean(e, axis=-1, keepdims=True)
        eh_mean = jnp.mean(e * hat, axis=-1, keepdims=True)
        dmid = g + (e - e_mean - hat * eh_mean) * inverse
        dmid_ref[...] = dmid
        db = (gate * dmid).astype(BF)
        db_one[...] = db
        datt_ref[:part] = dot(out_a[...], db, NT).astype(BF)
        datt_ref[part:] = dot(out_b[...], db, NT).astype(BF)
        sum_ref[0:1, :] += jnp.sum(dh, axis=0, keepdims=True)
        sum_ref[1:2, :] += jnp.sum(dh * hat, axis=0, keepdims=True)
        sum_ref[2:3, :] += jnp.sum(dmid * branch_ref[...], axis=0, keepdims=True)
        sum_ref[3:4, :] += jnp.sum(db_two[...].astype(F32), axis=0, keepdims=True)

    whole = lambda i: (0, 0)
    tok = pl.BlockSpec((rows, features), lambda i: (i, 0))
    wide = pl.BlockSpec((rows, hidden), lambda i: (i, 0))
    att = pl.BlockSpec((width, rows), lambda i: (0, i))
    fixed = lambda a: pl.BlockSpec(a.shape, whole, pipeline_mode=pl.Buffered(1))
    sums = pl.BlockSpec((1, hidden), whole)
    return call(
        body,
        (span // rows,),
        [att, tok, tok] + [fixed(a) for a in (*outs, *ups, *downs, *biases, vectors)],
        [tok, tok, tok, wide, wide, wide, wide, tok, tok, att, pl.BlockSpec((8, features), whole), sums, sums],
        [
            shaped((span, features), F32),
            shaped((span, features), BF),
            shaped((span, features), BF),
            *[shaped((span, hidden), BF)] * 4,
            shaped((span, features), F32),
            shaped((span, features), BF),
            shaped((width, span), BF),
            shaped((8, features), F32),
            shaped((1, hidden), F32),
            shaped((1, hidden), F32),
        ],
        4 * span * features * width + 12 * span * features * hidden,
    )(attended, tokens, upstream, *outs, *ups, *downs, *biases, vectors)


def weight_grad(left, right, out_type, received=None, bit=None, after=()):
    span, height = left.shape
    features = right.shape[1]
    block = height // 2
    count = height // block
    half = count // 2
    flops = 2 * span * height * features
    fixed = pl.BlockSpec(right.shape, lambda i, *n: (0, 0))
    if bit is None:

        def body(left_ref, right_ref, *rest):
            product = dot(left_ref[...], right_ref[...], TN)
            if received is not None:
                product = product + rest[0][...].astype(F32)
            rest[-1][...] = product.astype(out_type)

        row = pl.BlockSpec((block, features), lambda i: (i, 0))
        more = () if received is None else (received,)
        return call(
            body,
            (count,),
            [pl.BlockSpec((span, block), lambda i: (0, i)), fixed] + [row] * len(more),
            [row],
            [shaped((height, features), out_type)],
            flops,
            after=after,
        )(left, right, *more)[0]

    def body(bit_ref, left_ref, right_ref, received_ref, kept_ref, leaving_ref):
        product = dot(left_ref[...], right_ref[...], TN) + received_ref[...].astype(F32)

        @pl.when(pl.program_id(0) < half)
        def _():
            leaving_ref[...] = product.astype(BF)

        @pl.when(pl.program_id(0) >= half)
        def _():
            kept_ref[...] = product

    def place(i, n):
        return jnp.where(i < half, (1 - n[0]) * half + i, n[0] * half + i - half)

    return call(
        body,
        (count,),
        [
            pl.BlockSpec((span, block), lambda i, n: (0, place(i, n))),
            fixed,
            pl.BlockSpec((block, features), lambda i, n: (place(i, n), 0)),
        ],
        [
            pl.BlockSpec((block, features), lambda i, n: (jnp.maximum(i - half, 0), 0)),
            pl.BlockSpec((block, features), lambda i, n: (jnp.minimum(i, half - 1), 0)),
        ],
        [shaped((height // 2, features), F32), shaped((height // 2, features), BF)],
        flops,
        prefetch=1,
        after=after,
    )(bit, left, right, received)


def out_grad(attended, dbranch, which, out_type, received=None, bit=None, after=()):
    width, span = attended.shape
    features = dbranch.shape[1]
    height, block = width // 2, features // 2
    flops = 2 * span * height * features

    def product_of(att_ref, db_ref, received_ref):
        product = dot(att_ref[...], db_ref[...], NN)
        return product if received is None else product + received_ref[...].astype(F32)

    if bit is None:

        def body(att_ref, db_ref, *rest):
            rest[-1][...] = product_of(att_ref, db_ref, rest[0]).astype(out_type)

        part = pl.BlockSpec((height, block), lambda i: (i, 0))
        more = () if received is None else (received,)
        return call(
            body,
            (2,),
            [
                pl.BlockSpec((height, span), lambda i: (which, 0)),
                pl.BlockSpec((span, block), lambda i: (0, i)),
            ]
            + [part] * len(more),
            [part],
            [shaped((2 * height, block), out_type)],
            flops,
            after=after,
        )(attended, dbranch, *more)[0]

    def body(bit_ref, att_ref, db_ref, received_ref, kept_ref, leaving_ref):
        product = product_of(att_ref, db_ref, received_ref)

        @pl.when(pl.program_id(0) == 0)
        def _():
            leaving_ref[...] = product.astype(BF)

        @pl.when(pl.program_id(0) == 1)
        def _():
            kept_ref[...] = product

    def place(i, n):
        return jnp.where(i == 0, 1 - n[0], n[0])

    half = pl.BlockSpec((height, block), lambda i, n: (0, 0))
    return call(
        body,
        (2,),
        [
            pl.BlockSpec((height, span), lambda i, n: (which, 0)),
            pl.BlockSpec((span, block), lambda i, n: (0, place(i, n))),
            pl.BlockSpec((height, block), lambda i, n: (place(i, n), 0)),
        ],
        [half, half],
        [shaped((height, block), F32), shaped((height, block), BF)],
        flops,
        prefetch=1,
        after=after,
    )(bit, attended, dbranch, received)


def sent_first(blocks):
    half = blocks // 2

    def place(i, n):
        return jnp.where(i < half, (1 - n[0]) * half + i, n[0] * half + i - half)

    def gone(i, n):
        return (jnp.minimum(i, half - 1), 0)

    def kept(i, n):
        return (n[0], jnp.maximum(i - half, 0), 0)

    return place, gone, kept


def finish_forward(mine, acts, downs, branch, tokens, upstream, vectors, after=()):
    span, hidden = acts[0].shape
    features = tokens.shape[1]
    rows = 256
    count = span // rows
    place, gone, kept = sent_first(count)

    def body(mine_ref, act_a, act_b, down_a, down_b, branch_ref, tok_ref, g_ref, vec_ref, gone_ref, kept_ref, sum_ref):
        second = dot(act_a[...], down_a[...], NN) + dot(act_b[...], down_b[...], NN) + vec_ref[6:7, :]
        middle = tok_ref[...].astype(F32) + vec_ref[2:3, :] * branch_ref[...]
        out = (middle + vec_ref[5:6, :] * second).astype(BF)
        sums = jnp.sum(g_ref[...].astype(F32) * second, axis=0, keepdims=True)

        @pl.when(pl.program_id(0) == 0)
        def _():
            sum_ref[...] = sums

        @pl.when(pl.program_id(0) > 0)
        def _():
            sum_ref[...] += sums

        @pl.when(pl.program_id(0) < count // 2)
        def _():
            gone_ref[...] = out

        @pl.when(pl.program_id(0) >= count // 2)
        def _():
            kept_ref[0] = out

    whole = lambda i, n: (0, 0)
    tok = pl.BlockSpec((rows, features), lambda i, n: (place(i, n), 0))
    wide = pl.BlockSpec((rows, hidden), lambda i, n: (place(i, n), 0))
    fixed = lambda a: pl.BlockSpec(a.shape, whole)
    return call(
        body,
        (count,),
        [wide, wide] + [fixed(a) for a in downs] + [tok, tok, tok, fixed(vectors)],
        [
            pl.BlockSpec((rows, features), gone),
            pl.BlockSpec((1, rows, features), kept),
            pl.BlockSpec((1, features), whole),
        ],
        [
            shaped((span // 2, features), BF),
            shaped((2, span // 2, features), BF),
            shaped((1, features), F32),
        ],
        4 * span * features * hidden,
        prefetch=1,
        after=after,
    )(mine, *acts, *downs, branch, tokens, upstream, vectors)


def project_weight_back(h, pieces, out_type, received=None, bit=None, after=()):
    span, features = h.shape
    _, rows, _ = pieces[0].shape
    width = rows * len(pieces)
    block = features // 2
    flops = 6 * span * features * width
    if bit is None:

        def body(h_ref, *refs):
            joined = jnp.concatenate([ref[0] for ref in refs[: len(pieces)]], axis=0)
            product = dot(h_ref[...], joined, TT)
            if received is not None:
                product = product + refs[-2][...].astype(F32)
            refs[-1][...] = product.astype(out_type)

        row = pl.BlockSpec((features, width), lambda c: (c, 0))
        more = () if received is None else (received,)
        return call(
            body,
            (3,),
            [pl.BlockSpec((span, features), lambda c: (0, 0))]
            + [pl.BlockSpec((1, rows, span), lambda c: (c, 0, 0))] * len(pieces)
            + [row] * len(more),
            [row],
            [shaped((3 * features, width), out_type)],
            flops,
            after=after,
        )(h, *pieces, *more)[0]

    def body(bit_ref, h_ref, *refs):
        joined = jnp.concatenate([ref[0] for ref in refs[: len(pieces)]], axis=0)
        received_ref, kept_ref, leaving_ref = refs[len(pieces) :]
        product = dot(h_ref[...], joined, TT) + received_ref[...].astype(F32)

        @pl.when(pl.program_id(0) < 3)
        def _():
            leaving_ref[...] = product.astype(BF)

        @pl.when(pl.program_id(0) >= 3)
        def _():
            kept_ref[...] = product

    def place(i, n):
        return jnp.where(i < 3, (1 - n[0]) * 3 + i, n[0] * 3 + i - 3)

    return call(
        body,
        (6,),
        [pl.BlockSpec((span, block), lambda i, n: (0, place(i, n) % 2))]
        + [pl.BlockSpec((1, rows, span), lambda i, n: (place(i, n) // 2, 0, 0))] * len(pieces)
        + [pl.BlockSpec((block, width), lambda i, n: (place(i, n), 0))],
        [
            pl.BlockSpec((block, width), lambda i, n: (jnp.maximum(i - 3, 0), 0)),
            pl.BlockSpec((block, width), lambda i, n: (jnp.minimum(i, 2), 0)),
        ],
        [shaped((3 * block, width), F32), shaped((3 * block, width), BF)],
        flops,
        prefetch=1,
        after=after,
    )(bit, h, *pieces, received)


def project_back(mine, pieces, weights, tokens, dmiddle, vectors, after=()):
    _, part, span = pieces[0].shape
    features = tokens.shape[1]
    width = weights[0].shape[2]
    rows = 256
    count = span // rows
    each = len(pieces) // 2
    place, gone, kept = sent_first(count)

    def body(mine_ref, *refs):
        pieces, rest = refs[: 2 * each], refs[2 * each :]
        w_a, w_b, tok_ref, dmid_ref, vec_ref, gone_ref, kept_ref, sum_ref = rest
        dh = jnp.zeros((rows, features), F32)
        for c in range(3):
            for weight, held in ((w_a, pieces[:each]), (w_b, pieces[each:])):
                joined = jnp.concatenate([ref[c] for ref in held], axis=0)
                dh = dh + dot(joined, weight[c], TT)
        hat, inverse = normed_rows(tok_ref[...].astype(F32))
        e = dh * vec_ref[0:1, :]
        e_mean = jnp.mean(e, axis=-1, keepdims=True)
        eh_mean = jnp.mean(e * hat, axis=-1, keepdims=True)
        out = dmid_ref[...] + (e - e_mean - hat * eh_mean) * inverse
        sums = jnp.concatenate(
            [
                jnp.sum(dh, axis=0, keepdims=True),
                jnp.sum(dh * hat, axis=0, keepdims=True),
                jnp.zeros((6, features), F32),
            ],
            axis=0,
        )

        @pl.when(pl.program_id(0) == 0)
        def _():
            sum_ref[...] = sums

        @pl.when(pl.program_id(0) > 0)
        def _():
            sum_ref[...] += sums

        @pl.when(pl.program_id(0) < count // 2)
        def _():
            gone_ref[...] = out

        @pl.when(pl.program_id(0) >= count // 2)
        def _():
            kept_ref[0] = out

    whole = lambda i, n: (0, 0)
    tok = pl.BlockSpec((rows, features), lambda i, n: (place(i, n), 0))
    joined = pl.BlockSpec((3, part, rows), lambda i, n: (0, 0, place(i, n)))
    weight = pl.BlockSpec((3, features, width), lambda i, n: (0, 0, 0))
    return call(
        body,
        (count,),
        [joined] * len(pieces) + [weight, weight, tok, tok, pl.BlockSpec(vectors.shape, whole)],
        [
            pl.BlockSpec((rows, features), gone),
            pl.BlockSpec((1, rows, features), kept),
            pl.BlockSpec((8, features), whole),
        ],
        [
            shaped((span // 2, features), F32),
            shaped((2, span // 2, features), F32),
            shaped((8, features), F32),
        ],
        12 * span * features * width,
        prefetch=1,
        after=after,
    )(mine, *pieces, *weights, tokens, dmiddle, vectors)


def collect(sums_one, sums_two, dgate_two, bias_other, vectors):
    features = vectors.shape[1]

    def body(one_ref, two_ref, gate_ref, bias_ref, vec_ref, out_ref):
        def rounded(value):
            return value.astype(BF).astype(F32)

        one, two = one_ref[...], two_ref[...]
        out_ref[...] = jnp.concatenate(
            [
                one[1:2] * vec_ref[7:8, :],
                two[1:2] * vec_ref[8:9, :],
                two[3:4],
                rounded(one[0:1]),
                rounded(one[1:2] * vec_ref[9:10, :]),
                rounded(two[2:3]),
                rounded(two[0:1]),
                rounded(two[1:2] * vec_ref[10:11, :]),
                rounded(gate_ref[...]),
                vec_ref[11:12, :],
                bias_ref[:, :features],
                bias_ref[:, features:],
                jnp.zeros((4, features), F32),
            ],
            axis=0,
        )

    whole = lambda a: pl.BlockSpec(a.shape, lambda i: (0, 0))
    operands = (sums_one, sums_two, dgate_two, bias_other, vectors)
    out = shaped((16, features), F32)
    return call(body, (1,), [whole(a) for a in operands], [whole(out)], [out], 1000)(*operands)[0]


def chip_rows(mine, held, arrived, bias_own):
    features = held.shape[1]

    def body(mine_ref, held_ref, arrived_ref, bias_ref, out_ref):
        held, arrived = held_ref[...], arrived_ref[...]
        first = mine_ref[0] == 0
        low = jnp.where(first, held, arrived)
        high = jnp.where(first, arrived, held)
        sums = jnp.concatenate(
            [
                held[0:3] + arrived[0:3],
                bias_ref[:, :features] + arrived[10:11],
                bias_ref[:, features:] + arrived[11:12],
            ],
            axis=0,
        )
        top = sums.astype(BF).astype(F32)
        out_ref[...] = jnp.concatenate(
            [low[3:9], high[3:9], low[9:10], high[9:10], top, sums - top], axis=0
        ).astype(BF)

    whole = lambda a: pl.BlockSpec(a.shape, lambda i, n: (0, 0))
    operands = (held, arrived, bias_own)
    out = shaped((24, features), BF)
    return call(
        body, (1,), [whole(a) for a in operands], [whole(out)], [out], 1000, prefetch=1
    )(mine, *operands)[0]


def halving_steps(size):
    if size == 16:
        return [
            (1, lambda d: d & 1),
            (2, lambda d: (d >> 1) & 1),
            (4, lambda d: ((d >> 2) ^ (d >> 3)) & 1),
            (12, lambda d: (d >> 3) & 1),
        ]
    steps, mask = [], 1
    while mask < size:
        steps.append((mask, partial(lambda shift, d: (d >> shift) & 1, len(steps))))
        mask *= 2
    return steps


def fold(kept, arrived, bit, after=()):
    count = len(kept)

    def body(bit_ref, *refs):
        for at in range(count):
            kept_ref, arrived_ref, stay_ref, leave_ref = refs[at::count]
            total = kept_ref[...] + arrived_ref[...].astype(F32)

            @pl.when(pl.program_id(0) == 0)
            def _():
                leave_ref[...] = total.astype(BF)

            @pl.when(pl.program_id(0) == 1)
            def _():
                stay_ref[...] = total

    def place(at, i, n):
        return (jnp.where(i == 0, 1 - n[at], n[at]), 0)

    halves = [(a.shape[0] // 2, a.shape[1]) for a in kept]
    blocks = [pl.BlockSpec(half, partial(place, at)) for at, half in enumerate(halves)]
    fixed = [pl.BlockSpec(half, lambda i, n: (0, 0)) for half in halves]
    out = call(
        body,
        (2,),
        blocks * 2,
        fixed * 2,
        [shaped(half, F32) for half in halves] + [shaped(half, BF) for half in halves],
        sum(a.size for a in kept),
        prefetch=1,
        after=after,
    )(bit, *kept, *arrived)
    return out[:count], out[count:]


def fold_last(kept, arrived, after=()):
    count = len(kept)

    def body(*refs):
        for at in range(count):
            kept_ref, arrived_ref, out_ref = refs[at::count]
            out_ref[...] = (kept_ref[...].astype(F32) + arrived_ref[...].astype(F32)).astype(BF)

    whole = [pl.BlockSpec(a.shape, lambda i: (0, 0)) for a in kept]
    return call(
        body,
        (1,),
        whole * 2,
        whole,
        [shaped(a.shape, BF) for a in kept],
        sum(a.size for a in kept),
        after=after,
    )(*kept, *arrived)


def join(held, arrived, bit, out_type=BF, ways=(), after=()):
    count = len(held)
    ways = ways or ("above",) * count

    def body(bit_ref, *refs):
        for at in range(count):
            own = pl.program_id(0) == bit_ref[at]
            held_ref, arrived_ref, out_ref = refs[at::count]

            def lay(ref, at=at, out_ref=out_ref):
                value = ref[...].astype(out_type)
                out_ref[...] = value.T if ways[at] == "turned" else value

            pl.when(own)(partial(lay, held_ref))
            pl.when(jnp.logical_not(own))(partial(lay, arrived_ref))

    fixed = [pl.BlockSpec(a.shape, lambda i, n: (0, 0)) for a in held]
    blocks, shapes = [], []
    for a, way in zip(held, ways):
        rows, width = a.shape[::-1] if way == "turned" else a.shape
        if way == "above":
            blocks.append(pl.BlockSpec((rows, width), lambda i, n: (i, 0)))
            shapes.append(shaped((2 * rows, width), out_type))
        else:
            blocks.append(pl.BlockSpec((rows, width), lambda i, n: (0, i)))
            shapes.append(shaped((rows, 2 * width), out_type))
    return call(
        body,
        (2,),
        fixed * 2,
        blocks,
        shapes,
        sum(a.size for a in held),
        prefetch=1,
        after=after,
    )(bit, *held, *arrived)


HALVED = 3


class Halving:
    def __init__(self, dp_size, tensor_size, dp_index, tensor_index, orders):
        steps = halving_steps(dp_size)
        self.count = len(steps)
        self.pairs, bits = [], []
        for at in range(self.count):
            self.pairs.append([])
            bits.append([])
            for order in orders:
                chosen = [steps[order[t][at]] for t in range(tensor_size)]
                self.pairs[at].append(
                    [
                        (d * tensor_size + t, (d ^ chosen[t][0]) * tensor_size + t)
                        for d in range(dp_size)
                        for t in range(tensor_size)
                    ]
                )
                bit = chosen[0][1](dp_index)
                for t in range(1, tensor_size):
                    bit = jnp.where(tensor_index == t, chosen[t][1](dp_index), bit)
                bits[at].append(bit.astype(jnp.int32).reshape(1))
        self.single = bits
        self.bits = [jnp.concatenate(row) if len(row) > 1 else row[0] for row in bits]
        table = None
        for t, order in enumerate(orders[0]):
            places = np.zeros((dp_size, dp_size), np.float32)
            for d in range(dp_size):
                at = 0
                for step in order[:HALVED] + order[HALVED:][::-1]:
                    at = 2 * at + steps[step][1](d)
                places[d, at] = 1.0
            table = places if t == 0 else jnp.where(tensor_index == t, places, table)
        self.table = table
        self.at = 0
        self.payload = None

    def begin(self, *parts):
        self.kept, self.leaving = zip(*parts)
        return tuple(self.leaving)

    def exchange(self, place):
        if self.payload is not None:
            arrived = lax.ppermute(self.payload, ("dp", "tensor"), self.pairs[place][0])
            self.payload = jnp.where(
                self.single[place][0][0] == 0,
                jnp.concatenate([self.payload, arrived], axis=0),
                jnp.concatenate([arrived, self.payload], axis=0),
            )
        return [
            lax.ppermute(part, ("dp", "tensor"), pairs)
            for part, pairs in zip(self.leaving, self.pairs[place])
        ]

    def move(self, after=()):
        if self.at < HALVED:
            arrived = self.exchange(self.at)
            self.at += 1
            if self.at < HALVED:
                self.kept, self.leaving = fold(self.kept, arrived, self.bits[self.at], after)
            else:
                self.leaving = fold_last(self.kept, arrived, after)
        elif self.at < self.count:
            arrived = self.exchange(self.at)
            self.at += 1
            self.leaving = fold_last(self.leaving, arrived, after)
        else:
            place = self.count + HALVED - 1 - self.at
            arrived = self.exchange(place)
            self.at += 1
            self.leaving = join(self.leaving, arrived, self.bits[place], after=after)
        return tuple(self.leaving)

    def last(self):
        self.arrived = self.exchange(0)
        return tuple(self.arrived)

    def finish(self, ways=(), after=()):
        return join(self.leaving, self.arrived, self.bits[0], F32, ways, after)

    def spread(self, value):
        self.payload = value[None]

    def spreaded(self):
        flat = self.payload.reshape(self.payload.shape[0], -1)
        return dot(jnp.asarray(self.table).astype(BF), flat, NN).astype(BF)


def per_device(
    dp_size,
    tensor_size,
    tokens,
    condition,
    lengths,
    modulation_weight,
    modulation_bias,
    first_gain,
    query_key_value_weight,
    attention_out_weight,
    second_gain,
    up_projection_weight,
    upward_bias,
    down_projection_weight,
    downward_bias,
    cotangent,
):
    sequences, span, features = tokens.shape
    hidden = up_projection_weight.shape[1]
    width = attention_out_weight.shape[0]
    dp_index = lax.axis_index("dp")
    mine = lax.axis_index("tensor")
    swap = [(0, 1), (1, 0)]

    def from_sibling(value):
        return lax.ppermute(value, "tensor", swap)

    def ordered(own, other, axis):
        return jnp.where(
            mine == 0,
            jnp.concatenate([own, other], axis=axis),
            jnp.concatenate([other, own], axis=axis),
        )

    qkv_own = query_key_value_weight.transpose(1, 0, 2)
    qkv_weights = (qkv_own, from_sibling(qkv_own))
    out_weights = (attention_out_weight, from_sibling(attention_out_weight))
    up_weights = (up_projection_weight, from_sibling(up_projection_weight))
    up_biases = (upward_bias[None], from_sibling(upward_bias)[None])
    down_weights = (down_projection_weight, from_sibling(down_projection_weight))
    gone = lax.dynamic_index_in_dim(cotangent, 1 - mine, 0, keepdims=False)
    kept = lax.dynamic_index_in_dim(cotangent, mine, 0, keepdims=False)
    upstream = ordered(kept, from_sibling(gone), 0)
    rows = lax.dynamic_index_in_dim(tokens, mine, 0, keepdims=False)
    length = lax.dynamic_slice_in_dim(lengths, mine, 1, 0)

    cond_float = condition.astype(F32)
    silu_values, silu_pull = jax.vjp(jax.nn.silu, cond_float)
    silu_cond = silu_values.astype(BF)
    mods = dot(silu_cond, modulation_weight, NN) + modulation_bias
    mods = lax.dynamic_index_in_dim(mods, mine, 0, keepdims=False).reshape(6, features)
    shift_one, scale_one, gate_one, shift_two, scale_two, gate_two = mods
    silu_row = lax.dynamic_index_in_dim(silu_cond, mine, 0, keepdims=False).astype(F32)
    vectors = jnp.stack(
        [
            first_gain * (1.0 + scale_one),
            shift_one,
            gate_one,
            second_gain * (1.0 + scale_two),
            shift_two,
            gate_two,
            downward_bias,
            1.0 + scale_one,
            1.0 + scale_two,
            first_gain,
            second_gain,
            jnp.pad(silu_row, (0, features - silu_row.shape[0])),
        ]
        + [jnp.zeros((features,), F32)] * 4
    )
    cosine, sine = (jnp.asarray(table) for table in rotary_tables(span))

    leading, joined = project(rows, qkv_weights, vectors, cosine, sine)
    attended, totals = attend(length, joined)
    (
        branch_one, trailing, dbranch, act_own, act_other, dupper_own, dupper_other,
        dmiddle, dbranch_one, dattended, sums_two, gb_own, gb_other,
    ) = middle(
        attended, rows, upstream, out_weights, up_weights, down_weights, up_biases, vectors
    )
    halving = dp_size == 16
    orders = ((0, 1, 2, 3), (1, 0, 2, 3))

    def job(parts):
        return Halving(dp_size, tensor_size, dp_index, mine, (orders,) * parts) if halving else None

    def advance(work, *after):
        return work.move(after) if halving else ()

    def back(piece, after):
        return attend_back(
            length, joined, attended, dattended, totals, cosine, sine, piece, after=after
        )

    sum_down, sum_up, sum_input = job(1), job(2), job(1)
    gd_other = weight_grad(act_other, dbranch, BF)
    gu_other = weight_grad(dupper_other, trailing, BF, after=(gd_other,))
    go_other = out_grad(attended, dbranch_one, 1, BF, after=(gu_other,))
    gd_other, gu_other, go_other = (from_sibling(value) for value in (gd_other, gu_other, go_other))
    count = width // (2 * HEAD)
    backs = [None] * (2 * count)
    other, own = list(range(count, 2 * count)), list(range(count))
    if halving:
        sent = sum_down.begin(weight_grad(act_own, dbranch, F32, gd_other, sum_down.single[0][0]))
        for piece in other[:-1]:
            backs[piece] = back(piece, sent)
            sent = (backs[piece],)
        sent = advance(sum_down, *sent)
        bits = sum_up.single[0]
        up_parts = weight_grad(dupper_own, trailing, F32, gu_other, bits[0], after=sent)
        out_parts = out_grad(attended, dbranch_one, 0, F32, go_other, bits[1], after=up_parts[1:])
        sent = sum_up.begin(up_parts, out_parts)
        sent = sent + advance(sum_down, out_parts[1])
    else:
        grad_downward_weight = lax.psum(weight_grad(act_own, dbranch, F32, gd_other), "dp")
        grad_upward_weight = lax.psum(weight_grad(dupper_own, trailing, F32, gu_other), "dp").T
        both = lax.psum(out_grad(attended, dbranch_one, 0, F32, go_other), "dp")
        grad_output_weight = jnp.concatenate([both[:width], both[width:]], axis=1)
        sent = ()
        for piece in other[:-1]:
            backs[piece] = back(piece, sent)

    piece = other[-1]
    backs[piece] = back(piece, sent)
    sent = (backs[piece],) + advance(sum_down, backs[piece])
    product = project_weight_back(leading, backs[count:], BF, after=sent)
    gq_other = from_sibling(product)
    sent = (product,) + advance(sum_up, product)
    plan = [(sum_down,), (sum_up, sum_down), (sum_up, sum_down)]
    for place, piece in enumerate(own):
        backs[piece] = back(piece, sent)
        sent = (backs[piece],)
        for work in plan[place % len(plan)]:
            sent = sent + advance(work, backs[piece])
    if halving:
        parts = project_weight_back(
            leading, backs[:count], F32, gq_other, sum_input.single[0][0], after=sent
        )
        sent = sum_input.begin(parts)
    else:
        grad_input_weight = lax.psum(project_weight_back(leading, backs[:count], F32, gq_other), "dp")
    which = mine.astype(jnp.int32).reshape(1)
    gone_tokens, grad_tokens, sums_one = project_back(
        which, backs, qkv_weights, rows, dmiddle, vectors, after=sent
    )
    sent = advance(sum_input, gone_tokens) + advance(sum_up, gone_tokens)
    if halving:
        sent = sent + sum_down.last()
    gone_output, output, dgate_two = finish_forward(
        which, (act_own, act_other), down_weights, branch_one, rows, upstream, vectors, after=sent
    )
    sent = advance(sum_input, gone_output) + advance(sum_up, gone_output)

    grad_tokens = lax.dynamic_update_index_in_dim(
        grad_tokens, from_sibling(gone_tokens), 1 - mine, 0
    )
    output = lax.dynamic_update_index_in_dim(output, from_sibling(gone_output), 1 - mine, 0)

    held = collect(sums_one, sums_two, dgate_two, gb_other, vectors)
    chip = chip_rows(which, held, from_sibling(held), gb_own)
    wide, six = 6 * features, 6 * sequences
    sums_at, sums_count = six + sequences, 3 + hidden // features
    pair = chip[:six].reshape(sequences, wide)
    grad_condition = silu_pull(dot(pair, modulation_weight, NT))[0]
    if halving:
        (grad_downward_weight,) = sum_down.finish(after=sent)
        sent = advance(sum_input, grad_downward_weight) + advance(sum_up, grad_downward_weight)
        sum_input.spread(chip)
        sum_up.last()
        sent = advance(sum_input, *sent)
        sent = advance(sum_input, grad_tokens, output)
        grad_upward_weight, grad_output_weight = sum_up.finish(("turned", "beside"), after=sent)
        advance(sum_input, grad_upward_weight)
        sum_input.last()
        (grad_input_weight,) = sum_input.finish()
        gathered = sum_input.spreaded().reshape(dp_size, chip.shape[0], features)
    else:
        gathered = lax.all_gather(chip, "dp", axis=0)
    dmods_low = gathered[:, :six].reshape(-1, wide)
    everyone = gathered[:, six:sums_at, : silu_row.shape[0]].reshape(-1, silu_row.shape[0])
    sums = gathered[:, sums_at : sums_at + sums_count].astype(F32)
    sums = jnp.sum(sums + gathered[:, sums_at + sums_count :].astype(F32), axis=0)
    grad_input_weight = grad_input_weight.reshape(3, features, width).transpose(1, 0, 2)
    grad_modulation_bias = jnp.sum(dmods_low, axis=0, dtype=F32)
    grad_modulation_weight = dot(everyone, dmods_low, TN)
    grad_first_gain, grad_second_gain, grad_downward_bias = sums[0], sums[1], sums[2]
    grad_upward_bias = sums[3:].reshape(hidden)
    return (
        output,
        grad_tokens,
        grad_condition,
        grad_modulation_weight,
        grad_modulation_bias,
        grad_first_gain,
        grad_input_weight,
        grad_output_weight,
        grad_second_gain,
        grad_upward_weight,
        grad_upward_bias,
        grad_downward_weight,
        grad_downward_bias,
    )


def solution(mesh):
    placed = (
        P("dp", None, None),
        P("dp", None),
        P("dp"),
        P(),
        P(),
        P(),
        P(None, None, "tensor"),
        P("tensor", None),
        P(),
        P(None, "tensor"),
        P("tensor"),
        P("tensor", None),
        P(),
        P("dp", "tensor", None),
    )
    return jax.shard_map(
        partial(per_device, mesh.shape["dp"], mesh.shape["tensor"]),
        mesh=mesh,
        in_specs=placed,
        out_specs=(
            P("dp", "tensor", None),
            P("dp", "tensor", None),
            P("dp", None),
            P(),
            P(),
            P(),
            P(None, None, "tensor"),
            P("tensor", None),
            P(),
            P(None, "tensor"),
            P("tensor"),
            P("tensor", None),
            P(),
        ),
        check_vma=False,
    )
```

```python
import math
from functools import partial

import jax
import jax.numpy as jnp
import numpy as np
from jax import lax
from jax.experimental import pallas as pl
from jax.experimental.pallas import tpu as pltpu
from jax.sharding import PartitionSpec as P

HEAD = 64
HALF = HEAD // 2
EPS = 1e-05
LOG2_SCALE = math.log2(math.e) * HEAD ** (-0.5)
SAFE_BOUND = 70.0
GELU_A = math.sqrt(2.0 / math.pi)
GELU_B = 0.044715
BF = jnp.bfloat16
F32 = jnp.float32

NN = (((1,), (0,)), ((), ()))
NT = (((1,), (1,)), ((), ()))
TN = (((0,), (0,)), ((), ()))
TT = (((0,), (1,)), ((), ()))
dot = partial(lax.dot_general, preferred_element_type=F32)


def call(body, grid, in_specs, out_specs, out_shape, flops, scratch=(), prefetch=0, spare=8, after=()):
    known = prefetch + len(in_specs)

    def with_after(*refs):
        return body(*refs[:known], *refs[known + len(after) :])

    def run(*operands):
        held = 0
        for spec, array in zip(
            list(in_specs) + list(out_specs), list(operands[prefetch:]) + list(out_shape)
        ):
            size = math.prod(spec.block_shape) * array.dtype.itemsize
            held += size if spec.pipeline_mode is not None else 2 * size
        moved = sum(a.size * a.dtype.itemsize for a in operands)
        moved += sum(math.prod(a.shape) * a.dtype.itemsize for a in out_shape)
        return pl.pallas_call(
            with_after if after else body,
            grid_spec=pltpu.PrefetchScalarGridSpec(
                num_scalar_prefetch=prefetch,
                grid=grid,
                in_specs=list(in_specs) + [pl.BlockSpec(memory_space=pl.ANY)] * len(after),
                out_specs=out_specs,
                scratch_shapes=list(scratch),
            ),
            out_shape=out_shape,
            compiler_params=pltpu.CompilerParams(
                vmem_limit_bytes=min(held + spare * 2**20, 60 * 2**20)
            ),
            cost_estimate=pl.CostEstimate(
                flops=int(flops), bytes_accessed=int(moved), transcendentals=0
            ),
        )(*operands, *after)

    return run


def shaped(shape, dtype):
    return jax.ShapeDtypeStruct(shape, dtype)


def rotary_tables(span):
    frequency = (
        np.float32(10000.0) ** (-(np.arange(HALF, dtype=np.float32) * np.float32(2.0 / HEAD)))
    ).astype(np.float32)
    angles = (np.arange(span, dtype=np.float32)[None, :] * frequency[:, None]).astype(np.float32)
    angles = angles.astype(np.float64)
    return np.cos(angles).astype(np.float32), np.sin(angles).astype(np.float32)


def normed_rows(rows):
    centre = jnp.mean(rows, axis=-1, keepdims=True)
    centred = rows - centre
    spread = jnp.mean(centred * centred, axis=-1, keepdims=True)
    inverse = lax.rsqrt(spread + EPS)
    return centred * inverse, inverse


def project(source, weights, vectors, cosine, sine):
    span, features = source.shape
    width = weights[0].shape[2]

    def body(source_ref, own_ref, other_ref, vector_ref, cos_ref, sin_ref, rows_ref, out_ref):
        step = pl.program_id(0)

        @pl.when(step == 0)
        def _():
            for start in range(0, span, 128):
                hat, _ = normed_rows(source_ref[start : start + 128, :].astype(F32))
                rows_ref[start : start + 128, :] = (
                    hat * vector_ref[0:1, :] + vector_ref[1:2, :]
                ).astype(BF)

        def emit(weight_ref):
            joined = dot(weight_ref[0], rows_ref[...], TT)

            @pl.when(step % 3 < 2)
            def _():
                cos, sin = cos_ref[...], sin_ref[...]
                for at in range(0, width, HEAD):
                    low, high = joined[at : at + HALF], joined[at + HALF : at + HEAD]
                    out_ref[0, at : at + HALF, :] = (low * cos - high * sin).astype(BF)
                    out_ref[0, at + HALF : at + HEAD, :] = (high * cos + low * sin).astype(BF)

            @pl.when(step % 3 == 2)
            def _():
                out_ref[0] = joined.astype(BF)

        @pl.when(step < 3)
        def _():
            emit(own_ref)

        @pl.when(step >= 3)
        def _():
            emit(other_ref)

    whole = lambda i: (0, 0)
    return call(
        body,
        (6,),
        [
            pl.BlockSpec((span, features), whole),
            pl.BlockSpec((1, features, width), lambda i: (jnp.minimum(i, 2), 0, 0)),
            pl.BlockSpec((1, features, width), lambda i: (jnp.maximum(i - 3, 0), 0, 0)),
            pl.BlockSpec(vectors.shape, whole),
            pl.BlockSpec(cosine.shape, whole),
            pl.BlockSpec(sine.shape, whole),
        ],
        [
            pl.BlockSpec((span, features), whole),
            pl.BlockSpec((1, width, span), lambda i: (i % 3, i // 3, 0)),
        ],
        [shaped((span, features), BF), shaped((3, 2 * width, span), BF)],
        12 * span * features * width,
    )(source, *weights, vectors, cosine, sine)


def live_lengths(span):
    return (span, span // 2, span // 8)


def attend(length, joined):
    _, width, span = joined.shape
    per_step = 2
    query_block = min(512, span)

    def one_length(live, query_ref, key_ref, value_ref, out_ref, total_ref):
        key_block = min(512, live)
        largest = 0.0
        for head in range(per_step):
            at = slice(head * HEAD, (head + 1) * HEAD)
            query_size = jnp.sum(jnp.square(query_ref[0, at, :].astype(F32)), axis=0)
            key_size = jnp.sum(jnp.square(key_ref[0, at, :live].astype(F32)), axis=0)
            largest = jnp.maximum(largest, jnp.max(query_size) * jnp.max(key_size))
        safe = largest < (SAFE_BOUND / HEAD ** (-0.5)) ** 2

        @pl.when(safe)
        def _():
            for head in range(per_step):
                at = slice(head * HEAD, (head + 1) * HEAD)
                keys = key_ref[0, at, :live].T
                for first in range(0, span, query_block):
                    columns = slice(first, first + query_block)
                    queries = query_ref[0, at, columns]
                    result = jnp.zeros((HEAD, query_block), F32)
                    total = jnp.zeros((1, query_block), F32)
                    for start in range(0, live, key_block):
                        rows = slice(start, start + key_block)
                        probs = jnp.exp2(dot(keys[rows], queries, NN) * LOG2_SCALE)
                        total = total + jnp.sum(probs, axis=0, keepdims=True)
                        result = result + dot(value_ref[0, at, rows], probs.astype(BF), NN)
                    out_ref[at, columns] = (result * (1.0 / total)).astype(BF)
                    total_ref[0, head : head + 1, columns] = jnp.log2(total)

        @pl.when(jnp.logical_not(safe))
        def _():
            for head in range(per_step):
                at = slice(head * HEAD, (head + 1) * HEAD)
                keys = key_ref[0, at, :live].T
                for first in range(0, span, query_block):
                    columns = slice(first, first + query_block)
                    scores = dot(keys, query_ref[0, at, columns], NN) * LOG2_SCALE
                    highest = jnp.max(scores, axis=0, keepdims=True)
                    probs = jnp.exp2(scores - highest)
                    total = jnp.sum(probs, axis=0, keepdims=True)
                    result = dot(value_ref[0, at, :live], probs.astype(BF), NN)
                    out_ref[at, columns] = (result * (1.0 / total)).astype(BF)
                    total_ref[0, head : head + 1, columns] = highest + jnp.log2(total)

    def body(length_ref, query_ref, key_ref, value_ref, out_ref, total_ref):
        for live in live_lengths(span):

            @pl.when(length_ref[0] == live)
            def _():
                one_length(live, query_ref, key_ref, value_ref, out_ref, total_ref)

    rows = per_step * HEAD

    def part(c):
        return pl.BlockSpec((1, rows, span), lambda i, n: (c, i, 0))

    return call(
        body,
        (width // rows,),
        [part(0), part(1), part(2)],
        [
            pl.BlockSpec((rows, span), lambda i, n: (i, 0)),
            pl.BlockSpec((1, per_step, span), lambda i, n: (i, 0, 0)),
        ],
        [shaped((width, span), BF), shaped((width // rows, per_step, span), F32)],
        16 * span * span * width,
        prefetch=1,
    )(length, joined, joined, joined)


def attend_back(length, joined, attended, dattended, totals, cosine, sine, piece, after=()):
    _, width, span = joined.shape
    per_step = 2
    key_block_most = 256

    def turned(grads, cos, sin, out_ref, part, head, columns):
        low, high = grads[:HALF], grads[HALF:]
        top = head * HEAD
        out_ref[part, top : top + HALF, columns] = (low * cos + high * sin).astype(BF)
        out_ref[part, top + HALF : top + HEAD, columns] = (high * cos - low * sin).astype(BF)

    def one_length(live, query_ref, key_ref, value_ref, out_ref, dout_ref, total_ref, cos_ref, sin_ref, grad_ref):
        key_block = min(key_block_most, live)
        for head in range(per_step):
            at = slice(head * HEAD, (head + 1) * HEAD)
            keys = key_ref[0, at, :live].T
            values = value_ref[0, at, :live].T
            queries = query_ref[0, at, :]
            dout = dout_ref[at, :]
            weighted = jnp.sum(
                dout.astype(F32) * out_ref[at, :].astype(F32), axis=0, keepdims=True
            )
            totals = total_ref[0, head : head + 1, :]
            dquery = jnp.zeros((HEAD, span), F32)
            for start in range(0, live, key_block):
                rows = slice(start, start + key_block)
                probs = jnp.exp2(dot(keys[rows], queries, NN) * LOG2_SCALE - totals)
                dprobs = dot(values[rows], dout, NN)
                dscores = (probs * (dprobs - weighted)).astype(BF)
                dvalue = dot(dout, probs.astype(BF), NT)
                dkey = dot(queries, dscores, NT) * HEAD ** (-0.5)
                dquery = dquery + dot(key_ref[0, at, rows], dscores, NN)
                turned(dkey, cos_ref[:, rows], sin_ref[:, rows], grad_ref, 1, head, rows)
                grad_ref[2, at, rows] = dvalue.astype(BF)
            turned(dquery * HEAD ** (-0.5), cos_ref[...], sin_ref[...], grad_ref, 0, head, slice(0, span))
        if live < span:
            empty = jnp.zeros((per_step * HEAD, span - live), BF)
            grad_ref[1, :, live:] = empty
            grad_ref[2, :, live:] = empty

    def body(length_ref, *refs):
        for live in live_lengths(span):

            @pl.when(length_ref[0] == live)
            def _():
                one_length(live, *refs)

    rows = per_step * HEAD

    def part(c):
        return pl.BlockSpec((1, rows, span), lambda i, n: (c, piece, 0))

    flat = pl.BlockSpec((rows, span), lambda i, n: (piece, 0))
    table = pl.BlockSpec((HALF, span), lambda i, n: (0, 0))
    return call(
        body,
        (1,),
        [part(0), part(1), part(2), flat, flat, pl.BlockSpec((1, per_step, span), lambda i, n: (piece, 0, 0)), table, table],
        [pl.BlockSpec((3, rows, span), lambda i, n: (0, 0, 0))],
        [shaped((3, rows, span), BF)],
        40 * span * span * rows,
        prefetch=1,
        after=after,
    )(length, joined, joined, joined, attended, dattended, totals, cosine, sine)[0]


def middle(attended, tokens, upstream, outs, ups, downs, biases, vectors):
    features = tokens.shape[1]
    width, span = attended.shape
    part = outs[0].shape[0]
    hidden = ups[0].shape[1]
    rows = 512
    columns_each = 256

    def body(att_ref, tok_ref, g_ref, out_a, out_b, up_a, up_b, down_a, down_b, bias_a, bias_b, vec_ref,
             branch_ref, h_ref, db_two, act_a, act_b, du_a, du_b, dmid_ref, db_one, datt_ref, sum_ref, gb_a, gb_b):
        @pl.when(pl.program_id(0) == 0)
        def _():
            sum_ref[...] = jnp.zeros_like(sum_ref)
            gb_a[...] = jnp.zeros_like(gb_a)
            gb_b[...] = jnp.zeros_like(gb_b)

        branch = dot(att_ref[:part], out_a[...], TN) + dot(att_ref[part:], out_b[...], TN)
        branch_ref[...] = branch
        gate = vec_ref[2:3, :]
        hat, inverse = normed_rows(tok_ref[...].astype(F32) + gate * branch)
        h = (hat * vec_ref[3:4, :] + vec_ref[4:5, :]).astype(BF)
        h_ref[...] = h
        g = g_ref[...].astype(F32)
        db = (vec_ref[5:6, :] * g).astype(BF)
        db_two[...] = db
        for up, down, bias, act, du_ref, gb in (
            (up_a, down_a, bias_a, act_a, du_a, gb_a),
            (up_b, down_b, bias_b, act_b, du_b, gb_b),
        ):
            for at in range(0, hidden, columns_each):
                columns = slice(at, at + columns_each)
                upper = dot(h, up[:, columns], NN) + bias[0:1, columns]
                dact = dot(db, down[columns, :], NT)
                inner = GELU_A + (GELU_A * GELU_B) * (upper * upper)
                tanh = jnp.tanh(upper * inner)
                lean = 0.5 + 0.5 * tanh
                value = upper * lean
                act[:, columns] = value.astype(BF)
                slope = lean + value * (1.0 - tanh) * (3.0 * inner - 2.0 * GELU_A)
                du = (dact * slope).astype(BF)
                du_ref[:, columns] = du
                gb[0:1, columns] += jnp.sum(du.astype(F32), axis=0, keepdims=True)
        dh = dot(du_a[...], up_a[...], NT) + dot(du_b[...], up_b[...], NT)
        e = dh * vec_ref[3:4, :]
        e_mean = jnp.mean(e, axis=-1, keepdims=True)
        eh_mean = jnp.mean(e * hat, axis=-1, keepdims=True)
        dmid = g + (e - e_mean - hat * eh_mean) * inverse
        dmid_ref[...] = dmid
        db = (gate * dmid).astype(BF)
        db_one[...] = db
        datt_ref[:part] = dot(out_a[...], db, NT).astype(BF)
        datt_ref[part:] = dot(out_b[...], db, NT).astype(BF)
        sum_ref[0:1, :] += jnp.sum(dh, axis=0, keepdims=True)
        sum_ref[1:2, :] += jnp.sum(dh * hat, axis=0, keepdims=True)
        sum_ref[2:3, :] += jnp.sum(dmid * branch_ref[...], axis=0, keepdims=True)
        sum_ref[3:4, :] += jnp.sum(db_two[...].astype(F32), axis=0, keepdims=True)

    whole = lambda i: (0, 0)
    tok = pl.BlockSpec((rows, features), lambda i: (i, 0))
    wide = pl.BlockSpec((rows, hidden), lambda i: (i, 0))
    att = pl.BlockSpec((width, rows), lambda i: (0, i))
    fixed = lambda a: pl.BlockSpec(a.shape, whole, pipeline_mode=pl.Buffered(1))
    sums = pl.BlockSpec((1, hidden), whole)
    return call(
        body,
        (span // rows,),
        [att, tok, tok] + [fixed(a) for a in (*outs, *ups, *downs, *biases, vectors)],
        [tok, tok, tok, wide, wide, wide, wide, tok, tok, att, pl.BlockSpec((8, features), whole), sums, sums],
        [
            shaped((span, features), F32),
            shaped((span, features), BF),
            shaped((span, features), BF),
            *[shaped((span, hidden), BF)] * 4,
            shaped((span, features), F32),
            shaped((span, features), BF),
            shaped((width, span), BF),
            shaped((8, features), F32),
            shaped((1, hidden), F32),
            shaped((1, hidden), F32),
        ],
        4 * span * features * width + 12 * span * features * hidden,
    )(attended, tokens, upstream, *outs, *ups, *downs, *biases, vectors)


def weight_grad(left, right, out_type, received=None, bit=None, after=()):
    span, height = left.shape
    features = right.shape[1]
    block = height // 2
    count = height // block
    half = count // 2
    flops = 2 * span * height * features
    fixed = pl.BlockSpec(right.shape, lambda i, *n: (0, 0))
    if bit is None:

        def body(left_ref, right_ref, *rest):
            product = dot(left_ref[...], right_ref[...], TN)
            if received is not None:
                product = product + rest[0][...].astype(F32)
            rest[-1][...] = product.astype(out_type)

        row = pl.BlockSpec((block, features), lambda i: (i, 0))
        more = () if received is None else (received,)
        return call(
            body,
            (count,),
            [pl.BlockSpec((span, block), lambda i: (0, i)), fixed] + [row] * len(more),
            [row],
            [shaped((height, features), out_type)],
            flops,
            after=after,
        )(left, right, *more)[0]

    def body(bit_ref, left_ref, right_ref, received_ref, kept_ref, leaving_ref):
        product = dot(left_ref[...], right_ref[...], TN) + received_ref[...].astype(F32)

        @pl.when(pl.program_id(0) < half)
        def _():
            leaving_ref[...] = product.astype(BF)

        @pl.when(pl.program_id(0) >= half)
        def _():
            kept_ref[...] = product

    def place(i, n):
        return jnp.where(i < half, (1 - n[0]) * half + i, n[0] * half + i - half)

    return call(
        body,
        (count,),
        [
            pl.BlockSpec((span, block), lambda i, n: (0, place(i, n))),
            fixed,
            pl.BlockSpec((block, features), lambda i, n: (place(i, n), 0)),
        ],
        [
            pl.BlockSpec((block, features), lambda i, n: (jnp.maximum(i - half, 0), 0)),
            pl.BlockSpec((block, features), lambda i, n: (jnp.minimum(i, half - 1), 0)),
        ],
        [shaped((height // 2, features), F32), shaped((height // 2, features), BF)],
        flops,
        prefetch=1,
        after=after,
    )(bit, left, right, received)


def out_grad(attended, dbranch, which, out_type, received=None, bit=None, after=()):
    width, span = attended.shape
    features = dbranch.shape[1]
    height, block = width // 2, features // 2
    flops = 2 * span * height * features

    def product_of(att_ref, db_ref, received_ref):
        product = dot(att_ref[...], db_ref[...], NN)
        return product if received is None else product + received_ref[...].astype(F32)

    if bit is None:

        def body(att_ref, db_ref, *rest):
            rest[-1][...] = product_of(att_ref, db_ref, rest[0]).astype(out_type)

        part = pl.BlockSpec((height, block), lambda i: (i, 0))
        more = () if received is None else (received,)
        return call(
            body,
            (2,),
            [
                pl.BlockSpec((height, span), lambda i: (which, 0)),
                pl.BlockSpec((span, block), lambda i: (0, i)),
            ]
            + [part] * len(more),
            [part],
            [shaped((2 * height, block), out_type)],
            flops,
            after=after,
        )(attended, dbranch, *more)[0]

    def body(bit_ref, att_ref, db_ref, received_ref, kept_ref, leaving_ref):
        product = product_of(att_ref, db_ref, received_ref)

        @pl.when(pl.program_id(0) == 0)
        def _():
            leaving_ref[...] = product.astype(BF)

        @pl.when(pl.program_id(0) == 1)
        def _():
            kept_ref[...] = product

    def place(i, n):
        return jnp.where(i == 0, 1 - n[0], n[0])

    half = pl.BlockSpec((height, block), lambda i, n: (0, 0))
    return call(
        body,
        (2,),
        [
            pl.BlockSpec((height, span), lambda i, n: (which, 0)),
            pl.BlockSpec((span, block), lambda i, n: (0, place(i, n))),
            pl.BlockSpec((height, block), lambda i, n: (place(i, n), 0)),
        ],
        [half, half],
        [shaped((height, block), F32), shaped((height, block), BF)],
        flops,
        prefetch=1,
        after=after,
    )(bit, attended, dbranch, received)


def sent_first(blocks):
    half = blocks // 2

    def place(i, n):
        return jnp.where(i < half, (1 - n[0]) * half + i, n[0] * half + i - half)

    def gone(i, n):
        return (jnp.minimum(i, half - 1), 0)

    def kept(i, n):
        return (n[0], jnp.maximum(i - half, 0), 0)

    return place, gone, kept


def finish_forward(mine, acts, downs, branch, tokens, upstream, vectors, after=()):
    span, hidden = acts[0].shape
    features = tokens.shape[1]
    rows = 256
    count = span // rows
    place, gone, kept = sent_first(count)

    def body(mine_ref, act_a, act_b, down_a, down_b, branch_ref, tok_ref, g_ref, vec_ref, gone_ref, kept_ref, sum_ref):
        second = dot(act_a[...], down_a[...], NN) + dot(act_b[...], down_b[...], NN) + vec_ref[6:7, :]
        middle = tok_ref[...].astype(F32) + vec_ref[2:3, :] * branch_ref[...]
        out = (middle + vec_ref[5:6, :] * second).astype(BF)
        sums = jnp.sum(g_ref[...].astype(F32) * second, axis=0, keepdims=True)

        @pl.when(pl.program_id(0) == 0)
        def _():
            sum_ref[...] = sums

        @pl.when(pl.program_id(0) > 0)
        def _():
            sum_ref[...] += sums

        @pl.when(pl.program_id(0) < count // 2)
        def _():
            gone_ref[...] = out

        @pl.when(pl.program_id(0) >= count // 2)
        def _():
            kept_ref[0] = out

    whole = lambda i, n: (0, 0)
    tok = pl.BlockSpec((rows, features), lambda i, n: (place(i, n), 0))
    wide = pl.BlockSpec((rows, hidden), lambda i, n: (place(i, n), 0))
    fixed = lambda a: pl.BlockSpec(a.shape, whole)
    return call(
        body,
        (count,),
        [wide, wide] + [fixed(a) for a in downs] + [tok, tok, tok, fixed(vectors)],
        [
            pl.BlockSpec((rows, features), gone),
            pl.BlockSpec((1, rows, features), kept),
            pl.BlockSpec((1, features), whole),
        ],
        [
            shaped((span // 2, features), BF),
            shaped((2, span // 2, features), BF),
            shaped((1, features), F32),
        ],
        4 * span * features * hidden,
        prefetch=1,
        after=after,
    )(mine, *acts, *downs, branch, tokens, upstream, vectors)


def project_weight_back(h, pieces, out_type, received=None, bit=None, after=()):
    span, features = h.shape
    _, rows, _ = pieces[0].shape
    width = rows * len(pieces)
    block = features // 2
    flops = 6 * span * features * width
    if bit is None:

        def body(h_ref, *refs):
            joined = jnp.concatenate([ref[0] for ref in refs[: len(pieces)]], axis=0)
            product = dot(h_ref[...], joined, TT)
            if received is not None:
                product = product + refs[-2][...].astype(F32)
            refs[-1][...] = product.astype(out_type)

        row = pl.BlockSpec((features, width), lambda c: (c, 0))
        more = () if received is None else (received,)
        return call(
            body,
            (3,),
            [pl.BlockSpec((span, features), lambda c: (0, 0))]
            + [pl.BlockSpec((1, rows, span), lambda c: (c, 0, 0))] * len(pieces)
            + [row] * len(more),
            [row],
            [shaped((3 * features, width), out_type)],
            flops,
            after=after,
        )(h, *pieces, *more)[0]

    def body(bit_ref, h_ref, *refs):
        joined = jnp.concatenate([ref[0] for ref in refs[: len(pieces)]], axis=0)
        received_ref, kept_ref, leaving_ref = refs[len(pieces) :]
        product = dot(h_ref[...], joined, TT) + received_ref[...].astype(F32)

        @pl.when(pl.program_id(0) < 3)
        def _():
            leaving_ref[...] = product.astype(BF)

        @pl.when(pl.program_id(0) >= 3)
        def _():
            kept_ref[...] = product

    def place(i, n):
        return jnp.where(i < 3, (1 - n[0]) * 3 + i, n[0] * 3 + i - 3)

    return call(
        body,
        (6,),
        [pl.BlockSpec((span, block), lambda i, n: (0, place(i, n) % 2))]
        + [pl.BlockSpec((1, rows, span), lambda i, n: (place(i, n) // 2, 0, 0))] * len(pieces)
        + [pl.BlockSpec((block, width), lambda i, n: (place(i, n), 0))],
        [
            pl.BlockSpec((block, width), lambda i, n: (jnp.maximum(i - 3, 0), 0)),
            pl.BlockSpec((block, width), lambda i, n: (jnp.minimum(i, 2), 0)),
        ],
        [shaped((3 * block, width), F32), shaped((3 * block, width), BF)],
        flops,
        prefetch=1,
        after=after,
    )(bit, h, *pieces, received)


def project_back(mine, pieces, weights, tokens, dmiddle, vectors, after=()):
    _, part, span = pieces[0].shape
    features = tokens.shape[1]
    width = weights[0].shape[2]
    rows = 256
    count = span // rows
    each = len(pieces) // 2
    place, gone, kept = sent_first(count)

    def body(mine_ref, *refs):
        pieces, rest = refs[: 2 * each], refs[2 * each :]
        w_a, w_b, tok_ref, dmid_ref, vec_ref, gone_ref, kept_ref, sum_ref = rest
        dh = jnp.zeros((rows, features), F32)
        for c in range(3):
            for weight, held in ((w_a, pieces[:each]), (w_b, pieces[each:])):
                joined = jnp.concatenate([ref[c] for ref in held], axis=0)
                dh = dh + dot(joined, weight[c], TT)
        hat, inverse = normed_rows(tok_ref[...].astype(F32))
        e = dh * vec_ref[0:1, :]
        e_mean = jnp.mean(e, axis=-1, keepdims=True)
        eh_mean = jnp.mean(e * hat, axis=-1, keepdims=True)
        out = dmid_ref[...] + (e - e_mean - hat * eh_mean) * inverse
        sums = jnp.concatenate(
            [
                jnp.sum(dh, axis=0, keepdims=True),
                jnp.sum(dh * hat, axis=0, keepdims=True),
                jnp.zeros((6, features), F32),
            ],
            axis=0,
        )

        @pl.when(pl.program_id(0) == 0)
        def _():
            sum_ref[...] = sums

        @pl.when(pl.program_id(0) > 0)
        def _():
            sum_ref[...] += sums

        @pl.when(pl.program_id(0) < count // 2)
        def _():
            gone_ref[...] = out

        @pl.when(pl.program_id(0) >= count // 2)
        def _():
            kept_ref[0] = out

    whole = lambda i, n: (0, 0)
    tok = pl.BlockSpec((rows, features), lambda i, n: (place(i, n), 0))
    joined = pl.BlockSpec((3, part, rows), lambda i, n: (0, 0, place(i, n)))
    weight = pl.BlockSpec((3, features, width), lambda i, n: (0, 0, 0))
    return call(
        body,
        (count,),
        [joined] * len(pieces) + [weight, weight, tok, tok, pl.BlockSpec(vectors.shape, whole)],
        [
            pl.BlockSpec((rows, features), gone),
            pl.BlockSpec((1, rows, features), kept),
            pl.BlockSpec((8, features), whole),
        ],
        [
            shaped((span // 2, features), F32),
            shaped((2, span // 2, features), F32),
            shaped((8, features), F32),
        ],
        12 * span * features * width,
        prefetch=1,
        after=after,
    )(mine, *pieces, *weights, tokens, dmiddle, vectors)


def collect(sums_one, sums_two, dgate_two, bias_other, vectors):
    features = vectors.shape[1]

    def body(one_ref, two_ref, gate_ref, bias_ref, vec_ref, out_ref):
        def rounded(value):
            return value.astype(BF).astype(F32)

        one, two = one_ref[...], two_ref[...]
        out_ref[...] = jnp.concatenate(
            [
                one[1:2] * vec_ref[7:8, :],
                two[1:2] * vec_ref[8:9, :],
                two[3:4],
                rounded(one[0:1]),
                rounded(one[1:2] * vec_ref[9:10, :]),
                rounded(two[2:3]),
                rounded(two[0:1]),
                rounded(two[1:2] * vec_ref[10:11, :]),
                rounded(gate_ref[...]),
                vec_ref[11:12, :],
                bias_ref[:, :features],
                bias_ref[:, features:],
                jnp.zeros((4, features), F32),
            ],
            axis=0,
        )

    whole = lambda a: pl.BlockSpec(a.shape, lambda i: (0, 0))
    operands = (sums_one, sums_two, dgate_two, bias_other, vectors)
    out = shaped((16, features), F32)
    return call(body, (1,), [whole(a) for a in operands], [whole(out)], [out], 1000)(*operands)[0]


def chip_rows(mine, held, arrived, bias_own):
    features = held.shape[1]

    def body(mine_ref, held_ref, arrived_ref, bias_ref, out_ref):
        held, arrived = held_ref[...], arrived_ref[...]
        first = mine_ref[0] == 0
        low = jnp.where(first, held, arrived)
        high = jnp.where(first, arrived, held)
        sums = jnp.concatenate(
            [
                held[0:3] + arrived[0:3],
                bias_ref[:, :features] + arrived[10:11],
                bias_ref[:, features:] + arrived[11:12],
            ],
            axis=0,
        )
        top = sums.astype(BF).astype(F32)
        out_ref[...] = jnp.concatenate(
            [low[3:9], high[3:9], low[9:10], high[9:10], top, sums - top], axis=0
        ).astype(BF)

    whole = lambda a: pl.BlockSpec(a.shape, lambda i, n: (0, 0))
    operands = (held, arrived, bias_own)
    out = shaped((24, features), BF)
    return call(
        body, (1,), [whole(a) for a in operands], [whole(out)], [out], 1000, prefetch=1
    )(mine, *operands)[0]


def halving_steps(size):
    if size == 16:
        return [
            (1, lambda d: d & 1),
            (2, lambda d: (d >> 1) & 1),
            (4, lambda d: ((d >> 2) ^ (d >> 3)) & 1),
            (12, lambda d: (d >> 3) & 1),
        ]
    steps, mask = [], 1
    while mask < size:
        steps.append((mask, partial(lambda shift, d: (d >> shift) & 1, len(steps))))
        mask *= 2
    return steps


def fold(kept, arrived, bit, after=()):
    count = len(kept)

    def body(bit_ref, *refs):
        for at in range(count):
            kept_ref, arrived_ref, stay_ref, leave_ref = refs[at::count]
            total = kept_ref[...] + arrived_ref[...].astype(F32)

            @pl.when(pl.program_id(0) == 0)
            def _():
                leave_ref[...] = total.astype(BF)

            @pl.when(pl.program_id(0) == 1)
            def _():
                stay_ref[...] = total

    def place(at, i, n):
        return (jnp.where(i == 0, 1 - n[at], n[at]), 0)

    halves = [(a.shape[0] // 2, a.shape[1]) for a in kept]
    blocks = [pl.BlockSpec(half, partial(place, at)) for at, half in enumerate(halves)]
    fixed = [pl.BlockSpec(half, lambda i, n: (0, 0)) for half in halves]
    out = call(
        body,
        (2,),
        blocks * 2,
        fixed * 2,
        [shaped(half, F32) for half in halves] + [shaped(half, BF) for half in halves],
        sum(a.size for a in kept),
        prefetch=1,
        after=after,
    )(bit, *kept, *arrived)
    return out[:count], out[count:]


def fold_last(kept, arrived, after=()):
    count = len(kept)

    def body(*refs):
        for at in range(count):
            kept_ref, arrived_ref, out_ref = refs[at::count]
            out_ref[...] = (kept_ref[...].astype(F32) + arrived_ref[...].astype(F32)).astype(BF)

    whole = [pl.BlockSpec(a.shape, lambda i: (0, 0)) for a in kept]
    return call(
        body,
        (1,),
        whole * 2,
        whole,
        [shaped(a.shape, BF) for a in kept],
        sum(a.size for a in kept),
        after=after,
    )(*kept, *arrived)


def join(held, arrived, bit, out_type=BF, ways=(), after=()):
    count = len(held)
    ways = ways or ("above",) * count

    def body(bit_ref, *refs):
        for at in range(count):
            own = pl.program_id(0) == bit_ref[at]
            held_ref, arrived_ref, out_ref = refs[at::count]

            def lay(ref, at=at, out_ref=out_ref):
                value = ref[...].astype(out_type)
                out_ref[...] = value.T if ways[at] == "turned" else value

            pl.when(own)(partial(lay, held_ref))
            pl.when(jnp.logical_not(own))(partial(lay, arrived_ref))

    fixed = [pl.BlockSpec(a.shape, lambda i, n: (0, 0)) for a in held]
    blocks, shapes = [], []
    for a, way in zip(held, ways):
        rows, width = a.shape[::-1] if way == "turned" else a.shape
        if way == "above":
            blocks.append(pl.BlockSpec((rows, width), lambda i, n: (i, 0)))
            shapes.append(shaped((2 * rows, width), out_type))
        else:
            blocks.append(pl.BlockSpec((rows, width), lambda i, n: (0, i)))
            shapes.append(shaped((rows, 2 * width), out_type))
    return call(
        body,
        (2,),
        fixed * 2,
        blocks,
        shapes,
        sum(a.size for a in held),
        prefetch=1,
        after=after,
    )(bit, *held, *arrived)


HALVED = 3


class Halving:
    def __init__(self, dp_size, tensor_size, dp_index, tensor_index, orders):
        steps = halving_steps(dp_size)
        self.count = len(steps)
        self.pairs, bits = [], []
        for at in range(self.count):
            self.pairs.append([])
            bits.append([])
            for order in orders:
                chosen = [steps[order[t][at]] for t in range(tensor_size)]
                self.pairs[at].append(
                    [
                        (d * tensor_size + t, (d ^ chosen[t][0]) * tensor_size + t)
                        for d in range(dp_size)
                        for t in range(tensor_size)
                    ]
                )
                bit = chosen[0][1](dp_index)
                for t in range(1, tensor_size):
                    bit = jnp.where(tensor_index == t, chosen[t][1](dp_index), bit)
                bits[at].append(bit.astype(jnp.int32).reshape(1))
        self.single = bits
        self.bits = [jnp.concatenate(row) if len(row) > 1 else row[0] for row in bits]
        table = None
        for t, order in enumerate(orders[0]):
            places = np.zeros((dp_size, dp_size), np.float32)
            for d in range(dp_size):
                at = 0
                for step in order[:HALVED] + order[HALVED:][::-1]:
                    at = 2 * at + steps[step][1](d)
                places[d, at] = 1.0
            table = places if t == 0 else jnp.where(tensor_index == t, places, table)
        self.table = table
        self.at = 0
        self.payload = None

    def begin(self, *parts):
        self.kept, self.leaving = zip(*parts)
        return tuple(self.leaving)

    def exchange(self, place):
        if self.payload is not None:
            arrived = lax.ppermute(self.payload, ("dp", "tensor"), self.pairs[place][0])
            self.payload = jnp.where(
                self.single[place][0][0] == 0,
                jnp.concatenate([self.payload, arrived], axis=0),
                jnp.concatenate([arrived, self.payload], axis=0),
            )
        return [
            lax.ppermute(part, ("dp", "tensor"), pairs)
            for part, pairs in zip(self.leaving, self.pairs[place])
        ]

    def move(self, after=()):
        if self.at < HALVED:
            arrived = self.exchange(self.at)
            self.at += 1
            if self.at < HALVED:
                self.kept, self.leaving = fold(self.kept, arrived, self.bits[self.at], after)
            else:
                self.leaving = fold_last(self.kept, arrived, after)
        elif self.at < self.count:
            arrived = self.exchange(self.at)
            self.at += 1
            self.leaving = fold_last(self.leaving, arrived, after)
        else:
            place = self.count + HALVED - 1 - self.at
            arrived = self.exchange(place)
            self.at += 1
            self.leaving = join(self.leaving, arrived, self.bits[place], after=after)
        return tuple(self.leaving)

    def last(self):
        self.arrived = self.exchange(0)
        return tuple(self.arrived)

    def finish(self, ways=(), after=()):
        return join(self.leaving, self.arrived, self.bits[0], F32, ways, after)

    def spread(self, value):
        self.payload = value[None]

    def spreaded(self):
        flat = self.payload.reshape(self.payload.shape[0], -1)
        return dot(jnp.asarray(self.table).astype(BF), flat, NN).astype(BF)


def per_device(
    dp_size,
    tensor_size,
    tokens,
    condition,
    lengths,
    modulation_weight,
    modulation_bias,
    first_gain,
    query_key_value_weight,
    attention_out_weight,
    second_gain,
    up_projection_weight,
    upward_bias,
    down_projection_weight,
    downward_bias,
    cotangent,
):
    sequences, span, features = tokens.shape
    hidden = up_projection_weight.shape[1]
    width = attention_out_weight.shape[0]
    dp_index = lax.axis_index("dp")
    mine = lax.axis_index("tensor")
    swap = [(0, 1), (1, 0)]

    def from_sibling(value):
        return lax.ppermute(value, "tensor", swap)

    def ordered(own, other, axis):
        return jnp.where(
            mine == 0,
            jnp.concatenate([own, other], axis=axis),
            jnp.concatenate([other, own], axis=axis),
        )

    qkv_own = query_key_value_weight.transpose(1, 0, 2)
    qkv_weights = (qkv_own, from_sibling(qkv_own))
    out_weights = (attention_out_weight, from_sibling(attention_out_weight))
    up_weights = (up_projection_weight, from_sibling(up_projection_weight))
    up_biases = (upward_bias[None], from_sibling(upward_bias)[None])
    down_weights = (down_projection_weight, from_sibling(down_projection_weight))
    gone = lax.dynamic_index_in_dim(cotangent, 1 - mine, 0, keepdims=False)
    kept = lax.dynamic_index_in_dim(cotangent, mine, 0, keepdims=False)
    upstream = ordered(kept, from_sibling(gone), 0)
    rows = lax.dynamic_index_in_dim(tokens, mine, 0, keepdims=False)
    length = lax.dynamic_slice_in_dim(lengths, mine, 1, 0)

    cond_float = condition.astype(F32)
    silu_values, silu_pull = jax.vjp(jax.nn.silu, cond_float)
    silu_cond = silu_values.astype(BF)
    mods = dot(silu_cond, modulation_weight, NN) + modulation_bias
    mods = lax.dynamic_index_in_dim(mods, mine, 0, keepdims=False).reshape(6, features)
    shift_one, scale_one, gate_one, shift_two, scale_two, gate_two = mods
    silu_row = lax.dynamic_index_in_dim(silu_cond, mine, 0, keepdims=False).astype(F32)
    vectors = jnp.stack(
        [
            first_gain * (1.0 + scale_one),
            shift_one,
            gate_one,
            second_gain * (1.0 + scale_two),
            shift_two,
            gate_two,
            downward_bias,
            1.0 + scale_one,
            1.0 + scale_two,
            first_gain,
            second_gain,
            jnp.pad(silu_row, (0, features - silu_row.shape[0])),
        ]
        + [jnp.zeros((features,), F32)] * 4
    )
    cosine, sine = (jnp.asarray(table) for table in rotary_tables(span))

    leading, joined = project(rows, qkv_weights, vectors, cosine, sine)
    attended, totals = attend(length, joined)
    (
        branch_one, trailing, dbranch, act_own, act_other, dupper_own, dupper_other,
        dmiddle, dbranch_one, dattended, sums_two, gb_own, gb_other,
    ) = middle(
        attended, rows, upstream, out_weights, up_weights, down_weights, up_biases, vectors
    )
    halving = dp_size == 16
    orders = ((0, 1, 2, 3), (1, 0, 2, 3))

    def job(parts):
        return Halving(dp_size, tensor_size, dp_index, mine, (orders,) * parts) if halving else None

    def advance(work, *after):
        return work.move(after) if halving else ()

    def back(piece, after):
        return attend_back(
            length, joined, attended, dattended, totals, cosine, sine, piece, after=after
        )

    sum_down, sum_up, sum_input = job(1), job(2), job(1)
    gd_other = weight_grad(act_other, dbranch, BF)
    gu_other = weight_grad(dupper_other, trailing, BF, after=(gd_other,))
    go_other = out_grad(attended, dbranch_one, 1, BF, after=(gu_other,))
    gd_other, gu_other, go_other = (from_sibling(value) for value in (gd_other, gu_other, go_other))
    count = width // (2 * HEAD)
    backs = [None] * (2 * count)
    other, own = list(range(count, 2 * count)), list(range(count))
    if halving:
        sent = sum_down.begin(weight_grad(act_own, dbranch, F32, gd_other, sum_down.single[0][0]))
        for piece in other[:-1]:
            backs[piece] = back(piece, sent)
            sent = (backs[piece],)
        sent = advance(sum_down, *sent)
        bits = sum_up.single[0]
        up_parts = weight_grad(dupper_own, trailing, F32, gu_other, bits[0], after=sent)
        out_parts = out_grad(attended, dbranch_one, 0, F32, go_other, bits[1], after=up_parts[1:])
        sent = sum_up.begin(up_parts, out_parts)
        sent = sent + advance(sum_down, out_parts[1])
    else:
        grad_downward_weight = lax.psum(weight_grad(act_own, dbranch, F32, gd_other), "dp")
        grad_upward_weight = lax.psum(weight_grad(dupper_own, trailing, F32, gu_other), "dp").T
        both = lax.psum(out_grad(attended, dbranch_one, 0, F32, go_other), "dp")
        grad_output_weight = jnp.concatenate([both[:width], both[width:]], axis=1)
        sent = ()
        for piece in other[:-1]:
            backs[piece] = back(piece, sent)

    piece = other[-1]
    backs[piece] = back(piece, sent)
    sent = (backs[piece],) + advance(sum_down, backs[piece])
    product = project_weight_back(leading, backs[count:], BF, after=sent)
    gq_other = from_sibling(product)
    sent = (product,) + advance(sum_up, product)
    plan = [(sum_down,), (sum_up, sum_down), (sum_up, sum_down)]
    for place, piece in enumerate(own):
        backs[piece] = back(piece, sent)
        sent = (backs[piece],)
        for work in plan[place % len(plan)]:
            sent = sent + advance(work, backs[piece])
    if halving:
        parts = project_weight_back(
            leading, backs[:count], F32, gq_other, sum_input.single[0][0], after=sent
        )
        sent = sum_input.begin(parts)
    else:
        grad_input_weight = lax.psum(project_weight_back(leading, backs[:count], F32, gq_other), "dp")
    which = mine.astype(jnp.int32).reshape(1)
    gone_tokens, grad_tokens, sums_one = project_back(
        which, backs, qkv_weights, rows, dmiddle, vectors, after=sent
    )
    sent = advance(sum_input, gone_tokens) + advance(sum_up, gone_tokens)
    if halving:
        sent = sent + sum_down.last()
    gone_output, output, dgate_two = finish_forward(
        which, (act_own, act_other), down_weights, branch_one, rows, upstream, vectors, after=sent
    )
    sent = advance(sum_input, gone_output) + advance(sum_up, gone_output)

    grad_tokens = lax.dynamic_update_index_in_dim(
        grad_tokens, from_sibling(gone_tokens), 1 - mine, 0
    )
    output = lax.dynamic_update_index_in_dim(output, from_sibling(gone_output), 1 - mine, 0)

    held = collect(sums_one, sums_two, dgate_two, gb_other, vectors)
    chip = chip_rows(which, held, from_sibling(held), gb_own)
    wide, six = 6 * features, 6 * sequences
    sums_at, sums_count = six + sequences, 3 + hidden // features
    pair = chip[:six].reshape(sequences, wide)
    grad_condition = silu_pull(dot(pair, modulation_weight, NT))[0]
    if halving:
        (grad_downward_weight,) = sum_down.finish(after=sent)
        sent = advance(sum_input, grad_downward_weight) + advance(sum_up, grad_downward_weight)
        sum_input.spread(chip)
        sum_up.last()
        sent = advance(sum_input, *sent)
        sent = advance(sum_input, grad_tokens, output)
        grad_upward_weight, grad_output_weight = sum_up.finish(("turned", "beside"), after=sent)
        advance(sum_input, grad_upward_weight)
        sum_input.last()
        (grad_input_weight,) = sum_input.finish()
        gathered = sum_input.spreaded().reshape(dp_size, chip.shape[0], features)
    else:
        gathered = lax.all_gather(chip, "dp", axis=0)
    dmods_low = gathered[:, :six].reshape(-1, wide)
    everyone = gathered[:, six:sums_at, : silu_row.shape[0]].reshape(-1, silu_row.shape[0])
    sums = gathered[:, sums_at : sums_at + sums_count].astype(F32)
    sums = jnp.sum(sums + gathered[:, sums_at + sums_count :].astype(F32), axis=0)
    grad_input_weight = grad_input_weight.reshape(3, features, width).transpose(1, 0, 2)
    grad_modulation_bias = jnp.sum(dmods_low, axis=0, dtype=F32)
    grad_modulation_weight = dot(everyone, dmods_low, TN)
    grad_first_gain, grad_second_gain, grad_downward_bias = sums[0], sums[1], sums[2]
    grad_upward_bias = sums[3:].reshape(hidden)
    return (
        output,
        grad_tokens,
        grad_condition,
        grad_modulation_weight,
        grad_modulation_bias,
        grad_first_gain,
        grad_input_weight,
        grad_output_weight,
        grad_second_gain,
        grad_upward_weight,
        grad_upward_bias,
        grad_downward_weight,
        grad_downward_bias,
    )


def solution(mesh):
    placed = (
        P("dp", None, None),
        P("dp", None),
        P("dp"),
        P(),
        P(),
        P(),
        P(None, None, "tensor"),
        P("tensor", None),
        P(),
        P(None, "tensor"),
        P("tensor"),
        P("tensor", None),
        P(),
        P("dp", "tensor", None),
    )
    return jax.shard_map(
        partial(per_device, mesh.shape["dp"], mesh.shape["tensor"]),
        mesh=mesh,
        in_specs=placed,
        out_specs=(
            P("dp", "tensor", None),
            P("dp", "tensor", None),
            P("dp", None),
            P(),
            P(),
            P(),
            P(None, None, "tensor"),
            P("tensor", None),
            P(),
            P(None, "tensor"),
            P("tensor"),
            P("tensor", None),
            P(),
        ),
        check_vma=False,
    )
```
